512 devices in a mesh: section: 4 (over x), seq: 128 (over z, y, core).
Axes of the slice: x: 4, y: 4, z: 16, core: 2. Of those that a mesh axis runs over, the one named last changes fastest.
Arguments:
- feats: bfloat16 [4096, 8, 8, 768], P(('section', 'seq'))
- dw_weight: float32 [7, 7, 768], replicated, may hold values from -0.875 to 0.875
- dw_bias: float32 [768], replicated, may hold values from -3 to 3
- ln1_gain: float32 [768], replicated, may hold values from 0.5 to 2
- w_up: bfloat16 [1536, 768], P('section'), may hold values from -0.21875 to 0.21875
- b_up: bfloat16 [1536], P('section'), may hold values from -3 to 3
- w_down: bfloat16 [1536, 768], P('section'), may hold values from -0.15625 to 0.15625
- b_down: float32 [768], replicated, may hold values from -3 to 3
- layer_scale: float32 [768], replicated, may hold values from 0.3 to 1.5
- lnf_gain: float32 [768], replicated, may hold values from 0.5 to 2
- w_head: bfloat16 [768, 1536], P(None, 'section'), may hold values from -0.21875 to 0.21875
- prior: bfloat16 [77824, 1536], P(('section', 'seq')), may hold values from -6 to 6
- counts: int32 [512], P(('section', 'seq')), may hold values from 0 to 152, as said below
- positions: int32 [81920], P(('section', 'seq')), may hold values from 0 to 32767, as said below
- w_in: bfloat16 [1536, 768], P('section')
- ln_gain: float32 [768], replicated, may hold values from 0.5 to 2
- w_qkv: bfloat16 [768, 2304], P(None, 'section'), may hold values from -0.21875 to 0.21875
- qn_gain: float32 [64], replicated, may hold values from 0.5 to 2
- kn_gain: float32 [64], replicated, may hold values from 0.5 to 2
- offsets: int32 [12], replicated, may hold values from 0 to 15
- w_out: bfloat16 [768, 768], P('section'), may hold values from -6 to 6
Outputs:
- slide_out: bfloat16 [32768, 768], P('seq', 'section')
The draws below stay inside these ranges and needn't reach their ends.
Inputs may be any that keep to these rules, and one draw needn't show every extreme that they name: `counts`: slot k of a device is valid when k < 8 + its count. Some device of every section index has count 152. `positions`: only valid slots' entries count. The valid slots of all devices hold every position 0 to 32767 exactly once; a valid slot of a device with section index s holds a position p with (p mod 256) div (64) = s. At most 2 valid slots of one device have the same p div 256, and some device reaches 2.
All inputs are finite; a program needn't handle non-finite values.
Results may differ from the reference program's by a relative error of at most 0.014.
Values may be sent and summed in bfloat16 or wider, within the bound.
No kernel may reach another device: no remote copies, remote signals or barrier semaphores. Data moves between devices by JAX's collectives and lax.ppermute only.
A program may use at most 64 MiB of HBM per device.

```python
import math
import jax
import jax.numpy as jnp
from jax import lax

C = 768
HIDW = 1536
E = 1536
W = 768
HEADS = 12
HS = 64
KS = 7
SIDE = 8
RB = 16
ROWS = 256
FRESH = 8
HPS = 3
PRIOR = 152
TOKSLOTS = 160
SEQ = 32768
TILES = 4096
PRIORS = 77824
N_SECTION = 4
N_SEQ = 128


def tissue_layout(key):
    subkeys = jax.random.split(jax.random.fold_in(key, 4242), 6)
    q_rows = ROWS // N_SECTION
    heavy_src = jax.random.randint(subkeys[0], (N_SECTION, 1), 0, N_SEQ)
    rank_score = jax.random.randint(subkeys[1], (N_SECTION, N_SEQ), 0, 1 << 20) * N_SEQ + jnp.arange(N_SEQ)[None, :]
    weight_rank = jnp.argsort(jnp.argsort(rank_score, axis=1), axis=1)
    weight = 1 + weight_rank * 7 // (N_SEQ - 1)
    is_heavy = jnp.arange(N_SEQ)[None, :] == heavy_src
    weight = jnp.where(is_heavy, 0, weight)
    running = jnp.cumsum(weight, axis=1)
    weight_sum = running[:, -1:]
    spare_rows = N_SEQ * (q_rows - FRESH) - PRIOR
    prior_share = spare_rows * running // weight_sum - spare_rows * (running - weight) // weight_sum
    counts = jnp.where(is_heavy, PRIOR, prior_share).astype(jnp.int32)
    live_count = FRESH + counts
    first_rank = jnp.cumsum(live_count, axis=1) - live_count
    slot_ids = jnp.arange(TOKSLOTS)
    is_valid = slot_ids[None, None, :] < live_count[:, :, None]
    slot_score = jax.random.randint(subkeys[2], (N_SECTION, N_SEQ, TOKSLOTS), 0, 1 << 16) * TOKSLOTS + slot_ids[None, None, :]
    slot_score = jnp.where(is_valid, slot_score, slot_score + (1 << 30))
    local_rank = jnp.argsort(jnp.argsort(slot_score, axis=2), axis=2)
    global_rank = first_rank[:, :, None] + local_rank
    rotation = jax.random.randint(subkeys[3], (N_SECTION, 1, 1), 0, N_SEQ)
    dest_shard = (global_rank + rotation) % N_SEQ
    round_idx = jnp.minimum(global_rank // N_SEQ, q_rows - 1)
    perm_score = jax.random.randint(subkeys[4], (N_SECTION, N_SEQ, q_rows), 0, 1 << 16) * q_rows + jnp.arange(q_rows)[None, None, :]
    row_perm = jnp.argsort(perm_score, axis=2)
    section_ids = jnp.arange(N_SECTION)[:, None, None]
    row_pick = row_perm[section_ids, dest_shard, round_idx]
    placed = dest_shard * ROWS + section_ids * q_rows + row_pick
    filler = jax.random.randint(subkeys[5], (N_SECTION, N_SEQ, TOKSLOTS), 0, N_SEQ * ROWS)
    positions = jnp.where(is_valid, placed, filler).astype(jnp.int32)
    return (counts.reshape(-1), positions.reshape(-1))


def draw_counts(key, part):
    return tissue_layout(key)[0]


def draw_positions(key, part):
    return tissue_layout(key)[1]


def draw_feats(key, part):
    subkeys = jax.random.split(jax.random.fold_in(key, 17), 3)
    shape_all = (TILES, SIDE, SIDE, C)
    log_top = math.log(10.0)
    base_vals = jax.random.normal(subkeys[2], shape_all, jnp.float32)
    col_scale = jnp.exp(jax.random.uniform(subkeys[0], (C,), jnp.float32, 0.0, log_top))
    row_scale = jnp.exp(jax.random.uniform(subkeys[1], (TILES, SIDE, SIDE, 1), jnp.float32, 0.0, log_top))
    return (base_vals * col_scale * row_scale * 0.25).astype(jnp.bfloat16)


def draw_w_in(key, part):
    subkeys = jax.random.split(jax.random.fold_in(key, 29), 2)
    col_scale = jnp.exp(jax.random.uniform(subkeys[0], (W,), jnp.float32, math.log(0.5), math.log(5.0)))
    base_vals = jax.random.normal(subkeys[1], (E, W), jnp.float32)
    return (base_vals * col_scale / math.sqrt(E)).astype(jnp.bfloat16)


def touch_ends(drawn, key, low, largest):
    index_at = [jax.random.randint(jax.random.fold_in(key, axis), (), 0, length) for axis, length in enumerate(drawn.shape)]
    longest = drawn.shape.index(max(drawn.shape))
    next_to = index_at[:longest] + [(index_at[longest] + 1) % drawn.shape[longest]] + index_at[longest + 1:]
    return drawn.at[tuple(index_at)].set(low).at[tuple(next_to)].set(largest)


def steps_of(stream_key, extent, pieces, least, high):
    def one(axis_at, shards_of):
        steps = jax.random.uniform(jax.random.fold_in(jax.random.fold_in(stream_key, 6), axis_at), (shards_of,), jnp.float32, least / len(pieces), high / len(pieces))
        return jnp.repeat(jnp.exp(steps), extent[axis_at] // shards_of).reshape((-1,) + (1,) * (len(extent) - axis_at - 1))

    loudness = one(*pieces[0])
    for cut in pieces[1:]:
        loudness = loudness * one(*cut)
    return loudness


def bell_draw(key, dims, spread, reach, shards=(), kind=jnp.bfloat16):
    entries = spread * jax.random.normal(key, dims, jnp.float32)
    if shards:
        entries = entries * steps_of(key, dims, shards, -0.22, 0.18)
    return jnp.clip(entries, -reach, reach).astype(kind)


def setup_inputs(seed: int = 0) -> dict:
    streams_of = jax.random.split(jax.random.key(seed), 22)
    feats = draw_feats(jax.random.fold_in(streams_of[21], 71), 0)
    dw_weight = bell_draw(streams_of[1], (KS, KS, C), (KS * KS) ** -0.5, 0.875, (), jnp.float32)
    dw_bias = bell_draw(streams_of[2], (C,), 0.5, 3.0, (), jnp.float32)
    ln1_gain = jnp.clip(jnp.exp(jax.random.uniform(streams_of[3], (C,), jnp.float32, math.log(0.5), math.log(2.0))), 0.5, 2.0)
    w_up = bell_draw(streams_of[4], (HIDW, C), C ** -0.5, 0.21875, ((0, 4),))
    b_up = bell_draw(streams_of[5], (HIDW,), 0.5, 3.0, ((0, 4),))
    w_down = bell_draw(streams_of[6], (HIDW, C), HIDW ** -0.5, 0.15625, ((0, 4),))
    b_down = bell_draw(streams_of[7], (C,), 0.5, 3.0, (), jnp.float32)
    layer_scale = jnp.clip(jnp.exp(jax.random.uniform(streams_of[8], (C,), jnp.float32, math.log(0.3), math.log(1.5))), 0.3, 1.5)
    lnf_gain = jnp.clip(jnp.exp(jax.random.uniform(streams_of[9], (C,), jnp.float32, math.log(0.5), math.log(2.0))), 0.5, 2.0)
    w_head = bell_draw(streams_of[10], (C, E), C ** -0.5, 0.21875, ((1, 4),))
    prior = bell_draw(streams_of[11], (PRIORS, E), 1.0, 6.0, ((0, 512),))
    counts = draw_counts(jax.random.fold_in(streams_of[21], 71), 0)
    positions = draw_positions(jax.random.fold_in(streams_of[21], 71), 0)
    w_in = draw_w_in(jax.random.fold_in(streams_of[21], 71), 0)
    ln_gain = jnp.clip(jnp.exp(jax.random.uniform(streams_of[15], (W,), jnp.float32, math.log(0.5), math.log(2.0))), 0.5, 2.0)
    w_qkv = bell_draw(streams_of[16], (W, 3 * HEADS * HS), W ** -0.5, 0.21875, ((1, 4),))
    qn_gain = jnp.clip(jnp.exp(jax.random.uniform(streams_of[17], (HS,), jnp.float32, math.log(0.5), math.log(2.0))), 0.5, 2.0)
    kn_gain = jnp.clip(jnp.exp(jax.random.uniform(streams_of[18], (HS,), jnp.float32, math.log(0.5), math.log(2.0))), 0.5, 2.0)
    offsets = touch_ends(jax.random.randint(streams_of[19], (HEADS,), 0, RB), jax.random.fold_in(streams_of[19], 1), 0, RB - 1).astype(jnp.int32)
    w_out = bell_draw(streams_of[20], (HEADS * HS, W), 1 ** -0.5, 6.0, ((0, 4),))
    return dict(feats=feats, dw_weight=dw_weight, dw_bias=dw_bias, ln1_gain=ln1_gain, w_up=w_up, b_up=b_up, w_down=w_down, b_down=b_down, layer_scale=layer_scale, lnf_gain=lnf_gain, w_head=w_head, prior=prior, counts=counts, positions=positions, w_in=w_in, ln_gain=ln_gain, w_qkv=w_qkv, qn_gain=qn_gain, kn_gain=kn_gain, offsets=offsets, w_out=w_out)


def layer_norm(values, gain_vec):
    row_mean = lax.optimization_barrier(jnp.mean(values, axis=-1, keepdims=True))
    centered = values - row_mean
    variance = lax.optimization_barrier(jnp.mean(centered * centered, axis=-1, keepdims=True))
    return centered * lax.rsqrt(variance + 1e-06) * gain_vec

def rms_scale(values, gain_vec):
    return values * lax.rsqrt(lax.optimization_barrier(jnp.mean(values * values, axis=-1, keepdims=True)) + 1e-06) * gain_vec

def widen(values):
    return lax.optimization_barrier(values).astype(jnp.float32)

def encode_tiles(tile_maps, dw_weight, dw_bias, ln1_gain, w_up, b_up, w_down, b_down, layer_scale, lnf_gain, w_head):
    map_side = tile_maps.shape[1]
    kernel = dw_weight.shape[0]
    half_width = (kernel - 1) // 2
    source = tile_maps.astype(jnp.float32)
    padded = jnp.pad(source, ((0, 0), (half_width, half_width), (half_width, half_width), (0, 0)))
    conv_sum = jnp.zeros_like(source) + dw_bias
    for row_off in range(kernel):
        for col_off in range(kernel):
            conv_sum = conv_sum + padded[:, row_off:row_off + map_side, col_off:col_off + map_side, :] * dw_weight[row_off, col_off]
    channels = source.shape[-1]
    normed_maps = layer_norm(conv_sum, ln1_gain).astype(jnp.bfloat16).reshape(-1, channels)
    pre_act = lax.dot_general(normed_maps, w_up, (((1,), (1,)), ((), ())), preferred_element_type=jnp.float32) + b_up.astype(jnp.float32)
    hidden = jax.nn.gelu(pre_act, approximate=False).astype(jnp.bfloat16)
    branch = jnp.dot(hidden, w_down, preferred_element_type=jnp.float32) + b_down
    block_out = source + layer_scale * branch.reshape(source.shape)
    pooled = lax.optimization_barrier(jnp.mean(block_out, axis=(1, 2)))
    feature = layer_norm(pooled, lnf_gain).astype(jnp.bfloat16)
    return jnp.dot(feature, w_head, preferred_element_type=jnp.float32).astype(jnp.bfloat16)

def reference(feats, dw_weight, dw_bias, ln1_gain, w_up, b_up, w_down, b_down, layer_scale, lnf_gain, w_head, prior, counts, positions, w_in, ln_gain, w_qkv, qn_gain, kn_gain, offsets, w_out):
    dev_total = N_SECTION * N_SEQ
    group_size = FRESH * 8
    blocks = feats.reshape(TILES // group_size, group_size, SIDE, SIDE, C)

    def encode_block(tile_block):
        return encode_tiles(tile_block, dw_weight, dw_bias, ln1_gain, w_up, b_up, w_down, b_down, layer_scale, lnf_gain, w_head)
    fresh_emb = lax.map(encode_block, blocks).reshape(TILES, E)
    slot_rows = jnp.concatenate([fresh_emb.reshape(dev_total, FRESH, E), prior.reshape(dev_total, PRIOR, E)], axis=1)
    live_mask = jnp.arange(TOKSLOTS)[None, :] < (FRESH + counts)[:, None]
    target = jnp.where(live_mask, positions.reshape(dev_total, TOKSLOTS), SEQ).reshape(-1).astype(jnp.int32)
    seq_table = jnp.zeros((SEQ, E), jnp.bfloat16).at[target].set(slot_rows.reshape(-1, E), mode='drop')
    x_seq = jnp.dot(seq_table, w_in, preferred_element_type=jnp.float32).astype(jnp.bfloat16)
    normed = layer_norm(x_seq.astype(jnp.float32), ln_gain).astype(jnp.bfloat16)
    qkv_rows = jnp.dot(normed, w_qkv, preferred_element_type=jnp.float32).astype(jnp.bfloat16)
    qkv_rows = jnp.transpose(qkv_rows.reshape(SEQ, N_SECTION, 3, HPS, HS), (2, 1, 3, 0, 4)).reshape(3, HEADS, SEQ, HS)
    queries = rms_scale(qkv_rows[0].astype(jnp.float32), qn_gain).astype(jnp.bfloat16)
    keys_all = rms_scale(qkv_rows[1].astype(jnp.float32), kn_gain).astype(jnp.bfloat16)
    values_all = qkv_rows[2]
    score_scale = 1.0 / math.sqrt(HS)

    def one_head(items):
        query_mat, key_mat, value_mat, offset = items
        local_q = widen(query_mat).reshape(N_SEQ, ROWS, HS)
        local_k = widen(key_mat).reshape(N_SEQ, ROWS, HS)
        local_v = widen(value_mat).reshape(N_SEQ, ROWS, HS)
        scores = jnp.einsum('nqd,nkd->nqk', local_q, local_k) * score_scale
        weights = jnp.exp(scores)
        local_den = lax.optimization_barrier(jnp.sum(weights, axis=-1)).reshape(SEQ)
        local_num = jnp.einsum('nqk,nkd->nqd', widen(weights.astype(jnp.bfloat16)), local_v).reshape(SEQ, HS)
        far_q = lax.dynamic_index_in_dim(widen(query_mat).reshape(SEQ // RB, RB, HS), offset, axis=1, keepdims=False)
        far_k = lax.dynamic_index_in_dim(widen(key_mat).reshape(SEQ // RB, RB, HS), offset, axis=1, keepdims=False)
        far_v = lax.dynamic_index_in_dim(widen(value_mat).reshape(SEQ // RB, RB, HS), offset, axis=1, keepdims=False)
        far_weights = jnp.exp(jnp.einsum('ad,bd->ab', far_q, far_k) * score_scale)
        far_den = lax.optimization_barrier(jnp.sum(far_weights, axis=-1))
        far_num = jnp.einsum('ab,bd->ad', widen(far_weights.astype(jnp.bfloat16)), far_v)
        picker = (jnp.arange(RB) == offset).astype(jnp.float32)
        far_num_full = (far_num[:, None, :] * picker[None, :, None]).reshape(SEQ, HS)
        far_den_full = (far_den[:, None] * picker[None, :]).reshape(SEQ)
        attended = (local_num + far_num_full) / (local_den + far_den_full)[:, None]
        return attended.astype(jnp.bfloat16)
    heads_out = lax.map(one_head, (queries, keys_all, values_all, offsets))
    merged = jnp.transpose(heads_out, (1, 0, 2)).reshape(SEQ, HEADS * HS)
    return (x_seq.astype(jnp.float32) + jnp.dot(merged, w_out, preferred_element_type=jnp.float32)).astype(jnp.bfloat16)
```

```python
import math

import jax
import jax.numpy as jnp
from jax import lax
from jax.experimental import pallas as pl
from jax.experimental.pallas import tpu as pltpu
from jax.sharding import Mesh
from jax.sharding import PartitionSpec as P

HS = 64
RB = 16
ROWS = 256
N_SECTION = 4
N_Z, N_Y, N_CORE = 16, 4, 2
SEQ_AXES = ("z", "y", "core")
F32 = jnp.float32
BF16 = jnp.bfloat16


def layer_norm(values, gain_vec):
    row_mean = jnp.mean(values, axis=-1, keepdims=True)
    centered = values - row_mean
    variance = jnp.mean(centered * centered, axis=-1, keepdims=True)
    return centered * lax.rsqrt(variance + 1e-06) * gain_vec


def rms_scale(values, gain_vec):
    return values * lax.rsqrt(jnp.mean(values * values, axis=-1, keepdims=True) + 1e-06) * gain_vec


def conv_norm(tile_maps, dw_weight, dw_bias, ln1_gain):
    map_side = tile_maps.shape[1]
    kernel = dw_weight.shape[0]
    half_width = (kernel - 1) // 2
    source = tile_maps.astype(F32)
    padded = jnp.pad(source, ((0, 0), (half_width, half_width), (half_width, half_width), (0, 0)))
    conv_sum = jnp.zeros_like(source) + dw_bias
    for row_off in range(kernel):
        for col_off in range(kernel):
            conv_sum = (
                conv_sum
                + padded[:, row_off : row_off + map_side, col_off : col_off + map_side, :]
                * dw_weight[row_off, col_off]
            )
    channels = source.shape[-1]
    return layer_norm(conv_sum, ln1_gain).astype(BF16).reshape(-1, channels)


def rotate(block, axis, size, step):
    return lax.ppermute(block, axis, [(i, (i + step) % size) for i in range(size)])


def ring(block, cut):
    left = rotate(block, "section", N_SECTION, 1)
    right = rotate(block, "section", N_SECTION, -1)
    far_low = rotate(left[:cut], "section", N_SECTION, 1)
    far_high = rotate(right[cut:], "section", N_SECTION, -1)
    return jnp.stack([block, left, right, jnp.concatenate([far_low, far_high])])


def spread(block, axis, size):
    return lax.all_to_all(
        jnp.broadcast_to(block[None], (size,) + block.shape), axis, 0, 0, tiled=True
    )


def up_pool_kernel(maps_a, maps_b, up_a, up_b, bias, out):
    nt = (((1,), (1,)), ((), ()))
    pre = (
        lax.dot_general(maps_a[...], up_a[0], nt, preferred_element_type=F32)
        + lax.dot_general(maps_b[...], up_b[0], nt, preferred_element_type=F32)
        + bias[0].astype(F32)
    )
    hidden = (0.5 * pre * (1.0 + lax.erf(pre * (1.0 / math.sqrt(2.0))))).astype(BF16).astype(F32)
    tiles = out.shape[1]
    out[0] = jnp.mean(hidden.reshape(tiles, hidden.shape[0] // tiles, hidden.shape[1]), axis=1)


def up_pool(maps_a, maps_b, up_a, up_b, bias, tiles):
    blocks, width, depth = up_a.shape
    return pl.pallas_call(
        up_pool_kernel,
        grid=(blocks,),
        in_specs=[
            pl.BlockSpec(maps_a.shape, lambda i: (0, 0)),
            pl.BlockSpec(maps_b.shape, lambda i: (0, 0)),
            pl.BlockSpec((1, width, depth), lambda i: (i, 0, 0)),
            pl.BlockSpec((1, width, depth), lambda i: (i, 0, 0)),
            pl.BlockSpec((1, 1, width), lambda i: (i, 0, 0)),
        ],
        out_specs=pl.BlockSpec((1, tiles, width), lambda i: (i, 0, 0)),
        out_shape=jax.ShapeDtypeStruct((blocks, tiles, width), F32),
        compiler_params=pltpu.CompilerParams(vmem_limit_bytes=40 * 2**20),
        cost_estimate=pl.CostEstimate(
            flops=4 * blocks * width * depth * maps_a.shape[0],
            bytes_accessed=4 * blocks * width * depth + 4 * maps_a.size,
            transcendentals=blocks * width * maps_a.shape[0],
        ),
    )(maps_a, maps_b, up_a, up_b, bias)


def shards(
    feats,
    dw_weight,
    dw_bias,
    ln1_gain,
    w_up,
    b_up,
    w_down,
    b_down,
    layer_scale,
    lnf_gain,
    w_head,
    prior,
    counts,
    positions,
    w_in,
    ln_gain,
    w_qkv,
    qn_gain,
    kn_gain,
    offsets,
    w_out,
):
    n_section = N_SECTION
    n_seq = N_Z * N_Y * N_CORE
    section_idx = lax.axis_index("section")
    core = lax.axis_index("core")
    tiles = feats.shape[0]
    channels = feats.shape[3]
    half = channels // N_CORE
    share = w_up.shape[0]

    def mine(matrix, axis):
        return lax.dynamic_slice_in_dim(matrix, core * half, half, axis)

    def other(matrix, axis):
        return lax.dynamic_slice_in_dim(matrix, (1 - core) * half, half, axis)

    bias_rows = jnp.broadcast_to(b_up[None, :], (16, share))
    up_ring = ring(jnp.concatenate([mine(w_up, 1), bias_rows]), 192)
    rest_ring = ring(
        jnp.concatenate([mine(w_down, 1), mine(w_head, 0), mine(w_in, 1)]), 3 * share // 2
    )
    up_swap = rotate(up_ring[:, :share], "core", N_CORE, 1)
    rest_swap = rotate(rest_ring, "core", N_CORE, 1)

    slot_total = tiles + prior.shape[0]
    q_rows = ROWS // n_section
    capacity = -(-slot_total // n_seq)
    slot_ids = jnp.arange(slot_total)
    live_mask = slot_ids < tiles + counts[0]
    dest_shard = positions // ROWS
    row_in = positions % ROWS - section_idx * q_rows
    earlier = (
        (dest_shard[None, :] == dest_shard[:, None])
        & (slot_ids[None, :] < slot_ids[:, None])
        & live_mask[None, :]
    )
    within = jnp.sum(earlier.astype(jnp.int32), axis=1)
    bucket = jnp.where(live_mask, dest_shard * capacity + within, -1)
    select_mat = (jnp.arange(n_seq * capacity)[:, None] == bucket[None, :]).astype(BF16)
    row_code = jnp.broadcast_to((row_in + 1).astype(BF16)[:, None], (slot_total, 128))

    normed_maps = conv_norm(feats, dw_weight, dw_bias, ln1_gain)
    feat_mean = jnp.mean(feats.astype(F32), axis=(1, 2))
    hidden_mean = up_pool(
        mine(normed_maps, 1),
        other(normed_maps, 1),
        up_ring[:, :share],
        up_swap,
        up_ring[:, share : share + 1],
        tiles,
    )
    hidden_rows = jnp.transpose(hidden_mean, (1, 0, 2)).reshape(tiles, n_section * share)

    def joined(a, b):
        return jnp.where(core == 0, jnp.concatenate([a, b], 1), jnp.concatenate([b, a], 1))

    def dot(a, b):
        return jnp.dot(a, b, preferred_element_type=F32)

    def dot_split(a, b):
        high = a.astype(BF16)
        low = (a - high.astype(F32)).astype(BF16)
        return dot(high, b) + dot(low, b)

    def rows_of(stack, part):
        block = stack[:, part * share : (part + 1) * share]
        return block.reshape(n_section * share, half)

    branch = joined(
        dot_split(hidden_rows, rows_of(rest_ring, 0)), dot_split(hidden_rows, rows_of(rest_swap, 0))
    )
    pooled = feat_mean + layer_scale * (branch + b_down)
    feature = layer_norm(pooled, lnf_gain).astype(BF16)
    feature_a, feature_b = mine(feature, 1), other(feature, 1)
    relative = [section_idx, (section_idx + 3) % 4, (section_idx + 1) % 4, (section_idx + 2) % 4]
    fresh_emb = jnp.concatenate(
        [
            dot(feature_a, rest_ring[i, share : 2 * share])
            + dot(feature_b, rest_swap[i, share : 2 * share])
            for i in range(n_section)
        ],
        axis=1,
    ).astype(BF16)
    prior_rel = jnp.concatenate(
        [lax.dynamic_slice_in_dim(prior, r * share, share, 1) for r in relative], axis=1
    )
    slot_emb = jnp.concatenate([fresh_emb, prior_rel], axis=0)
    slot_x = joined(dot(slot_emb, rows_of(rest_ring, 2)), dot(slot_emb, rows_of(rest_swap, 2)))

    payload = dot(select_mat, jnp.concatenate([slot_x.astype(BF16), row_code], axis=1)).astype(BF16)
    got = lax.all_to_all(
        payload.reshape(n_seq, capacity, payload.shape[1]), SEQ_AXES, 0, 0, tiled=True
    ).reshape(n_seq * capacity, payload.shape[1])
    code = got[:, channels].astype(F32)
    placer = (jnp.arange(1, q_rows + 1).astype(F32)[:, None] == code[None, :]).astype(BF16)
    x_local = dot(placer, got[:, :channels]).astype(BF16)
    x_rows = lax.all_gather(x_local, "section", axis=0, tiled=True)

    rows_total = x_rows.shape[0]
    normed = layer_norm(x_rows.astype(F32), ln_gain).astype(BF16)
    heads_here = w_qkv.shape[1] // (3 * HS)
    qkv_rows = dot(normed, w_qkv).astype(BF16).reshape(rows_total, 3, heads_here, HS)
    queries = rms_scale(qkv_rows[:, 0].astype(F32), qn_gain).astype(BF16)
    keys_here = rms_scale(qkv_rows[:, 1].astype(F32), kn_gain).astype(BF16)
    values_here = qkv_rows[:, 2]
    score_scale = 1.0 / math.sqrt(HS)
    my_offsets = lax.dynamic_slice_in_dim(offsets, section_idx * heads_here, heads_here)
    picker = jnp.arange(RB)[None, :] == my_offsets[:, None]
    pick_half = picker.astype(BF16)
    stride_rows = rows_total // RB

    def strided(matrix):
        return jnp.einsum(
            "arhd,hr->ahd",
            matrix.reshape(stride_rows, RB, heads_here, HS),
            pick_half,
            preferred_element_type=F32,
        ).astype(BF16)

    far_q = strided(queries)
    far_kv = jnp.concatenate([strided(keys_here), strided(values_here)], axis=1).reshape(
        stride_rows, 2 * heads_here * HS
    )
    z_kv = spread(far_kv, "z", N_Z).reshape(N_Z * stride_rows, 2 * heads_here * HS)
    all_kv = lax.all_gather(z_kv, ("y", "core"), axis=0, tiled=True)
    all_kv = all_kv.reshape(n_seq * stride_rows, 2, heads_here, HS)
    piece_k, piece_v = all_kv[:, 0], all_kv[:, 1]

    scores = (
        jnp.einsum("qhd,khd->hqk", queries, keys_here, preferred_element_type=F32) * score_scale
    )
    weights = jnp.exp(scores)
    local_den = jnp.sum(weights, axis=-1)
    local_num = jnp.einsum(
        "hqk,khd->hqd", weights.astype(BF16), values_here, preferred_element_type=F32
    )
    far_scores = (
        jnp.einsum("ahd,bhd->hab", far_q, piece_k, preferred_element_type=F32) * score_scale
    )
    far_weights = jnp.exp(far_scores)
    far_add = jnp.einsum(
        "hab,bhd->had", far_weights.astype(BF16), piece_v, preferred_element_type=F32
    )
    far_den = jnp.sum(far_weights, axis=-1)
    pick_full = picker.astype(F32)
    far_num_full = (far_add[:, :, None, :] * pick_full[:, None, :, None]).reshape(
        heads_here, rows_total, HS
    )
    far_den_full = (far_den[:, :, None] * pick_full[:, None, :]).reshape(heads_here, rows_total)
    attended = ((local_num + far_num_full) / (local_den + far_den_full)[:, :, None]).astype(BF16)
    merged = jnp.transpose(attended, (1, 0, 2)).reshape(rows_total, heads_here * HS)
    width_part = w_out.shape[1] // n_section
    partial_out = dot(merged, w_out).reshape(rows_total, n_section, width_part)
    parts = lax.all_to_all(
        jnp.transpose(partial_out, (1, 0, 2)), "section", 0, 0, tiled=True
    )
    residual = lax.dynamic_slice_in_dim(x_rows, section_idx * width_part, width_part, 1)
    return (residual.astype(F32) + jnp.sum(parts, axis=0)).astype(BF16)


def solution(mesh):
    fine = Mesh(
        mesh.devices.reshape(N_SECTION, N_Z, N_Y, N_CORE), ("section",) + SEQ_AXES
    )
    both = ("section",) + SEQ_AXES
    placed = (
        P(both, None, None, None),
        P(),
        P(),
        P(),
        P("section", None),
        P("section"),
        P("section", None),
        P(),
        P(),
        P(),
        P(None, "section"),
        P(both, None),
        P(both),
        P(both),
        P("section", None),
        P(),
        P(None, "section"),
        P(),
        P(),
        P(),
        P("section", None),
    )
    return jax.shard_map(
        shards, mesh=fine, in_specs=placed, out_specs=P(SEQ_AXES, "section"), check_vma=False
    )
```

```python
import math

import jax
import jax.numpy as jnp
from jax import lax
from jax.experimental import pallas as pl
from jax.experimental.pallas import tpu as pltpu
from jax.sharding import Mesh
from jax.sharding import PartitionSpec as P

HS = 64
RB = 16
ROWS = 256
N_SECTION = 4
N_Z, N_Y, N_CORE = 16, 4, 2
SEQ_AXES = ("z", "y", "core")
F32 = jnp.float32
BF16 = jnp.bfloat16


def layer_norm(values, gain_vec):
    row_mean = jnp.mean(values, axis=-1, keepdims=True)
    centered = values - row_mean
    variance = jnp.mean(centered * centered, axis=-1, keepdims=True)
    return centered * lax.rsqrt(variance + 1e-06) * gain_vec


def conv_norm(tile_maps, dw_weight, dw_bias, ln1_gain):
    map_side = tile_maps.shape[1]
    kernel = dw_weight.shape[0]
    half_width = (kernel - 1) // 2
    source = tile_maps.astype(F32)
    padded = jnp.pad(source, ((0, 0), (half_width, half_width), (half_width, half_width), (0, 0)))
    conv_sum = jnp.zeros_like(source) + dw_bias
    for row_off in range(kernel):
        for col_off in range(kernel):
            conv_sum = (
                conv_sum
                + padded[:, row_off : row_off + map_side, col_off : col_off + map_side, :]
                * dw_weight[row_off, col_off]
            )
    channels = source.shape[-1]
    return layer_norm(conv_sum, ln1_gain).astype(BF16).reshape(-1, channels)


def rotate(block, axis, size, step):
    return lax.ppermute(block, axis, [(i, (i + step) % size) for i in range(size)])


def spread(block, axis, size):
    return lax.all_to_all(
        jnp.broadcast_to(block[None], (size,) + block.shape), axis, 0, 0, tiled=True
    )


NT = (((1,), (1,)), ((), ()))


def dot(a, b):
    return jnp.dot(a, b, preferred_element_type=F32)


def gelu_mean(pre, tiles):
    hidden = (0.5 * pre * (1.0 + lax.erf(pre * (1.0 / math.sqrt(2.0))))).astype(BF16).astype(F32)
    return jnp.mean(hidden.reshape(tiles, hidden.shape[0] // tiles, hidden.shape[1]), axis=1)


def lanes(ref, index, width):
    return ref[:, pl.ds(pl.multiple_of(index * width, 128), width)]


def pack_kernel(core_ref, w_up, w_down, w_head, w_in, bias_rows, out, sems):
    n = w_up.shape[0]
    start = pl.multiple_of(core_ref[0] * n, n)
    parts = (
        w_up.at[:, pl.ds(start, n)],
        w_down.at[:, pl.ds(start, n)],
        w_head.at[pl.ds(start, n), :],
        w_in.at[:, pl.ds(start, n)],
    )
    copies = [
        pltpu.make_async_copy(part, out.at[pl.ds(k * n, n), :], sems.at[k])
        for k, part in enumerate(parts)
    ]
    copies.append(pltpu.make_async_copy(bias_rows, out.at[pl.ds(4 * n, 16), :], sems.at[4]))
    for copy in copies:
        copy.start()
    for copy in copies:
        copy.wait()


def pack(core, w_up, w_down, w_head, w_in, bias_rows):
    n = w_up.shape[0]
    return pl.pallas_call(
        pack_kernel,
        in_specs=[pl.BlockSpec(memory_space=pltpu.SMEM)] + [pl.BlockSpec(memory_space=pl.ANY)] * 5,
        out_specs=pl.BlockSpec(memory_space=pltpu.VMEM),
        out_shape=jax.ShapeDtypeStruct((4 * n + 16, n), BF16),
        scratch_shapes=[pltpu.SemaphoreType.DMA((5,))],
        cost_estimate=pl.CostEstimate(flops=0, bytes_accessed=4 * n * n * 4, transcendentals=0),
    )(core.astype(jnp.int32)[None], w_up, w_down, w_head, w_in, bias_rows)


def early_kernel(
    where, maps, up, bias, w_in, prior, left, right, left_swap, right_swap, hid, x_prior
):
    core = where[0]
    n = up.shape[0]
    tiles = hid.shape[1]
    maps_a, maps_b = lanes(maps, core, n), lanes(maps, 1 - core, n)
    pre = lax.dot_general(maps[...], up[...], NT, preferred_element_type=F32)
    hid[0] = gelu_mean(pre + bias[...].astype(F32), tiles)
    own = dot(lanes(prior, where[1], n), w_in[...])
    x_a = jnp.zeros((prior.shape[0], n), F32)
    x_b = x_a
    for slot, (a, b) in enumerate(((left, left_swap), (right, right_swap))):
        pre = lax.dot_general(maps_a, a[0:n, :], NT, preferred_element_type=F32)
        pre += lax.dot_general(maps_b, b[0:n, :], NT, preferred_element_type=F32)
        hid[slot + 1] = gelu_mean(pre + a[4 * n : 4 * n + 1, :].astype(F32), tiles)
        columns = lanes(prior, where[slot + 2], n)
        x_a += dot(columns, a[3 * n : 4 * n, :])
        x_b += dot(columns, b[3 * n : 4 * n, :])
    x_prior[...] = own + natural(core, x_a, x_b)


def natural(core, a, b):
    return jnp.where(core == 0, jnp.concatenate([a, b], 1), jnp.concatenate([b, a], 1))


def late_kernel(
    where, maps, prior, hid, x_prior, feat_mean, layer_scale, b_down, lnf_gain, bucket, row_code,
    w_down, w_head, w_in, left, right, left_swap, right_swap, low, high, low_swap, high_swap,
    payload, slot_x,
):
    core = where[0]
    n = w_down.shape[0]
    tiles = hid.shape[1]
    pre = lax.dot_general(lanes(maps, core, n), low[0:n, :], NT, preferred_element_type=F32)
    pre += lax.dot_general(
        lanes(maps, 1 - core, n), low_swap[0:n, :], NT, preferred_element_type=F32
    )
    hid_far = gelu_mean(pre + high[2 * n : 2 * n + 1, :].astype(F32), tiles)

    def exact(block):
        upper = block.astype(BF16)
        lower = (block - upper.astype(F32)).astype(BF16)
        return jnp.concatenate([upper.astype(F32), lower.astype(F32)], 0).astype(BF16)

    def folded(block):
        return block[0:tiles] + block[tiles : 2 * tiles]

    sides = ((left, left_swap), (right, right_swap))
    own = dot(exact(hid[0]), w_down[...])
    part = exact(hid_far)
    br_a, br_b = dot(part, low[n : 2 * n, :]), dot(part, low_swap[n : 2 * n, :])
    for slot, (a, b) in enumerate(sides):
        part = exact(hid[slot + 1])
        br_a += dot(part, a[n : 2 * n, :])
        br_b += dot(part, b[n : 2 * n, :])
    branch = folded(own + natural(core, br_a, br_b))
    pooled = feat_mean[...] + layer_scale[...] * (branch + b_down[...])
    feature = layer_norm(pooled, lnf_gain[...])
    first, second = feature[:, 0:n], feature[:, n : 2 * n]
    feature_a = jnp.where(core == 0, first, second).astype(BF16)
    feature_b = jnp.where(core == 0, second, first).astype(BF16)
    emb = dot(feature.astype(BF16), w_head[...]).astype(BF16)
    own = dot(emb, w_in[...])
    emb = (dot(feature_a, high[0:n, :]) + dot(feature_b, high_swap[0:n, :])).astype(BF16)
    columns = lanes(prior, where[4], n)
    x_a, x_b = dot(emb, high[n : 2 * n, :]), dot(emb, high_swap[n : 2 * n, :])
    p_a, p_b = dot(columns, high[n : 2 * n, :]), dot(columns, high_swap[n : 2 * n, :])
    for a, b in sides:
        emb = (
            dot(feature_a, a[2 * n : 3 * n, :]) + dot(feature_b, b[2 * n : 3 * n, :])
        ).astype(BF16)
        x_a += dot(emb, a[3 * n : 4 * n, :])
        x_b += dot(emb, b[3 * n : 4 * n, :])
    slot_x[0:tiles, :] = own + natural(core, x_a, x_b)
    slot_x[tiles:, :] = x_prior[...] + natural(core, p_a, p_b)
    places = lax.broadcasted_iota(jnp.int32, (payload.shape[0], bucket.shape[1]), 0)
    select = jnp.where(places == bucket[...], 1.0, 0.0).astype(BF16)
    width = slot_x.shape[1]
    payload[:, 0:width] = dot(select, slot_x[...].astype(BF16)).astype(BF16)
    payload[:, width:] = dot(select, row_code[...]).astype(BF16)


def local_call(body, outs, scratch, flops, size, *operands):
    vmem = pl.BlockSpec(memory_space=pltpu.VMEM)
    return pl.pallas_call(
        body,
        in_specs=[pl.BlockSpec(memory_space=pltpu.SMEM)] + [vmem] * (len(operands) - 1),
        out_specs=jax.tree.map(lambda _: vmem, outs),
        out_shape=outs,
        scratch_shapes=scratch,
        compiler_params=pltpu.CompilerParams(vmem_limit_bytes=48 * 2**20),
        cost_estimate=pl.CostEstimate(flops=flops, bytes_accessed=size, transcendentals=0),
    )(*operands)


def head_lanes(shape, head):
    lane = lax.broadcasted_iota(jnp.int32, shape, len(shape) - 1)
    return (lane >= head * HS) & (lane < (head + 1) * HS)


def dilated(shape, off_lane):
    return lax.rem(lax.broadcasted_iota(jnp.int32, shape, 0), RB) == off_lane


def project_kernel(x, ln_gain, w_q, w_k, w_v, q_gain, k_gain, off_lane, q, k, v, far_q, far_kv):
    rows, width = q.shape
    normed = layer_norm(x[...].astype(F32), ln_gain[...]).astype(BF16)
    chosen = dilated((rows, width), off_lane[...])

    def unit(raw, gain):
        raw = raw.astype(BF16).astype(F32)
        square = raw * raw
        mean = jnp.zeros_like(raw)
        for head in range(width // HS):
            inside = head_lanes(raw.shape, head)
            total = jnp.sum(jnp.where(inside, square, 0.0), axis=1, keepdims=True) * (1.0 / HS)
            mean = jnp.where(inside, total, mean)
        return (raw * lax.rsqrt(mean + 1e-06) * gain).astype(BF16)

    def far_rows(part):
        kept = jnp.where(chosen, part.astype(F32), 0.0)
        return jnp.sum(kept.reshape(rows // RB, RB, width), axis=1)

    q_rows = unit(dot(normed, w_q[...]), q_gain[...])
    k_rows = unit(dot(normed, w_k[...]), k_gain[...])
    v_rows = dot(normed, w_v[...]).astype(BF16)
    q[...], k[...], v[...] = q_rows, k_rows, v_rows
    far_q[...] = far_rows(q_rows)
    far_kv[...] = jnp.concatenate([far_rows(k_rows), far_rows(v_rows)], axis=1).astype(BF16)


def by_head(block):
    heads = block.shape[1] // HS
    wide = block.astype(F32)
    kept = [jnp.where(head_lanes(wide.shape, head), wide, 0.0) for head in range(heads)]
    return jnp.concatenate(kept, axis=0)


def back(block, rows, width):
    out = jnp.zeros((rows, width), F32)
    for head in range(width // HS):
        part = jnp.broadcast_to(block[head * rows : (head + 1) * rows], (rows, width))
        out = jnp.where(head_lanes(out.shape, head), part, out)
    return out


def weigh(queries, keys, values):
    scores = lax.dot_general(queries, keys, NT, preferred_element_type=F32)
    weights = jnp.exp(scores * (1.0 / math.sqrt(HS)))
    return jnp.sum(weights, axis=1, keepdims=True), dot(weights.astype(BF16), values)


def far_part(far_q, kv):
    rows, width = far_q.shape
    spread_q = by_head(far_q[...])
    spread_q = jnp.concatenate([spread_q, jnp.zeros_like(spread_q)], axis=1).astype(BF16)
    den, num = weigh(spread_q, kv[...], kv[...])
    return back(den, rows, width), back(num[:, width:], rows, width)


def near_kernel(q, k, v, far_q, kv, den, num, far_den, far_num):
    rows, width = q.shape
    local_den, local_num = weigh(by_head(q[...]).astype(BF16), k[...], v[...])
    den[...] = back(local_den, rows, width)
    num[...] = back(local_num, rows, width)
    far_den[...], far_num[...] = far_part(far_q, kv)


def far_kernel(far_q, kv, off_lane, den, num, far_den, far_num, w_out, out):
    rows, width = num.shape
    chosen = dilated((rows, width), off_lane[...])
    more_den, more_num = far_part(far_q, kv)

    def placed(block):
        wide = jnp.broadcast_to(block[:, None, :], (rows // RB, RB, width))
        return jnp.where(chosen, wide.reshape(rows, width), 0.0)

    attended = (num[...] + placed(far_num[...] + more_num)) / (
        den[...] + placed(far_den[...] + more_den)
    )
    attended = attended.astype(BF16)
    out[...] = lax.dot_general(w_out[...], attended, NT, preferred_element_type=F32).astype(BF16)


def vmem_call(body, outs, flops, size, exps, *operands):
    vmem = pl.BlockSpec(memory_space=pltpu.VMEM)
    return pl.pallas_call(
        body,
        in_specs=[vmem] * len(operands),
        out_specs=jax.tree.map(lambda _: vmem, outs),
        out_shape=outs,
        compiler_params=pltpu.CompilerParams(vmem_limit_bytes=40 * 2**20),
        cost_estimate=pl.CostEstimate(flops=flops, bytes_accessed=size, transcendentals=exps),
    )(*operands)


def shards(
    feats,
    dw_weight,
    dw_bias,
    ln1_gain,
    w_up,
    b_up,
    w_down,
    b_down,
    layer_scale,
    lnf_gain,
    w_head,
    prior,
    counts,
    positions,
    w_in,
    ln_gain,
    w_qkv,
    qn_gain,
    kn_gain,
    offsets,
    w_out,
):
    n_section = N_SECTION
    n_seq = N_Z * N_Y * N_CORE
    section_idx = lax.axis_index("section")
    core = lax.axis_index("core")
    tiles = feats.shape[0]
    channels = feats.shape[3]
    half = channels // N_CORE
    share = w_up.shape[0]

    bias_rows = jnp.broadcast_to(b_up[None, :], (16, share))
    block = pack(core, w_up, w_down, w_head, w_in, bias_rows)
    left = rotate(block, "section", N_SECTION, 1)
    right = rotate(block, "section", N_SECTION, -1)
    left, right, low_in, high_in = lax.optimization_barrier(
        (left, right, left[: 2 * share], right[2 * share :])
    )
    low = rotate(low_in, "section", N_SECTION, 1)
    high = rotate(high_in, "section", N_SECTION, -1)
    left_swap = rotate(left, "core", N_CORE, 1)
    right_swap = rotate(right, "core", N_CORE, 1)
    low_swap = rotate(low, "core", N_CORE, 1)
    high_swap = rotate(high, "core", N_CORE, 1)

    slot_total = tiles + prior.shape[0]
    q_rows = ROWS // n_section
    capacity = -(-slot_total // n_seq)
    slot_ids = jnp.arange(slot_total)
    live_mask = slot_ids < tiles + counts[0]
    dest_shard = positions // ROWS
    row_in = positions % ROWS - section_idx * q_rows
    earlier = (
        (dest_shard[None, :] == dest_shard[:, None])
        & (slot_ids[None, :] < slot_ids[:, None])
        & live_mask[None, :]
    )
    within = jnp.sum(earlier.astype(jnp.int32), axis=1)
    bucket = jnp.where(live_mask, dest_shard * capacity + within, -1)
    row_code = jnp.broadcast_to((row_in + 1).astype(BF16)[:, None], (slot_total, 128))

    normed_maps = conv_norm(feats, dw_weight, dw_bias, ln1_gain)
    feat_mean = jnp.mean(feats.astype(F32), axis=(1, 2))
    where = jnp.stack(
        [core, section_idx, (section_idx + 3) % 4, (section_idx + 1) % 4, (section_idx + 2) % 4]
    ).astype(jnp.int32)
    row = lambda vec: vec[None, :]
    hid, x_prior = local_call(
        early_kernel,
        (
            jax.ShapeDtypeStruct((3, tiles, share), F32),
            jax.ShapeDtypeStruct((prior.shape[0], channels), F32),
        ),
        [],
        2_000_000_000,
        6_000_000,
        where, normed_maps, w_up, row(b_up), w_in, prior, left, right, left_swap, right_swap,
    )
    payload = local_call(
        late_kernel,
        jax.ShapeDtypeStruct((n_seq * capacity, channels + 128), BF16),
        [pltpu.VMEM((slot_total, channels), F32)],
        2_000_000_000,
        8_000_000,
        where, normed_maps, prior, hid, x_prior, feat_mean, row(layer_scale), row(b_down),
        row(lnf_gain), row(bucket), row_code, w_down, w_head, w_in, left, right, left_swap,
        right_swap, low, high, low_swap, high_swap,
    )

    got = lax.all_to_all(
        payload.reshape(n_seq, capacity, payload.shape[1]), SEQ_AXES, 0, 0, tiled=True
    ).reshape(n_seq * capacity, payload.shape[1])
    code = got[:, channels].astype(F32)
    placer = (jnp.arange(1, q_rows + 1).astype(F32)[:, None] == code[None, :]).astype(BF16)
    x_local = dot(placer, got[:, :channels]).astype(BF16)
    x_rows = spread(x_local, "section", n_section).reshape(ROWS, channels)

    heads_here = w_qkv.shape[1] // (3 * HS)
    width = heads_here * HS
    stride_rows = ROWS // RB
    my_offsets = lax.dynamic_slice_in_dim(offsets, section_idx * heads_here, heads_here)
    off_lane = row(jnp.repeat(my_offsets, HS))
    w_q, w_k, w_v = (w_qkv[:, part * width : (part + 1) * width] for part in range(3))
    small = lambda rows, kind: jax.ShapeDtypeStruct((rows, width), kind)
    q, k, v, far_q, far_kv = vmem_call(
        project_kernel,
        (small(ROWS, BF16),) * 3
        + (small(stride_rows, F32), jax.ShapeDtypeStruct((stride_rows, 2 * width), BF16)),
        300_000_000,
        2_000_000,
        0,
        x_rows, row(ln_gain), w_q, w_k, w_v, row(jnp.tile(qn_gain, heads_here)),
        row(jnp.tile(kn_gain, heads_here)), off_lane,
    )
    z_kv = spread(far_kv, "z", N_Z).reshape(N_Z * stride_rows, 2 * width)
    half_kv = lax.all_gather(z_kv, "y", axis=0, tiled=True)
    other_kv = rotate(half_kv, "core", N_CORE, 1)
    den, num, far_den, far_num = vmem_call(
        near_kernel,
        (small(ROWS, F32),) * 2 + (small(stride_rows, F32),) * 2,
        150_000_000,
        2_000_000,
        250_000,
        q, k, v, far_q, half_kv,
    )
    width_part = channels // n_section
    partial_out = vmem_call(
        far_kernel,
        jax.ShapeDtypeStruct((channels, ROWS), BF16),
        150_000_000,
        2_000_000,
        50_000,
        far_q, other_kv, off_lane, den, num, far_den, far_num,
        jnp.transpose(w_out),
    )
    parts = lax.all_to_all(
        partial_out.reshape(n_section, width_part, ROWS), "section", 0, 0, tiled=True
    )
    residual = lax.dynamic_slice_in_dim(x_rows, section_idx * width_part, width_part, 1)
    total = jnp.transpose(residual).astype(F32) + jnp.sum(parts.astype(F32), axis=0)
    return jnp.transpose(total.astype(BF16))


def solution(mesh):
    fine = Mesh(
        mesh.devices.reshape(N_SECTION, N_Z, N_Y, N_CORE), ("section",) + SEQ_AXES
    )
    both = ("section",) + SEQ_AXES
    placed = (
        P(both, None, None, None),
        P(),
        P(),
        P(),
        P("section", None),
        P("section"),
        P("section", None),
        P(),
        P(),
        P(),
        P(None, "section"),
        P(both, None),
        P(both),
        P(both),
        P("section", None),
        P(),
        P(None, "section"),
        P(),
        P(),
        P(),
        P("section", None),
    )
    return jax.shard_map(
        shards, mesh=fine, in_specs=placed, out_specs=P(SEQ_AXES, "section"), check_vma=False
    )
```

```python
import math

import jax
import jax.numpy as jnp
from jax import lax
from jax.experimental import pallas as pl
from jax.experimental.pallas import tpu as pltpu
from jax.sharding import Mesh
from jax.sharding import PartitionSpec as P

HS = 64
RB = 16
ROWS = 256
N_SECTION = 4
N_Z, N_Y, N_CORE = 16, 4, 2
SEQ_AXES = ("z", "y", "core")
F32 = jnp.float32
BF16 = jnp.bfloat16


def layer_norm(values, gain_vec):
    row_mean = jnp.mean(values, axis=-1, keepdims=True)
    centered = values - row_mean
    variance = jnp.mean(centered * centered, axis=-1, keepdims=True)
    return centered * lax.rsqrt(variance + 1e-06) * gain_vec


def conv_norm(tile_maps, dw_weight, dw_bias, ln1_gain):
    map_side = tile_maps.shape[1]
    kernel = dw_weight.shape[0]
    half_width = (kernel - 1) // 2
    source = tile_maps.astype(F32)
    padded = jnp.pad(source, ((0, 0), (half_width, half_width), (half_width, half_width), (0, 0)))
    conv_sum = jnp.zeros_like(source) + dw_bias
    for row_off in range(kernel):
        for col_off in range(kernel):
            conv_sum = (
                conv_sum
                + padded[:, row_off : row_off + map_side, col_off : col_off + map_side, :]
                * dw_weight[row_off, col_off]
            )
    channels = source.shape[-1]
    return layer_norm(conv_sum, ln1_gain).astype(BF16).reshape(-1, channels)


def rotate(block, axis, size, step):
    return lax.ppermute(block, axis, [(i, (i + step) % size) for i in range(size)])


def spread(block, axis, size):
    return lax.all_to_all(
        jnp.broadcast_to(block[None], (size,) + block.shape), axis, 0, 0, tiled=True
    )


NT = (((1,), (1,)), ((), ()))


def dot(a, b):
    return jnp.dot(a, b, preferred_element_type=F32)


def gelu_mean(pre, tiles):
    hidden = (0.5 * pre * (1.0 + lax.erf(pre * (1.0 / math.sqrt(2.0))))).astype(BF16).astype(F32)
    return jnp.mean(hidden.reshape(tiles, hidden.shape[0] // tiles, hidden.shape[1]), axis=1)


def lanes(ref, index, width):
    return ref[:, pl.ds(pl.multiple_of(index * width, 128), width)]


def pack_kernel(core_ref, w_up, w_down, w_head, w_in, bias, first, second, sems):
    n = w_up.shape[0]
    start = pl.multiple_of(core_ref[0] * n, n)
    copies = [
        pltpu.make_async_copy(part, out.at[pl.ds(k * n, n), :], sems.at[k, slot])
        for out, slot, k, part in (
            (first, 0, 0, w_up.at[:, pl.ds(start, n)]),
            (first, 0, 1, w_down.at[:, pl.ds(start, n)]),
            (second, 1, 0, w_head.at[pl.ds(start, n), :]),
            (second, 1, 1, w_in.at[:, pl.ds(start, n)]),
        )
    ]
    for copy in copies:
        copy.start()
    second[2 * n :, :] = jnp.broadcast_to(bias[...][None, :], (16, n))
    for copy in copies:
        copy.wait()


def pack(core, w_up, w_down, w_head, w_in, bias):
    n = w_up.shape[0]
    vmem = pl.BlockSpec(memory_space=pltpu.VMEM)
    return pl.pallas_call(
        pack_kernel,
        in_specs=[pl.BlockSpec(memory_space=pltpu.SMEM)]
        + [pl.BlockSpec(memory_space=pl.ANY)] * 4
        + [vmem],
        out_specs=(vmem, vmem),
        out_shape=(
            jax.ShapeDtypeStruct((2 * n, n), BF16),
            jax.ShapeDtypeStruct((2 * n + 16, n), BF16),
        ),
        scratch_shapes=[pltpu.SemaphoreType.DMA((2, 2))],
        cost_estimate=pl.CostEstimate(flops=0, bytes_accessed=4 * n * n * 4, transcendentals=0),
    )(core.astype(jnp.int32)[None], w_up, w_down, w_head, w_in, bias)


def early_kernel(
    where, maps, up, bias, w_in, prior,
    left, right, left_swap, right_swap, left2, right2, left2_swap, right2_swap, hid, x_prior,
):
    core = where[0]
    n = up.shape[0]
    tiles = hid.shape[1]
    maps_a, maps_b = lanes(maps, core, n), lanes(maps, 1 - core, n)
    pre = lax.dot_general(maps[...], up[...], NT, preferred_element_type=F32)
    hid[0] = gelu_mean(pre + bias[...].astype(F32), tiles)
    own = dot(lanes(prior, where[1], n), w_in[...])
    x_a = jnp.zeros((prior.shape[0], n), F32)
    x_b = x_a
    sides = ((left, left_swap, left2, left2_swap), (right, right_swap, right2, right2_swap))
    for slot, (a, b, a2, b2) in enumerate(sides):
        pre = lax.dot_general(maps_a, a[0:n, :], NT, preferred_element_type=F32)
        pre += lax.dot_general(maps_b, b[0:n, :], NT, preferred_element_type=F32)
        hid[slot + 1] = gelu_mean(pre + a2[2 * n : 2 * n + 1, :].astype(F32), tiles)
        columns = lanes(prior, where[slot + 2], n)
        x_a += dot(columns, a2[n : 2 * n, :])
        x_b += dot(columns, b2[n : 2 * n, :])
    x_prior[...] = own + natural(core, x_a, x_b)


def natural(core, a, b):
    return jnp.where(core == 0, jnp.concatenate([a, b], 1), jnp.concatenate([b, a], 1))


def late_kernel(
    where, maps, prior, hid, x_prior, feat_mean, layer_scale, b_down, lnf_gain, bucket, row_code,
    w_down, w_head, w_in,
    left, right, left_swap, right_swap, left2, right2, left2_swap, right2_swap,
    low, high, low_swap, high_swap, payload, slot_x,
):
    core = where[0]
    n = w_down.shape[0]
    tiles = hid.shape[1]
    pre = lax.dot_general(lanes(maps, core, n), low[0:n, :], NT, preferred_element_type=F32)
    pre += lax.dot_general(
        lanes(maps, 1 - core, n), low_swap[0:n, :], NT, preferred_element_type=F32
    )
    hid_far = gelu_mean(pre + high[2 * n : 2 * n + 1, :].astype(F32), tiles)

    def exact(block):
        upper = block.astype(BF16)
        lower = (block - upper.astype(F32)).astype(BF16)
        return jnp.concatenate([upper.astype(F32), lower.astype(F32)], 0).astype(BF16)

    def folded(block):
        return block[0:tiles] + block[tiles : 2 * tiles]

    sides = ((left, left_swap), (right, right_swap))
    own = dot(exact(hid[0]), w_down[...])
    part = exact(hid_far)
    br_a, br_b = dot(part, low[n : 2 * n, :]), dot(part, low_swap[n : 2 * n, :])
    for slot, (a, b) in enumerate(sides):
        part = exact(hid[slot + 1])
        br_a += dot(part, a[n : 2 * n, :])
        br_b += dot(part, b[n : 2 * n, :])
    branch = folded(own + natural(core, br_a, br_b))
    pooled = feat_mean[...] + layer_scale[...] * (branch + b_down[...])
    feature = layer_norm(pooled, lnf_gain[...])
    first, second = feature[:, 0:n], feature[:, n : 2 * n]
    feature_a = jnp.where(core == 0, first, second).astype(BF16)
    feature_b = jnp.where(core == 0, second, first).astype(BF16)
    emb = dot(feature.astype(BF16), w_head[...]).astype(BF16)
    own = dot(emb, w_in[...])
    emb = (dot(feature_a, high[0:n, :]) + dot(feature_b, high_swap[0:n, :])).astype(BF16)
    columns = lanes(prior, where[4], n)
    x_a, x_b = dot(emb, high[n : 2 * n, :]), dot(emb, high_swap[n : 2 * n, :])
    p_a, p_b = dot(columns, high[n : 2 * n, :]), dot(columns, high_swap[n : 2 * n, :])
    for a, b in ((left2, left2_swap), (right2, right2_swap)):
        emb = (dot(feature_a, a[0:n, :]) + dot(feature_b, b[0:n, :])).astype(BF16)
        x_a += dot(emb, a[n : 2 * n, :])
        x_b += dot(emb, b[n : 2 * n, :])
    slot_x[0:tiles, :] = own + natural(core, x_a, x_b)
    slot_x[tiles:, :] = x_prior[...] + natural(core, p_a, p_b)
    places = lax.broadcasted_iota(jnp.int32, (payload.shape[0], bucket.shape[1]), 0)
    select = jnp.where(places == bucket[...], 1.0, 0.0).astype(BF16)
    width = slot_x.shape[1]
    payload[:, 0:width] = dot(select, slot_x[...].astype(BF16)).astype(BF16)
    payload[:, width:] = dot(select, row_code[...]).astype(BF16)


def local_call(body, outs, scratch, flops, size, *operands):
    vmem = pl.BlockSpec(memory_space=pltpu.VMEM)
    return pl.pallas_call(
        body,
        in_specs=[pl.BlockSpec(memory_space=pltpu.SMEM)] + [vmem] * (len(operands) - 1),
        out_specs=jax.tree.map(lambda _: vmem, outs),
        out_shape=outs,
        scratch_shapes=scratch,
        compiler_params=pltpu.CompilerParams(vmem_limit_bytes=48 * 2**20),
        cost_estimate=pl.CostEstimate(flops=flops, bytes_accessed=size, transcendentals=0),
    )(*operands)


def head_lanes(shape, head):
    lane = lax.broadcasted_iota(jnp.int32, shape, len(shape) - 1)
    return (lane >= head * HS) & (lane < (head + 1) * HS)


def dilated(shape, off_lane):
    return lax.rem(lax.broadcasted_iota(jnp.int32, shape, 0), RB) == off_lane


def project_kernel(x, ln_gain, w_q, w_k, w_v, q_gain, k_gain, off_lane, q, k, v, far_q, far_kv):
    rows, width = q.shape
    normed = layer_norm(x[...].astype(F32), ln_gain[...]).astype(BF16)
    chosen = dilated((rows, width), off_lane[...])

    def unit(raw, gain):
        raw = raw.astype(BF16).astype(F32)
        square = raw * raw
        mean = jnp.zeros_like(raw)
        for head in range(width // HS):
            inside = head_lanes(raw.shape, head)
            total = jnp.sum(jnp.where(inside, square, 0.0), axis=1, keepdims=True) * (1.0 / HS)
            mean = jnp.where(inside, total, mean)
        return (raw * lax.rsqrt(mean + 1e-06) * gain).astype(BF16)

    def far_rows(part):
        kept = jnp.where(chosen, part.astype(F32), 0.0)
        return jnp.sum(kept.reshape(rows // RB, RB, width), axis=1)

    q_rows = unit(dot(normed, w_q[...]), q_gain[...])
    k_rows = unit(dot(normed, w_k[...]), k_gain[...])
    v_rows = dot(normed, w_v[...]).astype(BF16)
    q[...], k[...], v[...] = q_rows, k_rows, v_rows
    far_q[...] = far_rows(q_rows)
    far_kv[...] = jnp.concatenate([far_rows(k_rows), far_rows(v_rows)], axis=1).astype(BF16)


def by_head(block):
    heads = block.shape[1] // HS
    wide = block.astype(F32)
    kept = [jnp.where(head_lanes(wide.shape, head), wide, 0.0) for head in range(heads)]
    return jnp.concatenate(kept, axis=0)


def back(block, rows, width):
    out = jnp.zeros((rows, width), F32)
    for head in range(width // HS):
        part = jnp.broadcast_to(block[head * rows : (head + 1) * rows], (rows, width))
        out = jnp.where(head_lanes(out.shape, head), part, out)
    return out


def weigh(queries, keys, values):
    scores = lax.dot_general(queries, keys, NT, preferred_element_type=F32)
    weights = jnp.exp(scores * (1.0 / math.sqrt(HS)))
    return jnp.sum(weights, axis=1, keepdims=True), dot(weights.astype(BF16), values)


def far_part(far_q, kv):
    rows, width = far_q.shape
    spread_q = by_head(far_q[...])
    spread_q = jnp.concatenate([spread_q, jnp.zeros_like(spread_q)], axis=1).astype(BF16)
    den, num = weigh(spread_q, kv[...], kv[...])
    return back(den, rows, width), back(num[:, width:], rows, width)


def near_kernel(where, q, k, v, far_q, kv, x, den, num, far_den, far_num, residual):
    wanted = lax.broadcasted_iota(jnp.int32, (residual.shape[0], x.shape[1]), 0)
    column = lax.broadcasted_iota(jnp.int32, (residual.shape[0], x.shape[1]), 1)
    pick = jnp.where(column == wanted + where[1] * residual.shape[0], 1.0, 0.0).astype(BF16)
    residual[...] = lax.dot_general(pick, x[...], NT, preferred_element_type=F32)
    rows, width = q.shape
    local_den, local_num = weigh(by_head(q[...]).astype(BF16), k[...], v[...])
    den[...] = back(local_den, rows, width)
    num[...] = back(local_num, rows, width)
    far_den[...], far_num[...] = far_part(far_q, kv)


def far_kernel(far_q, kv, off_lane, den, num, far_den, far_num, w_out, out):
    rows, width = num.shape
    chosen = dilated((rows, width), off_lane[...])
    more_den, more_num = far_part(far_q, kv)

    def placed(block):
        wide = jnp.broadcast_to(block[:, None, :], (rows // RB, RB, width))
        return jnp.where(chosen, wide.reshape(rows, width), 0.0)

    attended = (num[...] + placed(far_num[...] + more_num)) / (
        den[...] + placed(far_den[...] + more_den)
    )
    attended = attended.astype(BF16)
    out[...] = lax.dot_general(w_out[...], attended, NT, preferred_element_type=F32).astype(BF16)


def sum_kernel(residual, parts, out):
    total = residual[...]
    for part in range(parts.shape[0]):
        total += parts[part].astype(F32)
    out[...] = total.astype(BF16)


def vmem_call(body, outs, flops, size, exps, *operands):
    vmem = pl.BlockSpec(memory_space=pltpu.VMEM)
    return pl.pallas_call(
        body,
        in_specs=[vmem] * len(operands),
        out_specs=jax.tree.map(lambda _: vmem, outs),
        out_shape=outs,
        compiler_params=pltpu.CompilerParams(vmem_limit_bytes=40 * 2**20),
        cost_estimate=pl.CostEstimate(flops=flops, bytes_accessed=size, transcendentals=exps),
    )(*operands)


def shards(
    feats,
    dw_weight,
    dw_bias,
    ln1_gain,
    w_up,
    b_up,
    w_down,
    b_down,
    layer_scale,
    lnf_gain,
    w_head,
    prior,
    counts,
    positions,
    w_in,
    ln_gain,
    w_qkv,
    qn_gain,
    kn_gain,
    offsets,
    w_out,
):
    n_section = N_SECTION
    n_seq = N_Z * N_Y * N_CORE
    section_idx = lax.axis_index("section")
    core = lax.axis_index("core")
    tiles = feats.shape[0]
    channels = feats.shape[3]
    half = channels // N_CORE
    share = w_up.shape[0]

    first, second = pack(core, w_up, w_down, w_head, w_in, b_up)
    left = rotate(first, "section", N_SECTION, 1)
    right2 = rotate(second, "section", N_SECTION, -1)
    left2 = rotate(second, "section", N_SECTION, 1)
    right = rotate(first, "section", N_SECTION, -1)
    normed_maps = conv_norm(feats, dw_weight, dw_bias, ln1_gain)
    left, right2, normed_maps = lax.optimization_barrier((left, right2, normed_maps))
    low = rotate(left, "section", N_SECTION, 1)
    high = rotate(right2, "section", N_SECTION, -1)
    left, right2, left2, right = lax.optimization_barrier((left, right2, left2, right))
    left_swap = rotate(left, "core", N_CORE, 1)
    right_swap = rotate(right, "core", N_CORE, 1)
    left2_swap = rotate(left2, "core", N_CORE, 1)
    right2_swap = rotate(right2, "core", N_CORE, 1)
    low_swap = rotate(low, "core", N_CORE, 1)
    high_swap = rotate(high, "core", N_CORE, 1)

    slot_total = tiles + prior.shape[0]
    q_rows = ROWS // n_section
    capacity = -(-slot_total // n_seq)
    slot_ids = jnp.arange(slot_total)
    live_mask = slot_ids < tiles + counts[0]
    dest_shard = positions // ROWS
    row_in = positions % ROWS - section_idx * q_rows
    earlier = (
        (dest_shard[None, :] == dest_shard[:, None])
        & (slot_ids[None, :] < slot_ids[:, None])
        & live_mask[None, :]
    )
    within = jnp.sum(earlier.astype(jnp.int32), axis=1)
    bucket = jnp.where(live_mask, dest_shard * capacity + within, -1)
    row_code = jnp.broadcast_to((row_in + 1).astype(BF16)[:, None], (slot_total, 128))

    feat_mean = jnp.mean(feats.astype(F32), axis=(1, 2))
    where = jnp.stack(
        [core, section_idx, (section_idx + 3) % 4, (section_idx + 1) % 4, (section_idx + 2) % 4]
    ).astype(jnp.int32)
    row = lambda vec: vec[None, :]
    hid, x_prior = local_call(
        early_kernel,
        (
            jax.ShapeDtypeStruct((3, tiles, share), F32),
            jax.ShapeDtypeStruct((prior.shape[0], channels), F32),
        ),
        [],
        2_000_000_000,
        6_000_000,
        where, normed_maps, w_up, row(b_up), w_in, prior, left, right, left_swap, right_swap,
        left2, right2, left2_swap, right2_swap,
    )
    payload = local_call(
        late_kernel,
        jax.ShapeDtypeStruct((n_seq * capacity, channels + 128), BF16),
        [pltpu.VMEM((slot_total, channels), F32)],
        2_000_000_000,
        8_000_000,
        where, normed_maps, prior, hid, x_prior, feat_mean, row(layer_scale), row(b_down),
        row(lnf_gain), row(bucket), row_code, w_down, w_head, w_in, left, right, left_swap,
        right_swap, left2, right2, left2_swap, right2_swap, low, high, low_swap, high_swap,
    )

    got = lax.all_to_all(
        payload.reshape(n_seq, capacity, payload.shape[1]), SEQ_AXES, 0, 0, tiled=True
    ).reshape(n_seq * capacity, payload.shape[1])
    code = got[:, channels].astype(F32)
    placer = (jnp.arange(1, q_rows + 1).astype(F32)[:, None] == code[None, :]).astype(BF16)
    x_local = dot(placer, got[:, :channels]).astype(BF16)
    x_rows = spread(x_local, "section", n_section).reshape(ROWS, channels)

    heads_here = w_qkv.shape[1] // (3 * HS)
    width = heads_here * HS
    stride_rows = ROWS // RB
    my_offsets = lax.dynamic_slice_in_dim(offsets, section_idx * heads_here, heads_here)
    off_lane = row(jnp.repeat(my_offsets, HS))
    w_q, w_k, w_v = (w_qkv[:, part * width : (part + 1) * width] for part in range(3))
    small = lambda rows, kind: jax.ShapeDtypeStruct((rows, width), kind)
    q, k, v, far_q, far_kv = vmem_call(
        project_kernel,
        (small(ROWS, BF16),) * 3
        + (small(stride_rows, F32), jax.ShapeDtypeStruct((stride_rows, 2 * width), BF16)),
        300_000_000,
        2_000_000,
        0,
        x_rows, row(ln_gain), w_q, w_k, w_v, row(jnp.tile(qn_gain, heads_here)),
        row(jnp.tile(kn_gain, heads_here)), off_lane,
    )
    z_kv = spread(far_kv, "z", N_Z).reshape(N_Z * stride_rows, 2 * width)
    half_kv = lax.all_gather(z_kv, "y", axis=0, tiled=True)
    other_kv = rotate(half_kv, "core", N_CORE, 1)
    width_part = channels // n_section
    den, num, far_den, far_num, residual = local_call(
        near_kernel,
        (small(ROWS, F32),) * 2
        + (small(stride_rows, F32),) * 2
        + (jax.ShapeDtypeStruct((width_part, ROWS), F32),),
        [],
        2_000_000_000,
        2_000_000,
        where, q, k, v, far_q, half_kv, x_rows,
    )
    partial_out = vmem_call(
        far_kernel,
        jax.ShapeDtypeStruct((channels, ROWS), BF16),
        150_000_000,
        2_000_000,
        50_000,
        far_q, other_kv, off_lane, den, num, far_den, far_num,
        jnp.transpose(w_out),
    )
    parts = lax.all_to_all(
        partial_out.reshape(n_section, width_part, ROWS), "section", 0, 0, tiled=True
    )
    total = vmem_call(
        sum_kernel,
        jax.ShapeDtypeStruct((width_part, ROWS), BF16),
        1_000_000,
        1_000_000,
        0,
        residual, parts,
    )
    return jnp.transpose(total)


def solution(mesh):
    fine = Mesh(
        mesh.devices.reshape(N_SECTION, N_Z, N_Y, N_CORE), ("section",) + SEQ_AXES
    )
    both = ("section",) + SEQ_AXES
    placed = (
        P(both, None, None, None),
        P(),
        P(),
        P(),
        P("section", None),
        P("section"),
        P("section", None),
        P(),
        P(),
        P(),
        P(None, "section"),
        P(both, None),
        P(both),
        P(both),
        P("section", None),
        P(),
        P(None, "section"),
        P(),
        P(),
        P(),
        P("section", None),
    )
    return jax.shard_map(
        shards, mesh=fine, in_specs=placed, out_specs=P(SEQ_AXES, "section"), check_vma=False
    )
```

```python
import math

import jax
import jax.numpy as jnp
from jax import lax
from jax.experimental import pallas as pl
from jax.experimental.pallas import tpu as pltpu
from jax.sharding import Mesh
from jax.sharding import PartitionSpec as P

HS = 64
RB = 16
ROWS = 256
N_SECTION = 4
N_Z, N_Y, N_CORE = 16, 4, 2
SEQ_AXES = ("z", "y", "core")
F32 = jnp.float32
BF16 = jnp.bfloat16


def layer_norm(values, gain_vec):
    row_mean = jnp.mean(values, axis=-1, keepdims=True)
    centered = values - row_mean
    variance = jnp.mean(centered * centered, axis=-1, keepdims=True)
    return centered * lax.rsqrt(variance + 1e-06) * gain_vec


def rotate(block, axis, size, step):
    return lax.ppermute(block, axis, [(i, (i + step) % size) for i in range(size)])


def spread(block, axis, size):
    return lax.all_to_all(
        jnp.broadcast_to(block[None], (size,) + block.shape), axis, 0, 0, tiled=True
    )


NT = (((1,), (1,)), ((), ()))


def dot(a, b):
    return jnp.dot(a, b, preferred_element_type=F32)


def gelu_mean(pre, tiles):
    hidden = (0.5 * pre * (1.0 + lax.erf(pre * (1.0 / math.sqrt(2.0))))).astype(BF16).astype(F32)
    return jnp.mean(hidden.reshape(tiles, hidden.shape[0] // tiles, hidden.shape[1]), axis=1)


def lanes(ref, index, width):
    return ref[:, pl.ds(pl.multiple_of(index * width, 128), width)]


def pack_kernel(core_ref, w_up, w_down, w_head, w_in, bias, out, sems):
    n = w_up.shape[0]
    start = pl.multiple_of(core_ref[0] * n, n)
    parts = (
        w_up.at[:, pl.ds(start, n)],
        w_down.at[:, pl.ds(start, n)],
        w_head.at[pl.ds(start, n), :],
        w_in.at[:, pl.ds(start, n)],
    )
    copies = [
        pltpu.make_async_copy(part, out.at[pl.ds(k * n, n), :], sems.at[k])
        for k, part in enumerate(parts)
    ]
    for copy in copies:
        copy.start()
    out[4 * n :, :] = jnp.broadcast_to(bias[...][None, :], (16, n))
    for copy in copies:
        copy.wait()


def pack(core, w_up, w_down, w_head, w_in, bias):
    n = w_up.shape[0]
    vmem = pl.BlockSpec(memory_space=pltpu.VMEM)
    return pl.pallas_call(
        pack_kernel,
        in_specs=[pl.BlockSpec(memory_space=pltpu.SMEM)]
        + [pl.BlockSpec(memory_space=pl.ANY)] * 4
        + [vmem],
        out_specs=vmem,
        out_shape=jax.ShapeDtypeStruct((4 * n + 16, n), BF16),
        scratch_shapes=[pltpu.SemaphoreType.DMA((4,))],
        cost_estimate=pl.CostEstimate(flops=0, bytes_accessed=4 * n * n * 4, transcendentals=0),
    )(core.astype(jnp.int32)[None], w_up, w_down, w_head, w_in, bias)


def natural(core, a, b):
    return jnp.where(core == 0, jnp.concatenate([a, b], 1), jnp.concatenate([b, a], 1))


def conv_kernel(feats, dw_weight, dw_bias, gain, out, mean, conv):
    tiles, side, _, channels = feats.shape
    taps = math.isqrt(dw_weight.shape[0])
    reach = (taps - 1) // 2
    column = lax.broadcasted_iota(jnp.int32, (side, side, 128), 1)
    tile_row = lax.broadcasted_iota(jnp.int32, (tiles, 128), 0)
    mean[...] = jnp.zeros_like(mean)

    def one_tile(tile, carry):
        for chunk in range(channels // 128):
            cols = pl.ds(chunk * 128, 128)
            source = feats[tile, :, :, cols].astype(F32)
            total = jnp.sum(jnp.sum(source, axis=0), axis=0, keepdims=True)
            total = jnp.broadcast_to(total * (1.0 / (side * side)), (tiles, 128))
            mean[:, cols] = jnp.where(tile_row == tile, total, mean[:, cols])
            bias = jnp.broadcast_to(dw_bias[0:1, cols], (side, 128))
            sums = [bias] * side
            for b in range(taps):
                move = b - reach
                moved = source
                if move:
                    moved = pltpu.roll(source, (-move) % side, 1)
                    inside = (column + move >= 0) & (column + move < side)
                    moved = jnp.where(inside, moved, 0.0)
                for a in range(taps):
                    tap = dw_weight[a * taps + b : a * taps + b + 1, cols]
                    tap = jnp.broadcast_to(tap, (side, 128))
                    for i in range(side):
                        if 0 <= i + a - reach < side:
                            sums[i] = sums[i] + moved[i + a - reach] * tap
            for i in range(side):
                conv[i * side : (i + 1) * side, cols] = sums[i]
        start = pl.multiple_of(tile * side * side, side * side)
        out[pl.ds(start, side * side), :] = layer_norm(conv[...], gain[...]).astype(BF16)
        return carry

    lax.fori_loop(0, tiles, one_tile, 0)


def early_kernel(where, maps, up, bias, left, right, left_swap, right_swap, hid):
    core = where[0]
    n = up.shape[0]
    tiles = hid.shape[1]
    maps_a, maps_b = lanes(maps, core, n), lanes(maps, 1 - core, n)
    pre = lax.dot_general(maps[...], up[...], NT, preferred_element_type=F32)
    hid[0] = gelu_mean(pre + bias[...].astype(F32), tiles)
    for slot, (a, b) in enumerate(((left, left_swap), (right, right_swap))):
        pre = lax.dot_general(maps_a, a[0:n, :], NT, preferred_element_type=F32)
        pre += lax.dot_general(maps_b, b[0:n, :], NT, preferred_element_type=F32)
        hid[slot + 1] = gelu_mean(pre + a[4 * n : 4 * n + 1, :].astype(F32), tiles)


def late_kernel(
    where, maps, hid, feat_mean, layer_scale, b_down, lnf_gain, code, w_down, w_head, w_in,
    left, right, left_swap, right_swap, low, high, low_swap, high_swap, out,
):
    core = where[0]
    n = w_down.shape[0]
    tiles = hid.shape[1]
    pre = lax.dot_general(lanes(maps, core, n), low[0:n, :], NT, preferred_element_type=F32)
    pre += lax.dot_general(
        lanes(maps, 1 - core, n), low_swap[0:n, :], NT, preferred_element_type=F32
    )
    hid_far = gelu_mean(pre + high[2 * n : 2 * n + 1, :].astype(F32), tiles)

    def exact(block):
        upper = block.astype(BF16)
        lower = (block - upper.astype(F32)).astype(BF16)
        return jnp.concatenate([upper.astype(F32), lower.astype(F32)], 0).astype(BF16)

    sides = ((left, left_swap), (right, right_swap))
    own = dot(exact(hid[0]), w_down[...])
    part = exact(hid_far)
    br_a, br_b = dot(part, low[n : 2 * n, :]), dot(part, low_swap[n : 2 * n, :])
    for slot, (a, b) in enumerate(sides):
        part = exact(hid[slot + 1])
        br_a += dot(part, a[n : 2 * n, :])
        br_b += dot(part, b[n : 2 * n, :])
    branch = own + natural(core, br_a, br_b)
    branch = branch[0:tiles] + branch[tiles : 2 * tiles]
    pooled = feat_mean[...] + layer_scale[...] * (branch + b_down[...])
    feature = layer_norm(pooled, lnf_gain[...])
    first, second = feature[:, 0:n], feature[:, n : 2 * n]
    feature_a = jnp.where(core == 0, first, second).astype(BF16)
    feature_b = jnp.where(core == 0, second, first).astype(BF16)
    emb = dot(feature.astype(BF16), w_head[...]).astype(BF16)
    own = dot(emb, w_in[...])
    emb = (dot(feature_a, high[0:n, :]) + dot(feature_b, high_swap[0:n, :])).astype(BF16)
    x_a, x_b = dot(emb, high[n : 2 * n, :]), dot(emb, high_swap[n : 2 * n, :])
    for a, b in sides:
        emb = dot(feature_a, a[2 * n : 3 * n, :]) + dot(feature_b, b[2 * n : 3 * n, :])
        emb = emb.astype(BF16)
        x_a += dot(emb, a[3 * n : 4 * n, :])
        x_b += dot(emb, b[3 * n : 4 * n, :])
    x_fresh = own + natural(core, x_a, x_b)
    out[...] = jnp.concatenate([x_fresh, code[...]], axis=1).astype(BF16)


def select_kernel(bucket, rows, code, out):
    places = lax.broadcasted_iota(jnp.int32, (out.shape[0], bucket.shape[1]), 0)
    select = jnp.where(places == bucket[...], 1.0, 0.0).astype(BF16)
    width = rows.shape[1]
    out[:, 0:width] = dot(select, rows[...]).astype(BF16)
    out[:, width:] = dot(select, code[...]).astype(BF16)


def column_as_row(ref, column):
    lane = lax.broadcasted_iota(jnp.int32, (8, 128), 1)
    unit_row = jnp.where(lane == column, 1.0, 0.0).astype(BF16)
    tail = ref[:, ref.shape[1] - 128 :]
    return lax.dot_general(unit_row, tail, NT, preferred_element_type=F32)[0:1, :]


def place_rows(got, q_rows):
    code = column_as_row(got, 0)
    places = lax.broadcasted_iota(jnp.int32, (q_rows, got.shape[0]), 0).astype(F32) + 1.0
    placer = jnp.where(places == code, 1.0, 0.0).astype(BF16)
    return dot(placer, got[:, 0 : got.shape[1] - 128])


def earlier_kernel(
    where, got, w_in, left, right, left_swap, right_swap, high, high_swap, out, rows
):
    n = w_in.shape[0]
    rows[...] = place_rows(got, out.shape[0]).astype(BF16)
    own = dot(lanes(rows, where[1], n), w_in[...])
    columns = lanes(rows, where[4], n)
    x_a, x_b = dot(columns, high[n : 2 * n, :]), dot(columns, high_swap[n : 2 * n, :])
    for slot, (a, b) in enumerate(((left, left_swap), (right, right_swap))):
        columns = lanes(rows, where[slot + 2], n)
        x_a += dot(columns, a[3 * n : 4 * n, :])
        x_b += dot(columns, b[3 * n : 4 * n, :])
    out[...] = own + natural(where[0], x_a, x_b)


def scatter_kernel(where, rows, out):
    count = rows.shape[0]
    dest_row = column_as_row(rows, 1)
    dest = rows[:, rows.shape[1] - 128 :].astype(F32)[:, 1:2]
    index_a = lax.broadcasted_iota(jnp.int32, (count, count), 0)
    index_b = lax.broadcasted_iota(jnp.int32, (count, count), 1)
    before = jnp.where((dest == dest_row) & (index_a < index_b), 1.0, 0.0)
    rank = jnp.sum(before, axis=0, keepdims=True).astype(jnp.int32)
    shard = dest_row.astype(jnp.int32)
    plane = N_Y * N_CORE
    room = out.shape[0] // plane
    inside = shard - where[5] * plane
    bucket = jnp.where((inside >= 0) & (inside < plane), inside * room + rank, -1)
    places = lax.broadcasted_iota(jnp.int32, (out.shape[0], count), 0)
    select = jnp.where(places == bucket, 1.0, 0.0).astype(BF16)
    out[...] = dot(select, rows[...]).astype(BF16)


def arrive_kernel(got, earlier, out):
    out[...] = (place_rows(got, out.shape[0]) + earlier[...]).astype(BF16)


def local_call(body, outs, scratch, flops, size, *operands):
    vmem = pl.BlockSpec(memory_space=pltpu.VMEM)
    return pl.pallas_call(
        body,
        in_specs=[pl.BlockSpec(memory_space=pltpu.SMEM)] + [vmem] * (len(operands) - 1),
        out_specs=jax.tree.map(lambda _: vmem, outs),
        out_shape=outs,
        scratch_shapes=scratch,
        compiler_params=pltpu.CompilerParams(vmem_limit_bytes=48 * 2**20),
        cost_estimate=pl.CostEstimate(flops=flops, bytes_accessed=size, transcendentals=0),
    )(*operands)


def head_lanes(shape, head):
    lane = lax.broadcasted_iota(jnp.int32, shape, len(shape) - 1)
    return (lane >= head * HS) & (lane < (head + 1) * HS)


def dilated(shape, off_lane):
    return lax.rem(lax.broadcasted_iota(jnp.int32, shape, 0), RB) == off_lane


def project_kernel(x, ln_gain, w_q, w_k, w_v, q_gain, k_gain, off_lane, q, k, v, far_q, far_kv):
    rows, width = q.shape
    normed = layer_norm(x[...].astype(F32), ln_gain[...]).astype(BF16)
    chosen = dilated((rows, width), off_lane[...])

    def unit(raw, gain):
        raw = raw.astype(BF16).astype(F32)
        square = raw * raw
        mean = jnp.zeros_like(raw)
        for head in range(width // HS):
            inside = head_lanes(raw.shape, head)
            total = jnp.sum(jnp.where(inside, square, 0.0), axis=1, keepdims=True) * (1.0 / HS)
            mean = jnp.where(inside, total, mean)
        return (raw * lax.rsqrt(mean + 1e-06) * gain).astype(BF16)

    def far_rows(part):
        kept = jnp.where(chosen, part.astype(F32), 0.0)
        return jnp.sum(kept.reshape(rows // RB, RB, width), axis=1)

    q_rows = unit(dot(normed, w_q[...]), q_gain[...])
    k_rows = unit(dot(normed, w_k[...]), k_gain[...])
    v_rows = dot(normed, w_v[...]).astype(BF16)
    q[...], k[...], v[...] = q_rows, k_rows, v_rows
    far_q[...] = far_rows(q_rows)
    far_kv[...] = jnp.concatenate([far_rows(k_rows), far_rows(v_rows)], axis=1).astype(BF16)


def by_head(block):
    heads = block.shape[1] // HS
    wide = block.astype(F32)
    kept = [jnp.where(head_lanes(wide.shape, head), wide, 0.0) for head in range(heads)]
    return jnp.concatenate(kept, axis=0)


def back(block, rows, width):
    out = jnp.zeros((rows, width), F32)
    for head in range(width // HS):
        part = jnp.broadcast_to(block[head * rows : (head + 1) * rows], (rows, width))
        out = jnp.where(head_lanes(out.shape, head), part, out)
    return out


def weigh(queries, keys, values):
    scores = lax.dot_general(queries, keys, NT, preferred_element_type=F32)
    weights = jnp.exp(scores * (1.0 / math.sqrt(HS)))
    return jnp.sum(weights, axis=1, keepdims=True), dot(weights.astype(BF16), values)


def far_part(far_q, kv):
    rows, width = far_q.shape
    spread_q = by_head(far_q[...])
    spread_q = jnp.concatenate([spread_q, jnp.zeros_like(spread_q)], axis=1).astype(BF16)
    den, num = weigh(spread_q, kv[...], kv[...])
    return back(den, rows, width), back(num[:, width:], rows, width)


def near_kernel(where, q, k, v, far_q, kv, x, den, num, far_den, far_num, residual):
    wanted = lax.broadcasted_iota(jnp.int32, (residual.shape[0], x.shape[1]), 0)
    column = lax.broadcasted_iota(jnp.int32, (residual.shape[0], x.shape[1]), 1)
    pick = jnp.where(column == wanted + where[1] * residual.shape[0], 1.0, 0.0).astype(BF16)
    residual[...] = lax.dot_general(pick, x[...], NT, preferred_element_type=F32)
    rows, width = q.shape
    local_den, local_num = weigh(by_head(q[...]).astype(BF16), k[...], v[...])
    den[...] = back(local_den, rows, width)
    num[...] = back(local_num, rows, width)
    far_den[...], far_num[...] = far_part(far_q, kv)


def far_kernel(far_q, kv, off_lane, den, num, far_den, far_num, w_out, out):
    rows, width = num.shape
    chosen = dilated((rows, width), off_lane[...])
    more_den, more_num = far_part(far_q, kv)

    def placed(block):
        wide = jnp.broadcast_to(block[:, None, :], (rows // RB, RB, width))
        return jnp.where(chosen, wide.reshape(rows, width), 0.0)

    attended = (num[...] + placed(far_num[...] + more_num)) / (
        den[...] + placed(far_den[...] + more_den)
    )
    attended = attended.astype(BF16)
    out[...] = lax.dot_general(w_out[...], attended, NT, preferred_element_type=F32).astype(BF16)


def sum_kernel(residual, parts, out):
    total = residual[...]
    for part in range(parts.shape[0]):
        total += parts[part].astype(F32)
    out[...] = total.astype(BF16)


def vmem_call(body, outs, flops, size, exps, *operands, scratch=()):
    vmem = pl.BlockSpec(memory_space=pltpu.VMEM)
    return pl.pallas_call(
        body,
        in_specs=[vmem] * len(operands),
        out_specs=jax.tree.map(lambda _: vmem, outs),
        out_shape=outs,
        scratch_shapes=list(scratch),
        compiler_params=pltpu.CompilerParams(vmem_limit_bytes=40 * 2**20),
        cost_estimate=pl.CostEstimate(flops=flops, bytes_accessed=size, transcendentals=exps),
    )(*operands)


def shards(
    feats,
    dw_weight,
    dw_bias,
    ln1_gain,
    w_up,
    b_up,
    w_down,
    b_down,
    layer_scale,
    lnf_gain,
    w_head,
    prior,
    counts,
    positions,
    w_in,
    ln_gain,
    w_qkv,
    qn_gain,
    kn_gain,
    offsets,
    w_out,
):
    n_section = N_SECTION
    n_seq = N_Z * N_Y * N_CORE
    section_idx = lax.axis_index("section")
    core = lax.axis_index("core")
    tiles = feats.shape[0]
    channels = feats.shape[3]
    half = channels // N_CORE
    share = w_up.shape[0]

    row = lambda vec: vec[None, :]
    others = [(section_idx + step) % N_SECTION for step in (3, 1, 2)]
    where = jnp.stack([core, section_idx] + others + [lax.axis_index("z")]).astype(jnp.int32)

    block = pack(core, w_up, w_down, w_head, w_in, b_up)
    block, prior = lax.optimization_barrier((block, prior))
    left = rotate(block, "section", N_SECTION, 1)
    right = rotate(block, "section", N_SECTION, -1)

    q_rows = ROWS // n_section
    capacity = -(-(tiles + prior.shape[0]) // n_seq)
    slot_ids = jnp.arange(prior.shape[0])
    live_mask = slot_ids < counts[0]
    dest_shard = positions // ROWS
    row_code = (positions % ROWS - section_idx * q_rows + 1).astype(BF16)
    dest_prior = dest_shard[tiles:]
    earlier = (
        (dest_prior[None, :] == dest_prior[:, None])
        & (slot_ids[None, :] < slot_ids[:, None])
        & live_mask[None, :]
    )
    within = jnp.sum(earlier.astype(jnp.int32), axis=1)
    bucket = jnp.where(live_mask, dest_prior * capacity + within, -1)
    code_prior = jnp.broadcast_to(row_code[tiles:, None], (prior.shape[0], 128))
    send = vmem_call(
        select_kernel,
        jax.ShapeDtypeStruct((n_seq * capacity, prior.shape[1] + 128), BF16),
        200_000_000,
        2_000_000,
        0,
        row(bucket), prior, code_prior,
    )

    got_prior = lax.all_to_all(
        send.reshape(n_seq, capacity, send.shape[1]), SEQ_AXES, 0, 0, tiled=True
    ).reshape(send.shape)
    left, right, low_in, high_in, feats = lax.optimization_barrier(
        (left, right, left[: 2 * share], right[2 * share :], feats)
    )
    low = rotate(low_in, "section", N_SECTION, 1)
    high = rotate(high_in, "section", N_SECTION, -1)
    left_swap = rotate(left, "core", N_CORE, 1)
    right_swap = rotate(right, "core", N_CORE, 1)
    pixels = feats.shape[1] * feats.shape[2]
    normed_maps, feat_mean = vmem_call(
        conv_kernel,
        (
            jax.ShapeDtypeStruct((tiles * pixels, channels), BF16),
            jax.ShapeDtypeStruct((tiles, channels), F32),
        ),
        30_000_000_000,
        8_000_000,
        0,
        feats, dw_weight.reshape(-1, channels), row(dw_bias), row(ln1_gain),
        scratch=[pltpu.VMEM((pixels, channels), F32)],
    )
    low, high, normed_maps, feat_mean = lax.optimization_barrier(
        (low, high, normed_maps, feat_mean)
    )
    low_swap = rotate(low, "core", N_CORE, 1)
    high_swap = rotate(high, "core", N_CORE, 1)
    code_fresh = jnp.where(
        jnp.arange(128)[None, :] == 0,
        row_code[:tiles, None].astype(F32),
        dest_shard[:tiles, None].astype(F32),
    )
    hid = local_call(
        early_kernel,
        jax.ShapeDtypeStruct((3, tiles, share), F32),
        [],
        2_000_000_000,
        6_000_000,
        where, normed_maps, w_up, row(b_up), left, right, left_swap, right_swap,
    )
    got_prior, hid = lax.optimization_barrier((got_prior, hid))
    fresh = local_call(
        late_kernel,
        jax.ShapeDtypeStruct((tiles, channels + 128), BF16),
        [],
        2_000_000_000,
        8_000_000,
        where, normed_maps, hid, feat_mean, row(layer_scale), row(b_down), row(lnf_gain),
        code_fresh, w_down, w_head, w_in, left, right, left_swap, right_swap, low, high, low_swap,
        high_swap,
    )
    x_earlier = local_call(
        earlier_kernel,
        jax.ShapeDtypeStruct((q_rows, channels), F32),
        [pltpu.VMEM((q_rows, prior.shape[1]), BF16)],
        500_000_000,
        4_000_000,
        where, got_prior, w_in, left, right, left_swap, right_swap, high, high_swap,
    )

    fresh_z = spread(fresh, "z", N_Z).reshape(N_Z * tiles, channels + 128)
    plane = N_Y * N_CORE
    room = N_Z * capacity
    to_plane = local_call(
        scatter_kernel,
        jax.ShapeDtypeStruct((plane * room, channels + 128), BF16),
        [],
        60_000_000,
        1_000_000,
        where, fresh_z,
    )
    got = lax.all_to_all(
        to_plane.reshape(plane, room, channels + 128), ("y", "core"), 0, 0, tiled=True
    ).reshape(plane * room, channels + 128)
    x_local = vmem_call(
        arrive_kernel,
        jax.ShapeDtypeStruct((q_rows, channels), BF16),
        30_000_000,
        1_000_000,
        0,
        got, x_earlier,
    )
    x_rows = spread(x_local, "section", n_section).reshape(ROWS, channels)

    heads_here = w_qkv.shape[1] // (3 * HS)
    width = heads_here * HS
    stride_rows = ROWS // RB
    my_offsets = lax.dynamic_slice_in_dim(offsets, section_idx * heads_here, heads_here)
    off_lane = row(jnp.repeat(my_offsets, HS))
    w_q, w_k, w_v = (w_qkv[:, part * width : (part + 1) * width] for part in range(3))
    small = lambda rows, kind: jax.ShapeDtypeStruct((rows, width), kind)
    q, k, v, far_q, far_kv = vmem_call(
        project_kernel,
        (small(ROWS, BF16),) * 3
        + (small(stride_rows, F32), jax.ShapeDtypeStruct((stride_rows, 2 * width), BF16)),
        300_000_000,
        2_000_000,
        0,
        x_rows, row(ln_gain), w_q, w_k, w_v, row(jnp.tile(qn_gain, heads_here)),
        row(jnp.tile(kn_gain, heads_here)), off_lane,
    )
    z_kv = spread(far_kv, "z", N_Z).reshape(N_Z * stride_rows, 2 * width)
    half_kv = lax.all_gather(z_kv, "y", axis=0, tiled=True)
    other_kv = rotate(half_kv, "core", N_CORE, 1)
    width_part = channels // n_section
    den, num, far_den, far_num, residual = local_call(
        near_kernel,
        (small(ROWS, F32),) * 2
        + (small(stride_rows, F32),) * 2
        + (jax.ShapeDtypeStruct((width_part, ROWS), F32),),
        [],
        2_000_000_000,
        2_000_000,
        where, q, k, v, far_q, half_kv, x_rows,
    )
    partial_out = vmem_call(
        far_kernel,
        jax.ShapeDtypeStruct((channels, ROWS), BF16),
        150_000_000,
        2_000_000,
        50_000,
        far_q, other_kv, off_lane, den, num, far_den, far_num,
        jnp.transpose(w_out),
    )
    parts = lax.all_to_all(
        partial_out.reshape(n_section, width_part, ROWS), "section", 0, 0, tiled=True
    )
    total = vmem_call(
        sum_kernel,
        jax.ShapeDtypeStruct((width_part, ROWS), BF16),
        1_000_000,
        1_000_000,
        0,
        residual, parts,
    )
    return jnp.transpose(total)


def solution(mesh):
    fine = Mesh(
        mesh.devices.reshape(N_SECTION, N_Z, N_Y, N_CORE), ("section",) + SEQ_AXES
    )
    both = ("section",) + SEQ_AXES
    placed = (
        P(both, None, None, None),
        P(),
        P(),
        P(),
        P("section", None),
        P("section"),
        P("section", None),
        P(),
        P(),
        P(),
        P(None, "section"),
        P(both, None),
        P(both),
        P(both),
        P("section", None),
        P(),
        P(None, "section"),
        P(),
        P(),
        P(),
        P("section", None),
    )
    return jax.shard_map(
        shards, mesh=fine, in_specs=placed, out_specs=P(SEQ_AXES, "section"), check_vma=False
    )
```

```python
import math

import jax
import jax.numpy as jnp
from jax import lax
from jax.experimental import pallas as pl
from jax.experimental.pallas import tpu as pltpu
from jax.sharding import Mesh
from jax.sharding import PartitionSpec as P

HS = 64
RB = 16
ROWS = 256
N_SECTION = 4
N_Z, N_Y, N_CORE = 16, 4, 2
SEQ_AXES = ("z", "y", "core")
F32 = jnp.float32
BF16 = jnp.bfloat16


def layer_norm(values, gain_vec):
    row_mean = jnp.mean(values, axis=-1, keepdims=True)
    centered = values - row_mean
    variance = jnp.mean(centered * centered, axis=-1, keepdims=True)
    return centered * lax.rsqrt(variance + 1e-06) * gain_vec


def rotate(block, axis, size, step):
    return lax.ppermute(block, axis, [(i, (i + step) % size) for i in range(size)])


def spread(block, axis, size):
    return lax.all_to_all(
        jnp.broadcast_to(block[None], (size,) + block.shape), axis, 0, 0, tiled=True
    )


NT = (((1,), (1,)), ((), ()))


def dot(a, b):
    return jnp.dot(a, b, preferred_element_type=F32)


def gelu_mean(pre, tiles):
    hidden = (0.5 * pre * (1.0 + lax.erf(pre * (1.0 / math.sqrt(2.0))))).astype(BF16).astype(F32)
    return jnp.mean(hidden.reshape(tiles, hidden.shape[0] // tiles, hidden.shape[1]), axis=1)


def lanes(ref, index, width):
    return ref[:, pl.ds(pl.multiple_of(index * width, 128), width)]


def pack_kernel(core_ref, w_up, w_down, w_head, w_in, bias, out, sems):
    n = w_up.shape[0]
    start = pl.multiple_of(core_ref[0] * n, n)
    parts = (
        w_up.at[:, pl.ds(start, n)],
        w_down.at[:, pl.ds(start, n)],
        w_head.at[pl.ds(start, n), :],
        w_in.at[:, pl.ds(start, n)],
    )
    copies = [
        pltpu.make_async_copy(part, out.at[pl.ds(k * n, n), :], sems.at[k])
        for k, part in enumerate(parts)
    ]
    for copy in copies:
        copy.start()
    out[4 * n :, :] = jnp.broadcast_to(bias[...][None, :], (16, n))
    for copy in copies:
        copy.wait()


def pack(core, w_up, w_down, w_head, w_in, bias):
    n = w_up.shape[0]
    vmem = pl.BlockSpec(memory_space=pltpu.VMEM)
    return pl.pallas_call(
        pack_kernel,
        in_specs=[pl.BlockSpec(memory_space=pltpu.SMEM)]
        + [pl.BlockSpec(memory_space=pl.ANY)] * 4
        + [vmem],
        out_specs=vmem,
        out_shape=jax.ShapeDtypeStruct((4 * n + 16, n), BF16),
        scratch_shapes=[pltpu.SemaphoreType.DMA((4,))],
        cost_estimate=pl.CostEstimate(flops=0, bytes_accessed=4 * n * n * 4, transcendentals=0),
    )(core.astype(jnp.int32)[None], w_up, w_down, w_head, w_in, bias)


def natural(core, a, b):
    return jnp.where(core == 0, jnp.concatenate([a, b], 1), jnp.concatenate([b, a], 1))


def conv_kernel(feats, dw_weight, dw_bias, gain, out, mean, conv):
    tiles, side, _, channels = feats.shape
    taps = math.isqrt(dw_weight.shape[0])
    reach = (taps - 1) // 2
    column = lax.broadcasted_iota(jnp.int32, (side, side, 128), 1)
    tile_row = lax.broadcasted_iota(jnp.int32, (tiles, 128), 0)
    mean[...] = jnp.zeros_like(mean)

    def one_tile(tile, carry):
        for chunk in range(channels // 128):
            cols = pl.ds(chunk * 128, 128)
            source = feats[tile, :, :, cols].astype(F32)
            total = jnp.sum(jnp.sum(source, axis=0), axis=0, keepdims=True)
            total = jnp.broadcast_to(total * (1.0 / (side * side)), (tiles, 128))
            mean[:, cols] = jnp.where(tile_row == tile, total, mean[:, cols])
            bias = jnp.broadcast_to(dw_bias[0:1, cols], (side, 128))
            sums = [bias] * side
            for b in range(taps):
                move = b - reach
                moved = source
                if move:
                    moved = pltpu.roll(source, (-move) % side, 1)
                    inside = (column + move >= 0) & (column + move < side)
                    moved = jnp.where(inside, moved, 0.0)
                for a in range(taps):
                    tap = dw_weight[a * taps + b : a * taps + b + 1, cols]
                    tap = jnp.broadcast_to(tap, (side, 128))
                    for i in range(side):
                        if 0 <= i + a - reach < side:
                            sums[i] = sums[i] + moved[i + a - reach] * tap
            for i in range(side):
                conv[i * side : (i + 1) * side, cols] = sums[i]
        start = pl.multiple_of(tile * side * side, side * side)
        out[pl.ds(start, side * side), :] = layer_norm(conv[...], gain[...]).astype(BF16)
        return carry

    lax.fori_loop(0, tiles, one_tile, 0)


def early_kernel(where, maps, up, bias, left, right, left_swap, right_swap, hid):
    core = where[0]
    n = up.shape[0]
    tiles = hid.shape[1]
    maps_a, maps_b = lanes(maps, core, n), lanes(maps, 1 - core, n)
    pre = lax.dot_general(maps[...], up[...], NT, preferred_element_type=F32)
    hid[0] = gelu_mean(pre + bias[...].astype(F32), tiles)
    for slot, (a, b) in enumerate(((left, left_swap), (right, right_swap))):
        pre = lax.dot_general(maps_a, a[0:n, :], NT, preferred_element_type=F32)
        pre += lax.dot_general(maps_b, b[0:n, :], NT, preferred_element_type=F32)
        hid[slot + 1] = gelu_mean(pre + a[4 * n : 4 * n + 1, :].astype(F32), tiles)


def late_kernel(
    where, maps, hid, feat_mean, layer_scale, b_down, lnf_gain, code, w_down, w_head, w_in,
    left, right, left_swap, right_swap, low, high, low_swap, high_swap, out,
):
    core = where[0]
    n = w_down.shape[0]
    tiles = hid.shape[1]
    pre = lax.dot_general(lanes(maps, core, n), low[0:n, :], NT, preferred_element_type=F32)
    pre += lax.dot_general(
        lanes(maps, 1 - core, n), low_swap[0:n, :], NT, preferred_element_type=F32
    )
    hid_far = gelu_mean(pre + high[2 * n : 2 * n + 1, :].astype(F32), tiles)

    def exact(block):
        upper = block.astype(BF16)
        lower = (block - upper.astype(F32)).astype(BF16)
        return jnp.concatenate([upper.astype(F32), lower.astype(F32)], 0).astype(BF16)

    sides = ((left, left_swap), (right, right_swap))
    own = dot(exact(hid[0]), w_down[...])
    part = exact(hid_far)
    br_a, br_b = dot(part, low[n : 2 * n, :]), dot(part, low_swap[n : 2 * n, :])
    for slot, (a, b) in enumerate(sides):
        part = exact(hid[slot + 1])
        br_a += dot(part, a[n : 2 * n, :])
        br_b += dot(part, b[n : 2 * n, :])
    branch = own + natural(core, br_a, br_b)
    branch = branch[0:tiles] + branch[tiles : 2 * tiles]
    pooled = feat_mean[...] + layer_scale[...] * (branch + b_down[...])
    feature = layer_norm(pooled, lnf_gain[...])
    first, second = feature[:, 0:n], feature[:, n : 2 * n]
    feature_a = jnp.where(core == 0, first, second).astype(BF16)
    feature_b = jnp.where(core == 0, second, first).astype(BF16)
    emb = dot(feature.astype(BF16), w_head[...]).astype(BF16)
    own = dot(emb, w_in[...])
    emb = (dot(feature_a, high[0:n, :]) + dot(feature_b, high_swap[0:n, :])).astype(BF16)
    x_a, x_b = dot(emb, high[n : 2 * n, :]), dot(emb, high_swap[n : 2 * n, :])
    for a, b in sides:
        emb = dot(feature_a, a[2 * n : 3 * n, :]) + dot(feature_b, b[2 * n : 3 * n, :])
        emb = emb.astype(BF16)
        x_a += dot(emb, a[3 * n : 4 * n, :])
        x_b += dot(emb, b[3 * n : 4 * n, :])
    x_fresh = own + natural(core, x_a, x_b)
    out[...] = jnp.concatenate([x_fresh, code[...]], axis=1).astype(BF16)


def select_kernel(bucket, rows, code, out):
    places = lax.broadcasted_iota(jnp.int32, (out.shape[0], bucket.shape[1]), 0)
    select = jnp.where(places == bucket[...], 1.0, 0.0).astype(BF16)
    width = rows.shape[1]
    out[:, 0:width] = dot(select, rows[...]).astype(BF16)
    out[:, width:] = dot(select, code[...]).astype(BF16)


def column_as_row(ref, column):
    lane = lax.broadcasted_iota(jnp.int32, (8, 128), 1)
    unit_row = jnp.where(lane == column, 1.0, 0.0).astype(BF16)
    tail = ref[:, ref.shape[1] - 128 :]
    return lax.dot_general(unit_row, tail, NT, preferred_element_type=F32)[0:1, :]


def place_rows(got, q_rows):
    code = column_as_row(got, 0)
    places = lax.broadcasted_iota(jnp.int32, (q_rows, got.shape[0]), 0).astype(F32) + 1.0
    placer = jnp.where(places == code, 1.0, 0.0).astype(BF16)
    return dot(placer, got[:, 0 : got.shape[1] - 128])


def earlier_kernel(
    where, got, w_in, left, right, left_swap, right_swap, high, high_swap, out, rows
):
    n = w_in.shape[0]
    rows[...] = place_rows(got, out.shape[0]).astype(BF16)
    own = dot(lanes(rows, where[1], n), w_in[...])
    columns = lanes(rows, where[4], n)
    x_a, x_b = dot(columns, high[n : 2 * n, :]), dot(columns, high_swap[n : 2 * n, :])
    for slot, (a, b) in enumerate(((left, left_swap), (right, right_swap))):
        columns = lanes(rows, where[slot + 2], n)
        x_a += dot(columns, a[3 * n : 4 * n, :])
        x_b += dot(columns, b[3 * n : 4 * n, :])
    out[...] = own + natural(where[0], x_a, x_b)


def scatter_kernel(where, rows, out):
    count = rows.shape[0]
    dest_row = column_as_row(rows, 1)
    dest = rows[:, rows.shape[1] - 128 :].astype(F32)[:, 1:2]
    index_a = lax.broadcasted_iota(jnp.int32, (count, count), 0)
    index_b = lax.broadcasted_iota(jnp.int32, (count, count), 1)
    before = jnp.where((dest == dest_row) & (index_a < index_b), 1.0, 0.0)
    rank = jnp.sum(before, axis=0, keepdims=True).astype(jnp.int32)
    shard = dest_row.astype(jnp.int32)
    plane = N_Y * N_CORE
    room = out.shape[0] // plane
    inside = shard - where[5] * plane
    bucket = jnp.where((inside >= 0) & (inside < plane), inside * room + rank, -1)
    places = lax.broadcasted_iota(jnp.int32, (out.shape[0], count), 0)
    select = jnp.where(places == bucket, 1.0, 0.0).astype(BF16)
    out[...] = dot(select, rows[...]).astype(BF16)


def arrive_kernel(got, earlier, out):
    out[...] = (place_rows(got, out.shape[0]) + earlier[...]).astype(BF16)


def local_call(body, outs, scratch, flops, size, *operands):
    vmem = pl.BlockSpec(memory_space=pltpu.VMEM)
    return pl.pallas_call(
        body,
        in_specs=[pl.BlockSpec(memory_space=pltpu.SMEM)] + [vmem] * (len(operands) - 1),
        out_specs=jax.tree.map(lambda _: vmem, outs),
        out_shape=outs,
        scratch_shapes=scratch,
        compiler_params=pltpu.CompilerParams(vmem_limit_bytes=24 * 2**20),
        cost_estimate=pl.CostEstimate(flops=flops, bytes_accessed=size, transcendentals=0),
    )(*operands)


def head_lanes(shape, head):
    lane = lax.broadcasted_iota(jnp.int32, shape, len(shape) - 1)
    return (lane >= head * HS) & (lane < (head + 1) * HS)


def dilated(shape, off_lane):
    return lax.rem(lax.broadcasted_iota(jnp.int32, shape, 0), RB) == off_lane


def project_kernel(x, ln_gain, w_q, w_k, w_v, q_gain, k_gain, off_lane, q, k, v, far_q, far_kv):
    rows, width = q.shape
    normed = layer_norm(x[...].astype(F32), ln_gain[...]).astype(BF16)
    chosen = dilated((rows, width), off_lane[...])

    def unit(raw, gain):
        raw = raw.astype(BF16).astype(F32)
        square = raw * raw
        mean = jnp.zeros_like(raw)
        for head in range(width // HS):
            inside = head_lanes(raw.shape, head)
            total = jnp.sum(jnp.where(inside, square, 0.0), axis=1, keepdims=True) * (1.0 / HS)
            mean = jnp.where(inside, total, mean)
        return (raw * lax.rsqrt(mean + 1e-06) * gain).astype(BF16)

    def far_rows(part):
        kept = jnp.where(chosen, part.astype(F32), 0.0)
        return jnp.sum(kept.reshape(rows // RB, RB, width), axis=1)

    q_rows = unit(dot(normed, w_q[...]), q_gain[...])
    k_rows = unit(dot(normed, w_k[...]), k_gain[...])
    v_rows = dot(normed, w_v[...]).astype(BF16)
    q[...], k[...], v[...] = q_rows, k_rows, v_rows
    far_q[...] = far_rows(q_rows)
    far_kv[...] = jnp.concatenate([far_rows(k_rows), far_rows(v_rows)], axis=1).astype(BF16)


def by_head(block):
    heads = block.shape[1] // HS
    wide = block.astype(F32)
    kept = [jnp.where(head_lanes(wide.shape, head), wide, 0.0) for head in range(heads)]
    return jnp.concatenate(kept, axis=0)


def back(block, rows, width):
    out = jnp.zeros((rows, width), F32)
    for head in range(width // HS):
        part = jnp.broadcast_to(block[head * rows : (head + 1) * rows], (rows, width))
        out = jnp.where(head_lanes(out.shape, head), part, out)
    return out


def weigh(queries, keys, values):
    scores = lax.dot_general(queries, keys, NT, preferred_element_type=F32)
    weights = jnp.exp(scores * (1.0 / math.sqrt(HS)))
    return jnp.sum(weights, axis=1, keepdims=True), dot(weights.astype(BF16), values)


def far_part(far_q, kv):
    rows, width = far_q.shape
    spread_q = by_head(far_q[...])
    spread_q = jnp.concatenate([spread_q, jnp.zeros_like(spread_q)], axis=1).astype(BF16)
    den, num = weigh(spread_q, kv[...], kv[...])
    return back(den, rows, width), back(num[:, width:], rows, width)


def near_kernel(where, q, k, v, far_q, kv, x, den, num, far_den, far_num, residual):
    wanted = lax.broadcasted_iota(jnp.int32, (residual.shape[0], x.shape[1]), 0)
    column = lax.broadcasted_iota(jnp.int32, (residual.shape[0], x.shape[1]), 1)
    pick = jnp.where(column == wanted + where[1] * residual.shape[0], 1.0, 0.0).astype(BF16)
    residual[...] = lax.dot_general(pick, x[...], NT, preferred_element_type=F32)
    rows, width = q.shape
    local_den, local_num = weigh(by_head(q[...]).astype(BF16), k[...], v[...])
    den[...] = back(local_den, rows, width)
    num[...] = back(local_num, rows, width)
    far_den[...], far_num[...] = far_part(far_q, kv)


def far_kernel(far_q, kv, off_lane, den, num, far_den, far_num, w_out, out):
    rows, width = num.shape
    chosen = dilated((rows, width), off_lane[...])
    more_den, more_num = far_part(far_q, kv)

    def placed(block):
        wide = jnp.broadcast_to(block[:, None, :], (rows // RB, RB, width))
        return jnp.where(chosen, wide.reshape(rows, width), 0.0)

    attended = (num[...] + placed(far_num[...] + more_num)) / (
        den[...] + placed(far_den[...] + more_den)
    )
    attended = attended.astype(BF16)
    out[...] = lax.dot_general(w_out[...], attended, NT, preferred_element_type=F32).astype(BF16)


def sum_kernel(residual, parts, out):
    total = residual[...]
    for part in range(parts.shape[0]):
        total += parts[part].astype(F32)
    out[...] = total.astype(BF16)


def vmem_call(body, outs, flops, size, exps, *operands, scratch=()):
    vmem = pl.BlockSpec(memory_space=pltpu.VMEM)
    return pl.pallas_call(
        body,
        in_specs=[vmem] * len(operands),
        out_specs=jax.tree.map(lambda _: vmem, outs),
        out_shape=outs,
        scratch_shapes=list(scratch),
        compiler_params=pltpu.CompilerParams(vmem_limit_bytes=16 * 2**20),
        cost_estimate=pl.CostEstimate(flops=flops, bytes_accessed=size, transcendentals=exps),
    )(*operands)


def shards(
    feats,
    dw_weight,
    dw_bias,
    ln1_gain,
    w_up,
    b_up,
    w_down,
    b_down,
    layer_scale,
    lnf_gain,
    w_head,
    prior,
    counts,
    positions,
    w_in,
    ln_gain,
    w_qkv,
    qn_gain,
    kn_gain,
    offsets,
    w_out,
):
    n_section = N_SECTION
    n_seq = N_Z * N_Y * N_CORE
    section_idx = lax.axis_index("section")
    core = lax.axis_index("core")
    tiles = feats.shape[0]
    channels = feats.shape[3]
    half = channels // N_CORE
    share = w_up.shape[0]

    row = lambda vec: vec[None, :]
    others = [(section_idx + step) % N_SECTION for step in (3, 1, 2)]
    where = jnp.stack([core, section_idx] + others + [lax.axis_index("z")]).astype(jnp.int32)

    block = pack(core, w_up, w_down, w_head, w_in, b_up)
    block, prior = lax.optimization_barrier((block, prior))
    left = rotate(block, "section", N_SECTION, 1)
    right = rotate(block, "section", N_SECTION, -1)

    q_rows = ROWS // n_section
    capacity = -(-(tiles + prior.shape[0]) // n_seq)
    slot_ids = jnp.arange(prior.shape[0])
    live_mask = slot_ids < counts[0]
    dest_shard = positions // ROWS
    row_code = (positions % ROWS - section_idx * q_rows + 1).astype(BF16)
    dest_prior = dest_shard[tiles:]
    earlier = (
        (dest_prior[None, :] == dest_prior[:, None])
        & (slot_ids[None, :] < slot_ids[:, None])
        & live_mask[None, :]
    )
    within = jnp.sum(earlier.astype(jnp.int32), axis=1)
    bucket = jnp.where(live_mask, dest_prior * capacity + within, -1)
    code_prior = jnp.broadcast_to(row_code[tiles:, None], (prior.shape[0], 128))
    send = vmem_call(
        select_kernel,
        jax.ShapeDtypeStruct((n_seq * capacity, prior.shape[1] + 128), BF16),
        200_000_000,
        2_000_000,
        0,
        row(bucket), prior, code_prior,
    )

    got_prior = lax.all_to_all(
        send.reshape(n_seq, capacity, send.shape[1]), SEQ_AXES, 0, 0, tiled=True
    ).reshape(send.shape)
    left, right, low_in, high_in, feats = lax.optimization_barrier(
        (left, right, left[: 2 * share], right[2 * share :], feats)
    )
    low = rotate(low_in, "section", N_SECTION, 1)
    high = rotate(high_in, "section", N_SECTION, -1)
    left_swap = rotate(left, "core", N_CORE, 1)
    right_swap = rotate(right, "core", N_CORE, 1)
    pixels = feats.shape[1] * feats.shape[2]
    normed_maps, feat_mean = vmem_call(
        conv_kernel,
        (
            jax.ShapeDtypeStruct((tiles * pixels, channels), BF16),
            jax.ShapeDtypeStruct((tiles, channels), F32),
        ),
        30_000_000_000,
        8_000_000,
        0,
        feats, dw_weight.reshape(-1, channels), row(dw_bias), row(ln1_gain),
        scratch=[pltpu.VMEM((pixels, channels), F32)],
    )
    low, high, normed_maps, feat_mean = lax.optimization_barrier(
        (low, high, normed_maps, feat_mean)
    )
    low_swap = rotate(low, "core", N_CORE, 1)
    high_swap = rotate(high, "core", N_CORE, 1)
    code_fresh = jnp.where(
        jnp.arange(128)[None, :] == 0,
        row_code[:tiles, None].astype(F32),
        dest_shard[:tiles, None].astype(F32),
    )
    hid = local_call(
        early_kernel,
        jax.ShapeDtypeStruct((3, tiles, share), F32),
        [],
        2_000_000_000,
        6_000_000,
        where, normed_maps, w_up, row(b_up), left, right, left_swap, right_swap,
    )
    fresh = local_call(
        late_kernel,
        jax.ShapeDtypeStruct((tiles, channels + 128), BF16),
        [],
        2_000_000_000,
        8_000_000,
        where, normed_maps, hid, feat_mean, row(layer_scale), row(b_down), row(lnf_gain),
        code_fresh, w_down, w_head, w_in, left, right, left_swap, right_swap, low, high, low_swap,
        high_swap,
    )
    got_prior, fresh = lax.optimization_barrier((got_prior, fresh))
    x_earlier = local_call(
        earlier_kernel,
        jax.ShapeDtypeStruct((q_rows, channels), F32),
        [pltpu.VMEM((q_rows, prior.shape[1]), BF16)],
        500_000_000,
        4_000_000,
        where, got_prior, w_in, left, right, left_swap, right_swap, high, high_swap,
    )

    fresh_z = spread(fresh, "z", N_Z).reshape(N_Z * tiles, channels + 128)
    plane = N_Y * N_CORE
    room = N_Z * capacity
    to_plane = local_call(
        scatter_kernel,
        jax.ShapeDtypeStruct((plane * room, channels + 128), BF16),
        [],
        60_000_000,
        1_000_000,
        where, fresh_z,
    )
    got = lax.all_to_all(
        to_plane.reshape(plane, room, channels + 128), ("y", "core"), 0, 0, tiled=True
    ).reshape(plane * room, channels + 128)
    x_local = vmem_call(
        arrive_kernel,
        jax.ShapeDtypeStruct((q_rows, channels), BF16),
        30_000_000,
        1_000_000,
        0,
        got, x_earlier,
    )
    x_rows = spread(x_local, "section", n_section).reshape(ROWS, channels)

    heads_here = w_qkv.shape[1] // (3 * HS)
    width = heads_here * HS
    stride_rows = ROWS // RB
    my_offsets = lax.dynamic_slice_in_dim(offsets, section_idx * heads_here, heads_here)
    off_lane = row(jnp.repeat(my_offsets, HS))
    w_q, w_k, w_v = (w_qkv[:, part * width : (part + 1) * width] for part in range(3))
    small = lambda rows, kind: jax.ShapeDtypeStruct((rows, width), kind)
    q, k, v, far_q, far_kv = vmem_call(
        project_kernel,
        (small(ROWS, BF16),) * 3
        + (small(stride_rows, F32), jax.ShapeDtypeStruct((stride_rows, 2 * width), BF16)),
        300_000_000,
        2_000_000,
        0,
        x_rows, row(ln_gain), w_q, w_k, w_v, row(jnp.tile(qn_gain, heads_here)),
        row(jnp.tile(kn_gain, heads_here)), off_lane,
    )
    z_kv = spread(far_kv, "z", N_Z).reshape(N_Z * stride_rows, 2 * width)
    half_kv = lax.all_gather(z_kv, "y", axis=0, tiled=True)
    other_kv = rotate(half_kv, "core", N_CORE, 1)
    width_part = channels // n_section
    den, num, far_den, far_num, residual = local_call(
        near_kernel,
        (small(ROWS, F32),) * 2
        + (small(stride_rows, F32),) * 2
        + (jax.ShapeDtypeStruct((width_part, ROWS), F32),),
        [],
        2_000_000_000,
        2_000_000,
        where, q, k, v, far_q, half_kv, x_rows,
    )
    partial_out = vmem_call(
        far_kernel,
        jax.ShapeDtypeStruct((channels, ROWS), BF16),
        150_000_000,
        2_000_000,
        50_000,
        far_q, other_kv, off_lane, den, num, far_den, far_num,
        jnp.transpose(w_out),
    )
    parts = lax.all_to_all(
        partial_out.reshape(n_section, width_part, ROWS), "section", 0, 0, tiled=True
    )
    total = vmem_call(
        sum_kernel,
        jax.ShapeDtypeStruct((width_part, ROWS), BF16),
        1_000_000,
        1_000_000,
        0,
        residual, parts,
    )
    return jnp.transpose(total)


def solution(mesh):
    fine = Mesh(
        mesh.devices.reshape(N_SECTION, N_Z, N_Y, N_CORE), ("section",) + SEQ_AXES
    )
    both = ("section",) + SEQ_AXES
    placed = (
        P(both, None, None, None),
        P(),
        P(),
        P(),
        P("section", None),
        P("section"),
        P("section", None),
        P(),
        P(),
        P(),
        P(None, "section"),
        P(both, None),
        P(both),
        P(both),
        P("section", None),
        P(),
        P(None, "section"),
        P(),
        P(),
        P(),
        P("section", None),
    )
    return jax.shard_map(
        shards, mesh=fine, in_specs=placed, out_specs=P(SEQ_AXES, "section"), check_vma=False
    )
```

```python
import math

import jax
import jax.numpy as jnp
from jax import lax
from jax.experimental import pallas as pl
from jax.experimental.pallas import tpu as pltpu
from jax.sharding import Mesh
from jax.sharding import PartitionSpec as P

HS = 64
RB = 16
ROWS = 256
N_SECTION = 4
N_Z, N_Y, N_CORE = 16, 4, 2
SEQ_AXES = ("z", "y", "core")
F32 = jnp.float32
BF16 = jnp.bfloat16


def layer_norm(values, gain_vec):
    row_mean = jnp.mean(values, axis=-1, keepdims=True)
    centered = values - row_mean
    variance = jnp.mean(centered * centered, axis=-1, keepdims=True)
    return centered * lax.rsqrt(variance + 1e-06) * gain_vec


def rotate(block, axis, size, step):
    return lax.ppermute(block, axis, [(i, (i + step) % size) for i in range(size)])


def spread(block, axis, size):
    return lax.all_to_all(
        jnp.broadcast_to(block[None], (size,) + block.shape), axis, 0, 0, tiled=True
    )


NT = (((1,), (1,)), ((), ()))


def dot(a, b):
    return jnp.dot(a, b, preferred_element_type=F32)


def gelu_mean(pre, tiles):
    hidden = (0.5 * pre * (1.0 + lax.erf(pre * (1.0 / math.sqrt(2.0))))).astype(BF16).astype(F32)
    return jnp.mean(hidden.reshape(tiles, hidden.shape[0] // tiles, hidden.shape[1]), axis=1)


def lanes(ref, index, width):
    return ref[:, pl.ds(pl.multiple_of(index * width, 128), width)]


def pack_kernel(core_ref, w_up, w_down, w_head, w_in, bias, out, sems):
    n = w_up.shape[0]
    start = pl.multiple_of(core_ref[0] * n, n)
    parts = (
        w_up.at[:, pl.ds(start, n)],
        w_down.at[:, pl.ds(start, n)],
        w_head.at[pl.ds(start, n), :],
        w_in.at[:, pl.ds(start, n)],
    )
    copies = [
        pltpu.make_async_copy(part, out.at[pl.ds(k * n, n), :], sems.at[k])
        for k, part in enumerate(parts)
    ]
    for copy in copies:
        copy.start()
    out[4 * n :, :] = jnp.broadcast_to(bias[...][None, :], (16, n))
    for copy in copies:
        copy.wait()


def pack(core, w_up, w_down, w_head, w_in, bias):
    n = w_up.shape[0]
    vmem = pl.BlockSpec(memory_space=pltpu.VMEM)
    return pl.pallas_call(
        pack_kernel,
        in_specs=[pl.BlockSpec(memory_space=pltpu.SMEM)]
        + [pl.BlockSpec(memory_space=pl.ANY)] * 4
        + [vmem],
        out_specs=vmem,
        out_shape=jax.ShapeDtypeStruct((4 * n + 16, n), BF16),
        scratch_shapes=[pltpu.SemaphoreType.DMA((4,))],
        cost_estimate=pl.CostEstimate(flops=0, bytes_accessed=4 * n * n * 4, transcendentals=0),
    )(core.astype(jnp.int32)[None], w_up, w_down, w_head, w_in, bias)


def natural(core, a, b):
    return jnp.where(core == 0, jnp.concatenate([a, b], 1), jnp.concatenate([b, a], 1))


def conv_kernel(feats, dw_weight, dw_bias, gain, out, mean, conv):
    tiles, side, _, channels = feats.shape
    taps = math.isqrt(dw_weight.shape[0])
    reach = (taps - 1) // 2
    column = lax.broadcasted_iota(jnp.int32, (side, side, 128), 1)
    tile_row = lax.broadcasted_iota(jnp.int32, (tiles, 128), 0)
    mean[...] = jnp.zeros_like(mean)

    def one_tile(tile, carry):
        for chunk in range(channels // 128):
            cols = pl.ds(chunk * 128, 128)
            source = feats[tile, :, :, cols].astype(F32)
            total = jnp.sum(jnp.sum(source, axis=0), axis=0, keepdims=True)
            total = jnp.broadcast_to(total * (1.0 / (side * side)), (tiles, 128))
            mean[:, cols] = jnp.where(tile_row == tile, total, mean[:, cols])
            bias = jnp.broadcast_to(dw_bias[0:1, cols], (side, 128))
            sums = [bias] * side
            for b in range(taps):
                move = b - reach
                moved = source
                if move:
                    moved = pltpu.roll(source, (-move) % side, 1)
                    inside = (column + move >= 0) & (column + move < side)
                    moved = jnp.where(inside, moved, 0.0)
                for a in range(taps):
                    tap = dw_weight[a * taps + b : a * taps + b + 1, cols]
                    tap = jnp.broadcast_to(tap, (side, 128))
                    for i in range(side):
                        if 0 <= i + a - reach < side:
                            sums[i] = sums[i] + moved[i + a - reach] * tap
            for i in range(side):
                conv[i * side : (i + 1) * side, cols] = sums[i]
        start = pl.multiple_of(tile * side * side, side * side)
        out[pl.ds(start, side * side), :] = layer_norm(conv[...], gain[...]).astype(BF16)
        return carry

    lax.fori_loop(0, tiles, one_tile, 0)


def early_kernel(where, maps, up, block, left, right, left_swap, right_swap, hid):
    core = where[0]
    n = up.shape[0]
    tiles = hid.shape[1]
    maps_a, maps_b = lanes(maps, core, n), lanes(maps, 1 - core, n)
    pre = lax.dot_general(maps[...], up[...], NT, preferred_element_type=F32)
    hid[0] = gelu_mean(pre + block[4 * n : 4 * n + 1, :].astype(F32), tiles)
    for slot, (a, b) in enumerate(((left, left_swap), (right, right_swap))):
        pre = lax.dot_general(maps_a, a[0:n, :], NT, preferred_element_type=F32)
        pre += lax.dot_general(maps_b, b[0:n, :], NT, preferred_element_type=F32)
        hid[slot + 1] = gelu_mean(pre + a[4 * n : 4 * n + 1, :].astype(F32), tiles)


def late_kernel(
    where, maps, hid, feat_mean, layer_scale, b_down, lnf_gain, code, w_down, w_head, w_in,
    left, right, left_swap, right_swap, low, high, low_swap, high_swap, out,
):
    core = where[0]
    n = w_down.shape[0]
    tiles = hid.shape[1]
    pre = lax.dot_general(lanes(maps, core, n), low[0:n, :], NT, preferred_element_type=F32)
    pre += lax.dot_general(
        lanes(maps, 1 - core, n), low_swap[0:n, :], NT, preferred_element_type=F32
    )
    hid_far = gelu_mean(pre + high[2 * n : 2 * n + 1, :].astype(F32), tiles)

    def exact(block):
        upper = block.astype(BF16)
        lower = (block - upper.astype(F32)).astype(BF16)
        return jnp.concatenate([upper.astype(F32), lower.astype(F32)], 0).astype(BF16)

    sides = ((left, left_swap), (right, right_swap))
    own = dot(exact(hid[0]), w_down[...])
    part = exact(hid_far)
    br_a, br_b = dot(part, low[n : 2 * n, :]), dot(part, low_swap[n : 2 * n, :])
    for slot, (a, b) in enumerate(sides):
        part = exact(hid[slot + 1])
        br_a += dot(part, a[n : 2 * n, :])
        br_b += dot(part, b[n : 2 * n, :])
    branch = own + natural(core, br_a, br_b)
    branch = branch[0:tiles] + branch[tiles : 2 * tiles]
    pooled = feat_mean[...] + layer_scale[...] * (branch + b_down[...])
    feature = layer_norm(pooled, lnf_gain[...])
    first, second = feature[:, 0:n], feature[:, n : 2 * n]
    feature_a = jnp.where(core == 0, first, second).astype(BF16)
    feature_b = jnp.where(core == 0, second, first).astype(BF16)
    emb = dot(feature.astype(BF16), w_head[...]).astype(BF16)
    own = dot(emb, w_in[...])
    emb = (dot(feature_a, high[0:n, :]) + dot(feature_b, high_swap[0:n, :])).astype(BF16)
    x_a, x_b = dot(emb, high[n : 2 * n, :]), dot(emb, high_swap[n : 2 * n, :])
    for a, b in sides:
        emb = dot(feature_a, a[2 * n : 3 * n, :]) + dot(feature_b, b[2 * n : 3 * n, :])
        emb = emb.astype(BF16)
        x_a += dot(emb, a[3 * n : 4 * n, :])
        x_b += dot(emb, b[3 * n : 4 * n, :])
    x_fresh = own + natural(core, x_a, x_b)
    out[...] = jnp.concatenate([x_fresh, code[...]], axis=1).astype(BF16)


def select_kernel(bucket, rows, code, out):
    places = lax.broadcasted_iota(jnp.int32, (out.shape[0], bucket.shape[1]), 0)
    select = jnp.where(places == bucket[...], 1.0, 0.0).astype(BF16)
    width = rows.shape[1]
    out[:, 0:width] = dot(select, rows[...]).astype(BF16)
    out[:, width:] = dot(select, code[...]).astype(BF16)


def column_as_row(ref, column):
    lane = lax.broadcasted_iota(jnp.int32, (8, 128), 1)
    unit_row = jnp.where(lane == column, 1.0, 0.0).astype(BF16)
    tail = ref[:, ref.shape[1] - 128 :]
    return lax.dot_general(unit_row, tail, NT, preferred_element_type=F32)[0:1, :]


def place_rows(got, q_rows):
    code = column_as_row(got, 0)
    places = lax.broadcasted_iota(jnp.int32, (q_rows, got.shape[0]), 0).astype(F32) + 1.0
    placer = jnp.where(places == code, 1.0, 0.0).astype(BF16)
    return dot(placer, got[:, 0 : got.shape[1] - 128])


def earlier_kernel(
    where, got, w_in, left, right, left_swap, right_swap, high, high_swap, out, rows
):
    n = w_in.shape[0]
    rows[...] = place_rows(got, out.shape[0]).astype(BF16)
    own = dot(lanes(rows, where[1], n), w_in[...])
    columns = lanes(rows, where[4], n)
    x_a, x_b = dot(columns, high[n : 2 * n, :]), dot(columns, high_swap[n : 2 * n, :])
    for slot, (a, b) in enumerate(((left, left_swap), (right, right_swap))):
        columns = lanes(rows, where[slot + 2], n)
        x_a += dot(columns, a[3 * n : 4 * n, :])
        x_b += dot(columns, b[3 * n : 4 * n, :])
    out[...] = own + natural(where[0], x_a, x_b)


def scatter_kernel(where, rows, out):
    count = rows.shape[0]
    dest_row = column_as_row(rows, 1)
    dest = rows[:, rows.shape[1] - 128 :].astype(F32)[:, 1:2]
    index_a = lax.broadcasted_iota(jnp.int32, (count, count), 0)
    index_b = lax.broadcasted_iota(jnp.int32, (count, count), 1)
    before = jnp.where((dest == dest_row) & (index_a < index_b), 1.0, 0.0)
    rank = jnp.sum(before, axis=0, keepdims=True).astype(jnp.int32)
    shard = dest_row.astype(jnp.int32)
    plane = N_Y * N_CORE
    room = out.shape[0] // plane
    inside = shard - where[5] * plane
    bucket = jnp.where((inside >= 0) & (inside < plane), inside * room + rank, -1)
    places = lax.broadcasted_iota(jnp.int32, (out.shape[0], count), 0)
    select = jnp.where(places == bucket, 1.0, 0.0).astype(BF16)
    out[...] = dot(select, rows[...]).astype(BF16)


def arrive_kernel(got, earlier, out):
    out[...] = (place_rows(got, out.shape[0]) + earlier[...]).astype(BF16)


def local_call(body, outs, scratch, flops, size, *operands):
    vmem = pl.BlockSpec(memory_space=pltpu.VMEM)
    return pl.pallas_call(
        body,
        in_specs=[pl.BlockSpec(memory_space=pltpu.SMEM)] + [vmem] * (len(operands) - 1),
        out_specs=jax.tree.map(lambda _: vmem, outs),
        out_shape=outs,
        scratch_shapes=scratch,
        compiler_params=pltpu.CompilerParams(vmem_limit_bytes=16 * 2**20),
        cost_estimate=pl.CostEstimate(flops=flops, bytes_accessed=size, transcendentals=0),
    )(*operands)


def head_lanes(shape, head):
    lane = lax.broadcasted_iota(jnp.int32, shape, len(shape) - 1)
    return (lane >= head * HS) & (lane < (head + 1) * HS)


def dilated(shape, off_lane):
    return lax.rem(lax.broadcasted_iota(jnp.int32, shape, 0), RB) == off_lane


def project_kernel(x, ln_gain, w_q, w_k, w_v, q_gain, k_gain, off_lane, q, k, v, far_q, far_kv):
    rows, width = q.shape
    normed = layer_norm(x[...].astype(F32), ln_gain[...]).astype(BF16)
    chosen = dilated((rows, width), off_lane[...])

    def unit(raw, gain):
        raw = raw.astype(BF16).astype(F32)
        square = raw * raw
        mean = jnp.zeros_like(raw)
        for head in range(width // HS):
            inside = head_lanes(raw.shape, head)
            total = jnp.sum(jnp.where(inside, square, 0.0), axis=1, keepdims=True) * (1.0 / HS)
            mean = jnp.where(inside, total, mean)
        return (raw * lax.rsqrt(mean + 1e-06) * gain).astype(BF16)

    def far_rows(part):
        kept = jnp.where(chosen, part.astype(F32), 0.0)
        return jnp.sum(kept.reshape(rows // RB, RB, width), axis=1)

    q_rows = unit(dot(normed, w_q[...]), q_gain[...])
    k_rows = unit(dot(normed, w_k[...]), k_gain[...])
    v_rows = dot(normed, w_v[...]).astype(BF16)
    q[...], k[...], v[...] = q_rows, k_rows, v_rows
    far_q[...] = far_rows(q_rows)
    far_kv[...] = jnp.concatenate([far_rows(k_rows), far_rows(v_rows)], axis=1).astype(BF16)


def by_head(block):
    heads = block.shape[1] // HS
    wide = block.astype(F32)
    kept = [jnp.where(head_lanes(wide.shape, head), wide, 0.0) for head in range(heads)]
    return jnp.concatenate(kept, axis=0)


def back(block, rows, width):
    out = jnp.zeros((rows, width), F32)
    for head in range(width // HS):
        part = jnp.broadcast_to(block[head * rows : (head + 1) * rows], (rows, width))
        out = jnp.where(head_lanes(out.shape, head), part, out)
    return out


def weigh(queries, keys, values):
    scores = lax.dot_general(queries, keys, NT, preferred_element_type=F32)
    weights = jnp.exp(scores * (1.0 / math.sqrt(HS)))
    return jnp.sum(weights, axis=1, keepdims=True), dot(weights.astype(BF16), values)


def far_part(far_q, kv):
    rows, width = far_q.shape
    spread_q = by_head(far_q[...])
    spread_q = jnp.concatenate([spread_q, jnp.zeros_like(spread_q)], axis=1).astype(BF16)
    den, num = weigh(spread_q, kv[...], kv[...])
    return back(den, rows, width), back(num[:, width:], rows, width)


def near_kernel(where, q, k, v, far_q, kv, x, den, num, far_den, far_num, residual):
    wanted = lax.broadcasted_iota(jnp.int32, (residual.shape[0], x.shape[1]), 0)
    column = lax.broadcasted_iota(jnp.int32, (residual.shape[0], x.shape[1]), 1)
    pick = jnp.where(column == wanted + where[1] * residual.shape[0], 1.0, 0.0).astype(BF16)
    residual[...] = lax.dot_general(pick, x[...], NT, preferred_element_type=F32)
    rows, width = q.shape
    local_den, local_num = weigh(by_head(q[...]).astype(BF16), k[...], v[...])
    den[...] = back(local_den, rows, width)
    num[...] = back(local_num, rows, width)
    far_den[...], far_num[...] = far_part(far_q, kv)


def far_kernel(far_q, kv, off_lane, den, num, far_den, far_num, w_out, out):
    rows, width = num.shape
    chosen = dilated((rows, width), off_lane[...])
    more_den, more_num = far_part(far_q, kv)

    def placed(block):
        wide = jnp.broadcast_to(block[:, None, :], (rows // RB, RB, width))
        return jnp.where(chosen, wide.reshape(rows, width), 0.0)

    attended = (num[...] + placed(far_num[...] + more_num)) / (
        den[...] + placed(far_den[...] + more_den)
    )
    attended = attended.astype(BF16)
    out[...] = lax.dot_general(w_out[...], attended, NT, preferred_element_type=F32).astype(BF16)


def sum_kernel(residual, parts, out):
    total = residual[...]
    for part in range(parts.shape[0]):
        total += parts[part].astype(F32)
    out[...] = total.astype(BF16)


def vmem_call(body, outs, flops, size, exps, *operands, scratch=()):
    vmem = pl.BlockSpec(memory_space=pltpu.VMEM)
    return pl.pallas_call(
        body,
        in_specs=[vmem] * len(operands),
        out_specs=jax.tree.map(lambda _: vmem, outs),
        out_shape=outs,
        scratch_shapes=list(scratch),
        compiler_params=pltpu.CompilerParams(vmem_limit_bytes=16 * 2**20),
        cost_estimate=pl.CostEstimate(flops=flops, bytes_accessed=size, transcendentals=exps),
    )(*operands)


def shards(
    feats,
    dw_weight,
    dw_bias,
    ln1_gain,
    w_up,
    b_up,
    w_down,
    b_down,
    layer_scale,
    lnf_gain,
    w_head,
    prior,
    counts,
    positions,
    w_in,
    ln_gain,
    w_qkv,
    qn_gain,
    kn_gain,
    offsets,
    w_out,
):
    n_section = N_SECTION
    n_seq = N_Z * N_Y * N_CORE
    section_idx = lax.axis_index("section")
    core = lax.axis_index("core")
    tiles = feats.shape[0]
    channels = feats.shape[3]
    half = channels // N_CORE
    share = w_up.shape[0]

    row = lambda vec: vec[None, :]
    others = [(section_idx + step) % N_SECTION for step in (3, 1, 2)]
    where = jnp.stack([core, section_idx] + others + [lax.axis_index("z")]).astype(jnp.int32)

    block = pack(core, w_up, w_down, w_head, w_in, b_up)
    block, prior = lax.optimization_barrier((block, prior))
    left = rotate(block, "section", N_SECTION, 1)
    right = rotate(block, "section", N_SECTION, -1)

    q_rows = ROWS // n_section
    capacity = -(-(tiles + prior.shape[0]) // n_seq)
    slot_ids = jnp.arange(prior.shape[0])
    live_mask = slot_ids < counts[0]
    dest_shard = positions // ROWS
    row_code = (positions % ROWS - section_idx * q_rows + 1).astype(BF16)
    dest_prior = dest_shard[tiles:]
    earlier = (
        (dest_prior[None, :] == dest_prior[:, None])
        & (slot_ids[None, :] < slot_ids[:, None])
        & live_mask[None, :]
    )
    within = jnp.sum(earlier.astype(jnp.int32), axis=1)
    bucket = jnp.where(live_mask, dest_prior * capacity + within, -1)
    code_prior = jnp.broadcast_to(row_code[tiles:, None], (prior.shape[0], 128))
    send = vmem_call(
        select_kernel,
        jax.ShapeDtypeStruct((n_seq * capacity, prior.shape[1] + 128), BF16),
        200_000_000,
        2_000_000,
        0,
        row(bucket), prior, code_prior,
    )

    got_prior = lax.all_to_all(
        send.reshape(n_seq, capacity, send.shape[1]), SEQ_AXES, 0, 0, tiled=True
    )
    left, right, low_in, high_in, feats = lax.optimization_barrier(
        (left, right, left[: 2 * share], right[2 * share :], feats)
    )
    low = rotate(low_in, "section", N_SECTION, 1)
    high = rotate(high_in, "section", N_SECTION, -1)
    left_swap = rotate(left, "core", N_CORE, 1)
    right_swap = rotate(right, "core", N_CORE, 1)
    pixels = feats.shape[1] * feats.shape[2]
    normed_maps, feat_mean = vmem_call(
        conv_kernel,
        (
            jax.ShapeDtypeStruct((tiles * pixels, channels), BF16),
            jax.ShapeDtypeStruct((tiles, channels), F32),
        ),
        30_000_000_000,
        8_000_000,
        0,
        feats, dw_weight.reshape(-1, channels), row(dw_bias), row(ln1_gain),
        scratch=[pltpu.VMEM((pixels, channels), F32)],
    )
    low, high, normed_maps, feat_mean = lax.optimization_barrier(
        (low, high, normed_maps, feat_mean)
    )
    low_swap = rotate(low, "core", N_CORE, 1)
    high_swap = rotate(high, "core", N_CORE, 1)
    code_fresh = jnp.where(
        jnp.arange(128)[None, :] == 0,
        row_code[:tiles, None].astype(F32),
        dest_shard[:tiles, None].astype(F32),
    )
    hid = local_call(
        early_kernel,
        jax.ShapeDtypeStruct((3, tiles, share), F32),
        [],
        2_000_000_000,
        6_000_000,
        where, normed_maps, w_up, block, left, right, left_swap, right_swap,
    )
    fresh = local_call(
        late_kernel,
        jax.ShapeDtypeStruct((tiles, channels + 128), BF16),
        [],
        2_000_000_000,
        8_000_000,
        where, normed_maps, hid, feat_mean, row(layer_scale), row(b_down), row(lnf_gain),
        code_fresh, w_down, w_head, w_in, left, right, left_swap, right_swap, low, high, low_swap,
        high_swap,
    )
    got_prior, fresh = lax.optimization_barrier((got_prior, fresh))
    fresh_z = spread(fresh, "z", N_Z).reshape(N_Z * tiles, channels + 128)
    x_earlier = local_call(
        earlier_kernel,
        jax.ShapeDtypeStruct((q_rows, channels), F32),
        [pltpu.VMEM((q_rows, prior.shape[1]), BF16)],
        500_000_000,
        4_000_000,
        where, got_prior.reshape(send.shape), w_in, left, right, left_swap, right_swap, high, high_swap,
    )
    fresh_z, x_earlier = lax.optimization_barrier((fresh_z, x_earlier))
    plane = N_Y * N_CORE
    room = N_Z * capacity
    to_plane = local_call(
        scatter_kernel,
        jax.ShapeDtypeStruct((plane * room, channels + 128), BF16),
        [],
        60_000_000,
        1_000_000,
        where, fresh_z,
    )
    got = lax.all_to_all(
        to_plane.reshape(plane, room, channels + 128), ("y", "core"), 0, 0, tiled=True
    ).reshape(plane * room, channels + 128)
    x_local = vmem_call(
        arrive_kernel,
        jax.ShapeDtypeStruct((q_rows, channels), BF16),
        30_000_000,
        1_000_000,
        0,
        got, x_earlier,
    )
    x_rows = spread(x_local, "section", n_section).reshape(ROWS, channels)

    heads_here = w_qkv.shape[1] // (3 * HS)
    width = heads_here * HS
    stride_rows = ROWS // RB
    my_offsets = lax.dynamic_slice_in_dim(offsets, section_idx * heads_here, heads_here)
    off_lane = row(jnp.repeat(my_offsets, HS))
    w_q, w_k, w_v = (w_qkv[:, part * width : (part + 1) * width] for part in range(3))
    small = lambda rows, kind: jax.ShapeDtypeStruct((rows, width), kind)
    q, k, v, far_q, far_kv = vmem_call(
        project_kernel,
        (small(ROWS, BF16),) * 3
        + (small(stride_rows, F32), jax.ShapeDtypeStruct((stride_rows, 2 * width), BF16)),
        300_000_000,
        2_000_000,
        0,
        x_rows, row(ln_gain), w_q, w_k, w_v, row(jnp.tile(qn_gain, heads_here)),
        row(jnp.tile(kn_gain, heads_here)), off_lane,
    )
    z_kv = spread(far_kv, "z", N_Z).reshape(N_Z * stride_rows, 2 * width)
    half_kv = lax.all_gather(z_kv, "y", axis=0, tiled=True)
    other_kv = rotate(half_kv, "core", N_CORE, 1)
    width_part = channels // n_section
    den, num, far_den, far_num, residual = local_call(
        near_kernel,
        (small(ROWS, F32),) * 2
        + (small(stride_rows, F32),) * 2
        + (jax.ShapeDtypeStruct((width_part, ROWS), F32),),
        [],
        2_000_000_000,
        2_000_000,
        where, q, k, v, far_q, half_kv, x_rows,
    )
    partial_out = vmem_call(
        far_kernel,
        jax.ShapeDtypeStruct((channels, ROWS), BF16),
        150_000_000,
        2_000_000,
        50_000,
        far_q, other_kv, off_lane, den, num, far_den, far_num,
        jnp.transpose(w_out),
    )
    parts = lax.all_to_all(
        partial_out.reshape(n_section, width_part, ROWS), "section", 0, 0, tiled=True
    )
    total = vmem_call(
        sum_kernel,
        jax.ShapeDtypeStruct((width_part, ROWS), BF16),
        1_000_000,
        1_000_000,
        0,
        residual, parts,
    )
    return jnp.transpose(total)


def solution(mesh):
    fine = Mesh(
        mesh.devices.reshape(N_SECTION, N_Z, N_Y, N_CORE), ("section",) + SEQ_AXES
    )
    both = ("section",) + SEQ_AXES
    placed = (
        P(both, None, None, None),
        P(),
        P(),
        P(),
        P("section", None),
        P("section"),
        P("section", None),
        P(),
        P(),
        P(),
        P(None, "section"),
        P(both, None),
        P(both),
        P(both),
        P("section", None),
        P(),
        P(None, "section"),
        P(),
        P(),
        P(),
        P("section", None),
    )
    return jax.shard_map(
        shards, mesh=fine, in_specs=placed, out_specs=P(SEQ_AXES, "section"), check_vma=False
    )
```

```python
import math

import jax
import jax.numpy as jnp
from jax import lax
from jax.experimental import pallas as pl
from jax.experimental.pallas import tpu as pltpu
from jax.sharding import Mesh
from jax.sharding import PartitionSpec as P

HS = 64
RB = 16
ROWS = 256
N_SECTION = 4
N_ZH, N_ZL, N_Y, N_CORE = 4, 4, 4, 2
SEQ_AXES = ("zh", "zl", "y", "core")
F32 = jnp.float32
BF16 = jnp.bfloat16


def layer_norm(values, gain_vec):
    row_mean = jnp.mean(values, axis=-1, keepdims=True)
    centered = values - row_mean
    variance = jnp.mean(centered * centered, axis=-1, keepdims=True)
    return centered * lax.rsqrt(variance + 1e-06) * gain_vec


def rotate(block, axis, size, step):
    return lax.ppermute(block, axis, [(i, (i + step) % size) for i in range(size)])


def exchange(copies, axis):
    return lax.all_to_all(copies, axis, 0, 0, tiled=True)


NT = (((1,), (1,)), ((), ()))


def dot(a, b):
    return jnp.dot(a, b, preferred_element_type=F32)


def gelu_mean(pre, tiles):
    hidden = (0.5 * pre * (1.0 + lax.erf(pre * (1.0 / math.sqrt(2.0))))).astype(BF16).astype(F32)
    return jnp.mean(hidden.reshape(tiles, hidden.shape[0] // tiles, hidden.shape[1]), axis=1)


def lanes(ref, index, width):
    return ref[:, pl.ds(pl.multiple_of(index * width, 128), width)]


def pack_kernel(core_ref, w_up, w_down, w_head, w_in, bias, out, sems):
    n = w_up.shape[0]
    start = pl.multiple_of(core_ref[0] * n, n)
    parts = (
        w_up.at[:, pl.ds(start, n)],
        w_down.at[:, pl.ds(start, n)],
        w_head.at[pl.ds(start, n), :],
        w_in.at[:, pl.ds(start, n)],
    )
    copies = [
        pltpu.make_async_copy(part, out.at[pl.ds(k * n, n), :], sems.at[k])
        for k, part in enumerate(parts)
    ]
    for copy in copies:
        copy.start()
    out[4 * n :, :] = jnp.broadcast_to(bias[...][None, :], (16, n))
    for copy in copies:
        copy.wait()


def pack(core, w_up, w_down, w_head, w_in, bias):
    n = w_up.shape[0]
    vmem = pl.BlockSpec(memory_space=pltpu.VMEM)
    return pl.pallas_call(
        pack_kernel,
        in_specs=[pl.BlockSpec(memory_space=pltpu.SMEM)]
        + [pl.BlockSpec(memory_space=pl.ANY)] * 4
        + [vmem],
        out_specs=vmem,
        out_shape=jax.ShapeDtypeStruct((4 * n + 16, n), BF16),
        scratch_shapes=[pltpu.SemaphoreType.DMA((4,))],
        cost_estimate=pl.CostEstimate(flops=0, bytes_accessed=4 * n * n * 4, transcendentals=0),
    )(core.astype(jnp.int32)[None], w_up, w_down, w_head, w_in, bias)


def natural(core, a, b):
    return jnp.where(core == 0, jnp.concatenate([a, b], 1), jnp.concatenate([b, a], 1))


def conv_kernel(feats, dw_weight, dw_bias, gain, out, mean, conv):
    tiles, channels = mean.shape
    side = math.isqrt(feats.shape[0] // tiles)
    taps = math.isqrt(dw_weight.shape[0])
    reach = (taps - 1) // 2
    column = lax.broadcasted_iota(jnp.int32, (side, side, 128), 1)
    tile_row = lax.broadcasted_iota(jnp.int32, (tiles, 128), 0)
    mean[...] = jnp.zeros_like(mean)

    def one_tile(tile, carry):
        start = pl.multiple_of(tile * side * side, side * side)
        for chunk in range(channels // 128):
            cols = pl.ds(chunk * 128, 128)
            source = feats[pl.ds(start, side * side), cols].astype(F32)
            source = source.reshape(side, side, 128)
            total = jnp.sum(jnp.sum(source, axis=0), axis=0, keepdims=True)
            total = jnp.broadcast_to(total * (1.0 / (side * side)), (tiles, 128))
            mean[:, cols] = jnp.where(tile_row == tile, total, mean[:, cols])
            bias = jnp.broadcast_to(dw_bias[0:1, cols], (side, 128))
            sums = [bias] * side
            for b in range(taps):
                move = b - reach
                moved = source
                if move:
                    moved = pltpu.roll(source, (-move) % side, 1)
                    inside = (column + move >= 0) & (column + move < side)
                    moved = jnp.where(inside, moved, 0.0)
                for a in range(taps):
                    tap = dw_weight[a * taps + b : a * taps + b + 1, cols]
                    tap = jnp.broadcast_to(tap, (side, 128))
                    for i in range(side):
                        if 0 <= i + a - reach < side:
                            sums[i] = sums[i] + moved[i + a - reach] * tap
            for i in range(side):
                conv[i * side : (i + 1) * side, cols] = sums[i]
        out[pl.ds(start, side * side), :] = layer_norm(conv[...], gain[...]).astype(BF16)
        return carry

    lax.fori_loop(0, tiles, one_tile, 0)


def first_row(ref, start):
    return ref[start : start + 16, :].astype(F32)[0:1, :]


def early_kernel(where, maps, up, block, left, right, left_swap, right_swap, hid):
    core = where[0]
    n = up.shape[0]
    tiles = hid.shape[1]
    maps_a, maps_b = lanes(maps, core, n), lanes(maps, 1 - core, n)
    pre = lax.dot_general(maps[...], up[...], NT, preferred_element_type=F32)
    hid[0] = gelu_mean(pre + first_row(block, 4 * n), tiles)
    for slot, (a, b) in enumerate(((left, left_swap), (right, right_swap))):
        pre = lax.dot_general(maps_a, a[0:n, :], NT, preferred_element_type=F32)
        pre += lax.dot_general(maps_b, b[0:n, :], NT, preferred_element_type=F32)
        hid[slot + 1] = gelu_mean(pre + first_row(a, 4 * n), tiles)


def late_kernel(
    where, maps, hid, feat_mean, layer_scale, b_down, lnf_gain, code, w_down, w_head, w_in,
    left, right, left_swap, right_swap, low, high, low_swap, high_swap, out,
):
    core = where[0]
    n = w_down.shape[0]
    tiles = hid.shape[1]
    pre = lax.dot_general(lanes(maps, core, n), low[0:n, :], NT, preferred_element_type=F32)
    pre += lax.dot_general(
        lanes(maps, 1 - core, n), low_swap[0:n, :], NT, preferred_element_type=F32
    )
    hid_far = gelu_mean(pre + first_row(high, 2 * n), tiles)

    def exact(block):
        upper = block.astype(BF16)
        lower = (block - upper.astype(F32)).astype(BF16)
        return jnp.concatenate([upper.astype(F32), lower.astype(F32)], 0).astype(BF16)

    sides = ((left, left_swap), (right, right_swap))
    own = dot(exact(hid[0]), w_down[...])
    part = exact(hid_far)
    br_a, br_b = dot(part, low[n : 2 * n, :]), dot(part, low_swap[n : 2 * n, :])
    for slot, (a, b) in enumerate(sides):
        part = exact(hid[slot + 1])
        br_a += dot(part, a[n : 2 * n, :])
        br_b += dot(part, b[n : 2 * n, :])
    branch = own + natural(core, br_a, br_b)
    branch = branch[0:tiles] + branch[tiles : 2 * tiles]
    pooled = feat_mean[...] + layer_scale[...] * (branch + b_down[...])
    feature = layer_norm(pooled, lnf_gain[...])
    first, second = feature[:, 0:n], feature[:, n : 2 * n]
    feature_a = jnp.where(core == 0, first, second).astype(BF16)
    feature_b = jnp.where(core == 0, second, first).astype(BF16)
    emb = dot(feature.astype(BF16), w_head[...]).astype(BF16)
    own = dot(emb, w_in[...])
    emb = (dot(feature_a, high[0:n, :]) + dot(feature_b, high_swap[0:n, :])).astype(BF16)
    x_a, x_b = dot(emb, high[n : 2 * n, :]), dot(emb, high_swap[n : 2 * n, :])
    for a, b in sides:
        emb = dot(feature_a, a[2 * n : 3 * n, :]) + dot(feature_b, b[2 * n : 3 * n, :])
        emb = emb.astype(BF16)
        x_a += dot(emb, a[3 * n : 4 * n, :])
        x_b += dot(emb, b[3 * n : 4 * n, :])
    x_fresh = own + natural(core, x_a, x_b)
    out[...] = jnp.concatenate([x_fresh, code[...]], axis=1).astype(BF16)


def select_kernel(bucket, rows, code, out):
    places = lax.broadcasted_iota(jnp.int32, (out.shape[0], bucket.shape[1]), 0)
    select = jnp.where(places == bucket[...], 1.0, 0.0).astype(BF16)
    width = rows.shape[1]
    out[:, 0:width] = dot(select, rows[...]).astype(BF16)
    out[:, width:] = dot(select, code[...]).astype(BF16)


def column_as_row(ref, column):
    lane = lax.broadcasted_iota(jnp.int32, (8, 128), 1)
    unit_row = jnp.where(lane == column, 1.0, 0.0).astype(BF16)
    tail = ref[:, ref.shape[1] - 128 :]
    return lax.dot_general(unit_row, tail, NT, preferred_element_type=F32)[0:1, :]


def place_rows(got, q_rows):
    code = column_as_row(got, 0)
    places = lax.broadcasted_iota(jnp.int32, (q_rows, got.shape[0]), 0).astype(F32) + 1.0
    placer = jnp.where(places == code, 1.0, 0.0).astype(BF16)
    return dot(placer, got[:, 0 : got.shape[1] - 128])


def earlier_kernel(
    where, got, w_in, left, right, left_swap, right_swap, high, high_swap, out, rows
):
    n = w_in.shape[0]
    rows[...] = place_rows(got, out.shape[0]).astype(BF16)
    own = dot(lanes(rows, where[1], n), w_in[...])
    columns = lanes(rows, where[4], n)
    x_a, x_b = dot(columns, high[n : 2 * n, :]), dot(columns, high_swap[n : 2 * n, :])
    for slot, (a, b) in enumerate(((left, left_swap), (right, right_swap))):
        columns = lanes(rows, where[slot + 2], n)
        x_a += dot(columns, a[3 * n : 4 * n, :])
        x_b += dot(columns, b[3 * n : 4 * n, :])
    out[...] = own + natural(where[0], x_a, x_b)


def scatter_kernel(where, rows, out):
    count = rows.shape[0]
    dest_row = column_as_row(rows, 1)
    dest = rows[:, rows.shape[1] - 128 :].astype(F32)[:, 1:2]
    index_a = lax.broadcasted_iota(jnp.int32, (count, count), 0)
    index_b = lax.broadcasted_iota(jnp.int32, (count, count), 1)
    before = jnp.where((dest == dest_row) & (index_a < index_b), 1.0, 0.0)
    rank = jnp.sum(before, axis=0, keepdims=True).astype(jnp.int32)
    shard = dest_row.astype(jnp.int32)
    plane = N_ZL * N_Y * N_CORE
    room = out.shape[0] // plane
    inside = shard - where[5] * plane
    bucket = jnp.where((inside >= 0) & (inside < plane), inside * room + rank, -1)
    places = lax.broadcasted_iota(jnp.int32, (out.shape[0], count), 0)
    select = jnp.where(places == bucket, 1.0, 0.0).astype(BF16)
    out[...] = dot(select, rows[...]).astype(BF16)


def arrive_kernel(got, earlier, out):
    rows = (place_rows(got, out.shape[1]) + earlier[...]).astype(BF16)
    for copy in range(out.shape[0]):
        out[copy] = rows


def local_call(body, outs, scratch, flops, size, *operands):
    vmem = pl.BlockSpec(memory_space=pltpu.VMEM)
    return pl.pallas_call(
        body,
        in_specs=[pl.BlockSpec(memory_space=pltpu.SMEM)] + [vmem] * (len(operands) - 1),
        out_specs=jax.tree.map(lambda _: vmem, outs),
        out_shape=outs,
        scratch_shapes=scratch,
        compiler_params=pltpu.CompilerParams(vmem_limit_bytes=16 * 2**20),
        cost_estimate=pl.CostEstimate(flops=flops, bytes_accessed=size, transcendentals=0),
    )(*operands)


def head_lanes(shape, head):
    lane = lax.broadcasted_iota(jnp.int32, shape, len(shape) - 1)
    return (lane >= head * HS) & (lane < (head + 1) * HS)


def dilated(shape, off_lane):
    return lax.rem(lax.broadcasted_iota(jnp.int32, shape, 0), RB) == off_lane


def project_kernel(x, ln_gain, w_q, w_k, w_v, q_gain, k_gain, off_lane, q, k, v, far_q, far_kv):
    rows, width = q.shape
    normed = layer_norm(x[...].astype(F32), ln_gain[...]).astype(BF16)
    chosen = dilated((rows, width), off_lane[...])

    def unit(raw, gain):
        raw = raw.astype(BF16).astype(F32)
        square = raw * raw
        mean = jnp.zeros_like(raw)
        for head in range(width // HS):
            inside = head_lanes(raw.shape, head)
            total = jnp.sum(jnp.where(inside, square, 0.0), axis=1, keepdims=True) * (1.0 / HS)
            mean = jnp.where(inside, total, mean)
        return (raw * lax.rsqrt(mean + 1e-06) * gain).astype(BF16)

    def far_rows(part):
        kept = jnp.where(chosen, part.astype(F32), 0.0)
        return jnp.sum(kept.reshape(rows // RB, RB, width), axis=1)

    q_rows = unit(dot(normed, w_q[...]), q_gain[...])
    k_rows = unit(dot(normed, w_k[...]), k_gain[...])
    v_rows = dot(normed, w_v[...]).astype(BF16)
    q[...], k[...], v[...] = q_rows, k_rows, v_rows
    far_q[...] = far_rows(q_rows)
    pairs = jnp.concatenate([far_rows(k_rows), far_rows(v_rows)], axis=1).astype(BF16)
    for copy in range(far_kv.shape[0]):
        far_kv[copy] = pairs


def by_head(block):
    heads = block.shape[1] // HS
    wide = block.astype(F32)
    kept = [jnp.where(head_lanes(wide.shape, head), wide, 0.0) for head in range(heads)]
    return jnp.concatenate(kept, axis=0)


def back(block, rows, width):
    out = jnp.zeros((rows, width), F32)
    for head in range(width // HS):
        part = jnp.broadcast_to(block[head * rows : (head + 1) * rows], (rows, width))
        out = jnp.where(head_lanes(out.shape, head), part, out)
    return out


def weigh(queries, keys, values):
    scores = lax.dot_general(queries, keys, NT, preferred_element_type=F32)
    weights = jnp.exp(scores * (1.0 / math.sqrt(HS)))
    return jnp.sum(weights, axis=1, keepdims=True), dot(weights.astype(BF16), values)


def far_part(far_q, kv):
    rows, width = far_q.shape
    spread_q = by_head(far_q[...])
    spread_q = jnp.concatenate([spread_q, jnp.zeros_like(spread_q)], axis=1).astype(BF16)
    den, num = weigh(spread_q, kv[...], kv[...])
    return back(den, rows, width), back(num[:, width:], rows, width)


def near_kernel(where, q, k, v, far_q, kv, x, den, num, far_den, far_num, residual):
    wanted = lax.broadcasted_iota(jnp.int32, (residual.shape[0], x.shape[1]), 0)
    column = lax.broadcasted_iota(jnp.int32, (residual.shape[0], x.shape[1]), 1)
    pick = jnp.where(column == wanted + where[1] * residual.shape[0], 1.0, 0.0).astype(BF16)
    residual[...] = lax.dot_general(pick, x[...], NT, preferred_element_type=F32)
    rows, width = q.shape
    local_den, local_num = weigh(by_head(q[...]).astype(BF16), k[...], v[...])
    den[...] = back(local_den, rows, width)
    num[...] = back(local_num, rows, width)
    far_den[...], far_num[...] = far_part(far_q, kv)


def far_kernel(far_q, kv, off_lane, den, num, far_den, far_num, w_out, out):
    rows, width = num.shape
    chosen = dilated((rows, width), off_lane[...])
    more_den, more_num = far_part(far_q, kv)

    def placed(block):
        wide = jnp.broadcast_to(block[:, None, :], (rows // RB, RB, width))
        return jnp.where(chosen, wide.reshape(rows, width), 0.0)

    attended = (num[...] + placed(far_num[...] + more_num)) / (
        den[...] + placed(far_den[...] + more_den)
    )
    attended = attended.astype(BF16)
    out[...] = lax.dot_general(w_out[...], attended, NT, preferred_element_type=F32).astype(BF16)


def sum_kernel(residual, parts, out):
    total = residual[...]
    for part in range(parts.shape[0]):
        total += parts[part].astype(F32)
    out[...] = total.astype(BF16)


def vmem_call(body, outs, flops, size, exps, *operands, scratch=()):
    vmem = pl.BlockSpec(memory_space=pltpu.VMEM)
    return pl.pallas_call(
        body,
        in_specs=[vmem] * len(operands),
        out_specs=jax.tree.map(lambda _: vmem, outs),
        out_shape=outs,
        scratch_shapes=list(scratch),
        compiler_params=pltpu.CompilerParams(vmem_limit_bytes=16 * 2**20),
        cost_estimate=pl.CostEstimate(flops=flops, bytes_accessed=size, transcendentals=exps),
    )(*operands)


def shards(
    feats,
    dw_weight,
    dw_bias,
    ln1_gain,
    w_up,
    b_up,
    w_down,
    b_down,
    layer_scale,
    lnf_gain,
    w_head,
    prior,
    counts,
    positions,
    w_in,
    ln_gain,
    w_qkv,
    qn_gain,
    kn_gain,
    offsets,
    w_out,
):
    n_section = N_SECTION
    n_seq = N_ZH * N_ZL * N_Y * N_CORE
    section_idx = lax.axis_index("section")
    core = lax.axis_index("core")
    tiles = feats.shape[0]
    channels = feats.shape[3]
    half = channels // N_CORE
    share = w_up.shape[0]

    row = lambda vec: vec[None, :]
    others = [(section_idx + step) % N_SECTION for step in (3, 1, 2)]
    where = jnp.stack([core, section_idx] + others + [lax.axis_index("zh")]).astype(jnp.int32)

    block = pack(core, w_up, w_down, w_head, w_in, b_up)
    block, prior = lax.optimization_barrier((block, prior))
    left = rotate(block, "section", N_SECTION, 1)
    right = rotate(block, "section", N_SECTION, -1)

    q_rows = ROWS // n_section
    capacity = -(-(tiles + prior.shape[0]) // n_seq)
    slot_ids = jnp.arange(prior.shape[0])
    live_mask = slot_ids < counts[0]
    dest_shard = positions // ROWS
    row_code = (positions % ROWS - section_idx * q_rows + 1).astype(BF16)
    dest_prior = dest_shard[tiles:]
    earlier = (
        (dest_prior[None, :] == dest_prior[:, None])
        & (slot_ids[None, :] < slot_ids[:, None])
        & live_mask[None, :]
    )
    within = jnp.sum(earlier.astype(jnp.int32), axis=1)
    bucket = jnp.where(live_mask, dest_prior * capacity + within, -1)
    code_prior = jnp.broadcast_to(row_code[tiles:, None], (prior.shape[0], 128))
    send = vmem_call(
        select_kernel,
        jax.ShapeDtypeStruct((n_seq * capacity, prior.shape[1] + 128), BF16),
        200_000_000,
        2_000_000,
        0,
        row(bucket), prior, code_prior,
    )

    got_prior = lax.all_to_all(
        send.reshape(n_seq, capacity, send.shape[1]), SEQ_AXES, 0, 0, tiled=True
    )
    left, right, low_in, high_in, feats = lax.optimization_barrier(
        (left, right, left[: 2 * share], right[2 * share :], feats)
    )
    low = rotate(low_in, "section", N_SECTION, 1)
    high = rotate(high_in, "section", N_SECTION, -1)
    left_swap = rotate(left, "core", N_CORE, 1)
    right_swap = rotate(right, "core", N_CORE, 1)
    pixels = feats.shape[1] * feats.shape[2]
    normed_maps, feat_mean = vmem_call(
        conv_kernel,
        (
            jax.ShapeDtypeStruct((tiles * pixels, channels), BF16),
            jax.ShapeDtypeStruct((tiles, channels), F32),
        ),
        30_000_000_000,
        8_000_000,
        0,
        feats.reshape(-1, channels), dw_weight.reshape(-1, channels), row(dw_bias), row(ln1_gain),
        scratch=[pltpu.VMEM((pixels, channels), F32)],
    )
    low, high, normed_maps, feat_mean = lax.optimization_barrier(
        (low, high, normed_maps, feat_mean)
    )
    low_swap = rotate(low, "core", N_CORE, 1)
    high_swap = rotate(high, "core", N_CORE, 1)
    code_fresh = jnp.where(
        jnp.arange(128)[None, :] == 0,
        row_code[:tiles, None].astype(F32),
        dest_shard[:tiles, None].astype(F32),
    )
    hid = local_call(
        early_kernel,
        jax.ShapeDtypeStruct((3, tiles, share), F32),
        [],
        2_000_000_000,
        6_000_000,
        where, normed_maps, w_up, block, left, right, left_swap, right_swap,
    )
    fresh = local_call(
        late_kernel,
        jax.ShapeDtypeStruct((tiles, channels + 128), BF16),
        [],
        2_000_000_000,
        8_000_000,
        where, normed_maps, hid, feat_mean, row(layer_scale), row(b_down), row(lnf_gain),
        code_fresh, w_down, w_head, w_in, left, right, left_swap, right_swap, low, high, low_swap,
        high_swap,
    )
    fresh_z = lax.all_gather(fresh, "zh", axis=0, tiled=True)
    plane = N_ZL * N_Y * N_CORE
    room = N_ZH * capacity
    to_plane = local_call(
        scatter_kernel,
        jax.ShapeDtypeStruct((plane * room, channels + 128), BF16),
        [],
        60_000_000,
        1_000_000,
        where, fresh_z,
    )
    to_plane, got_prior = lax.optimization_barrier((to_plane, got_prior))
    got = lax.all_to_all(
        to_plane.reshape(plane, room, channels + 128), SEQ_AXES[1:], 0, 0, tiled=True
    ).reshape(plane * room, channels + 128)
    x_earlier = local_call(
        earlier_kernel,
        jax.ShapeDtypeStruct((q_rows, channels), F32),
        [pltpu.VMEM((q_rows, prior.shape[1]), BF16)],
        500_000_000,
        4_000_000,
        where, got_prior.reshape(send.shape), w_in, left, right, left_swap, right_swap, high,
        high_swap,
    )
    x_copies = vmem_call(
        arrive_kernel,
        jax.ShapeDtypeStruct((n_section, q_rows, channels), BF16),
        30_000_000,
        1_000_000,
        0,
        got, x_earlier,
    )
    x_rows = exchange(x_copies, "section").reshape(ROWS, channels)

    heads_here = w_qkv.shape[1] // (3 * HS)
    width = heads_here * HS
    stride_rows = ROWS // RB
    my_offsets = lax.dynamic_slice_in_dim(offsets, section_idx * heads_here, heads_here)
    off_lane = row(jnp.repeat(my_offsets, HS))
    w_q, w_k, w_v = (w_qkv[:, part * width : (part + 1) * width] for part in range(3))
    small = lambda rows, kind: jax.ShapeDtypeStruct((rows, width), kind)
    q, k, v, far_q, far_kv = vmem_call(
        project_kernel,
        (small(ROWS, BF16),) * 3
        + (small(stride_rows, F32), jax.ShapeDtypeStruct((N_ZH, stride_rows, 2 * width), BF16)),
        300_000_000,
        2_000_000,
        0,
        x_rows, row(ln_gain), w_q, w_k, w_v, row(jnp.tile(qn_gain, heads_here)),
        row(jnp.tile(kn_gain, heads_here)), off_lane,
    )
    z_kv = exchange(far_kv, "zh").reshape(N_ZH * stride_rows, 2 * width)
    z_copies = jnp.broadcast_to(z_kv[None], (N_ZL * N_Y,) + z_kv.shape)
    half_kv = exchange(z_copies, ("zl", "y")).reshape(n_seq // N_CORE * stride_rows, 2 * width)
    other_kv = rotate(half_kv, "core", N_CORE, 1)
    width_part = channels // n_section
    den, num, far_den, far_num, residual = local_call(
        near_kernel,
        (small(ROWS, F32),) * 2
        + (small(stride_rows, F32),) * 2
        + (jax.ShapeDtypeStruct((width_part, ROWS), F32),),
        [],
        2_000_000_000,
        2_000_000,
        where, q, k, v, far_q, half_kv, x_rows,
    )
    partial_out = vmem_call(
        far_kernel,
        jax.ShapeDtypeStruct((channels, ROWS), BF16),
        150_000_000,
        2_000_000,
        50_000,
        far_q, other_kv, off_lane, den, num, far_den, far_num,
        jnp.transpose(w_out),
    )
    parts = lax.all_to_all(
        partial_out.reshape(n_section, width_part, ROWS), "section", 0, 0, tiled=True
    )
    total = vmem_call(
        sum_kernel,
        jax.ShapeDtypeStruct((width_part, ROWS), BF16),
        1_000_000,
        1_000_000,
        0,
        residual, parts,
    )
    return jnp.transpose(total)


def solution(mesh):
    fine = Mesh(
        mesh.devices.reshape(N_SECTION, N_ZH, N_ZL, N_Y, N_CORE), ("section",) + SEQ_AXES
    )
    both = ("section",) + SEQ_AXES
    placed = (
        P(both, None, None, None),
        P(),
        P(),
        P(),
        P("section", None),
        P("section"),
        P("section", None),
        P(),
        P(),
        P(),
        P(None, "section"),
        P(both, None),
        P(both),
        P(both),
        P("section", None),
        P(),
        P(None, "section"),
        P(),
        P(),
        P(),
        P("section", None),
    )
    return jax.shard_map(
        shards, mesh=fine, in_specs=placed, out_specs=P(SEQ_AXES, "section"), check_vma=False
    )
```

```python
import math

import jax
import jax.numpy as jnp
from jax import lax
from jax.experimental import pallas as pl
from jax.experimental.pallas import tpu as pltpu
from jax.sharding import Mesh
from jax.sharding import PartitionSpec as P

HS = 64
RB = 16
ROWS = 256
N_SECTION = 4
N_Z, N_Y, N_CORE = 16, 4, 2
SEQ_AXES = ("z", "y", "core")
F32 = jnp.float32
BF16 = jnp.bfloat16


def layer_norm(values, gain_vec):
    row_mean = jnp.mean(values, axis=-1, keepdims=True)
    centered = values - row_mean
    variance = jnp.mean(centered * centered, axis=-1, keepdims=True)
    return centered * lax.rsqrt(variance + 1e-06) * gain_vec


def rotate(block, axis, size, step):
    return lax.ppermute(block, axis, [(i, (i + step) % size) for i in range(size)])


def exchange(copies, axis):
    return lax.all_to_all(copies, axis, 0, 0, tiled=True)


NT = (((1,), (1,)), ((), ()))


def dot(a, b):
    return jnp.dot(a, b, preferred_element_type=F32)


def gelu_mean(pre, tiles):
    hidden = (0.5 * pre * (1.0 + lax.erf(pre * (1.0 / math.sqrt(2.0))))).astype(BF16).astype(F32)
    return jnp.mean(hidden.reshape(tiles, hidden.shape[0] // tiles, hidden.shape[1]), axis=1)


def lanes(ref, index, width):
    return ref[:, pl.ds(pl.multiple_of(index * width, 128), width)]


def pack_kernel(core_ref, w_up, w_down, w_head, w_in, bias, out, rows, sems):
    n = w_up.shape[0]
    start = pl.multiple_of(core_ref[0] * n, n)
    parts = (
        w_up.at[:, pl.ds(start, n)],
        w_down.at[:, pl.ds(start, n)],
        w_head.at[pl.ds(start, n), :],
        w_in.at[:, pl.ds(start, n)],
    )
    copies = [
        pltpu.make_async_copy(part, out.at[pl.ds(k * n, n), :], sems.at[k])
        for k, part in enumerate(parts)
    ]
    for copy in copies:
        copy.start()
    rows[...] = jnp.broadcast_to(bias[...][None, :], (16, n))
    copies.append(pltpu.make_async_copy(rows, out.at[pl.ds(4 * n, 16), :], sems.at[4]))
    copies[-1].start()
    for copy in copies:
        copy.wait()


def pack(core, w_up, w_down, w_head, w_in, bias):
    n = w_up.shape[0]
    vmem = pl.BlockSpec(memory_space=pltpu.VMEM)
    return pl.pallas_call(
        pack_kernel,
        in_specs=[pl.BlockSpec(memory_space=pltpu.SMEM)]
        + [pl.BlockSpec(memory_space=pl.ANY)] * 4
        + [vmem],
        out_specs=pl.BlockSpec(memory_space=pl.ANY),
        out_shape=jax.ShapeDtypeStruct((4 * n + 16, n), BF16),
        scratch_shapes=[pltpu.VMEM((16, n), BF16), pltpu.SemaphoreType.DMA((5,))],
        cost_estimate=pl.CostEstimate(flops=0, bytes_accessed=4 * n * n * 4, transcendentals=0),
    )(core.astype(jnp.int32)[None], w_up, w_down, w_head, w_in, bias)


def natural(core, a, b):
    return jnp.where(core == 0, jnp.concatenate([a, b], 1), jnp.concatenate([b, a], 1))


def conv_kernel(feats, dw_weight, dw_bias, gain, out, mean, conv):
    tiles, channels = mean.shape
    side = math.isqrt(feats.shape[0] // tiles)
    taps = math.isqrt(dw_weight.shape[0])
    reach = (taps - 1) // 2
    column = lax.broadcasted_iota(jnp.int32, (side, side, 128), 1)
    tile_row = lax.broadcasted_iota(jnp.int32, (tiles, 128), 0)
    mean[...] = jnp.zeros_like(mean)

    def one_tile(tile, carry):
        start = pl.multiple_of(tile * side * side, side * side)
        for chunk in range(channels // 128):
            cols = pl.ds(chunk * 128, 128)
            source = feats[pl.ds(start, side * side), cols].astype(F32)
            source = source.reshape(side, side, 128)
            total = jnp.sum(jnp.sum(source, axis=0), axis=0, keepdims=True)
            total = jnp.broadcast_to(total * (1.0 / (side * side)), (tiles, 128))
            mean[:, cols] = jnp.where(tile_row == tile, total, mean[:, cols])
            bias = jnp.broadcast_to(dw_bias[0:1, cols], (side, 128))
            sums = [bias] * side
            for b in range(taps):
                move = b - reach
                moved = source
                if move:
                    moved = pltpu.roll(source, (-move) % side, 1)
                    inside = (column + move >= 0) & (column + move < side)
                    moved = jnp.where(inside, moved, 0.0)
                for a in range(taps):
                    tap = dw_weight[a * taps + b : a * taps + b + 1, cols]
                    tap = jnp.broadcast_to(tap, (side, 128))
                    for i in range(side):
                        if 0 <= i + a - reach < side:
                            sums[i] = sums[i] + moved[i + a - reach] * tap
            for i in range(side):
                conv[i * side : (i + 1) * side, cols] = sums[i]
        out[pl.ds(start, side * side), :] = layer_norm(conv[...], gain[...]).astype(BF16)
        return carry

    lax.fori_loop(0, tiles, one_tile, 0)


def first_row(ref, start):
    return ref[start : start + 16, :].astype(F32)[0:1, :]


def early_kernel(where, maps, up, block, left, right, left_swap, right_swap, hid):
    core = where[0]
    n = up.shape[0]
    tiles = hid.shape[1]
    maps_a, maps_b = lanes(maps, core, n), lanes(maps, 1 - core, n)
    pre = lax.dot_general(maps[...], up[...], NT, preferred_element_type=F32)
    hid[0] = gelu_mean(pre + first_row(block, 4 * n), tiles)
    for slot, (a, b) in enumerate(((left, left_swap), (right, right_swap))):
        pre = lax.dot_general(maps_a, a[0:n, :], NT, preferred_element_type=F32)
        pre += lax.dot_general(maps_b, b[0:n, :], NT, preferred_element_type=F32)
        hid[slot + 1] = gelu_mean(pre + first_row(a, 4 * n), tiles)


def late_kernel(
    where, maps, hid, feat_mean, layer_scale, b_down, lnf_gain, code, w_down, w_head, w_in,
    left, right, left_swap, right_swap, low, high, low_swap, high_swap, out,
):
    core = where[0]
    n = w_down.shape[0]
    tiles = hid.shape[1]
    pre = lax.dot_general(lanes(maps, core, n), low[0:n, :], NT, preferred_element_type=F32)
    pre += lax.dot_general(
        lanes(maps, 1 - core, n), low_swap[0:n, :], NT, preferred_element_type=F32
    )
    hid_far = gelu_mean(pre + first_row(high, 2 * n), tiles)

    def exact(block):
        upper = block.astype(BF16)
        lower = (block - upper.astype(F32)).astype(BF16)
        return jnp.concatenate([upper.astype(F32), lower.astype(F32)], 0).astype(BF16)

    sides = ((left, left_swap), (right, right_swap))
    own = dot(exact(hid[0]), w_down[...])
    part = exact(hid_far)
    br_a, br_b = dot(part, low[n : 2 * n, :]), dot(part, low_swap[n : 2 * n, :])
    for slot, (a, b) in enumerate(sides):
        part = exact(hid[slot + 1])
        br_a += dot(part, a[n : 2 * n, :])
        br_b += dot(part, b[n : 2 * n, :])
    branch = own + natural(core, br_a, br_b)
    branch = branch[0:tiles] + branch[tiles : 2 * tiles]
    pooled = feat_mean[...] + layer_scale[...] * (branch + b_down[...])
    feature = layer_norm(pooled, lnf_gain[...])
    first, second = feature[:, 0:n], feature[:, n : 2 * n]
    feature_a = jnp.where(core == 0, first, second).astype(BF16)
    feature_b = jnp.where(core == 0, second, first).astype(BF16)
    emb = dot(feature.astype(BF16), w_head[...]).astype(BF16)
    own = dot(emb, w_in[...])
    emb = (dot(feature_a, high[0:n, :]) + dot(feature_b, high_swap[0:n, :])).astype(BF16)
    x_a, x_b = dot(emb, high[n : 2 * n, :]), dot(emb, high_swap[n : 2 * n, :])
    for a, b in sides:
        emb = dot(feature_a, a[2 * n : 3 * n, :]) + dot(feature_b, b[2 * n : 3 * n, :])
        emb = emb.astype(BF16)
        x_a += dot(emb, a[3 * n : 4 * n, :])
        x_b += dot(emb, b[3 * n : 4 * n, :])
    x_fresh = own + natural(core, x_a, x_b)
    out[...] = jnp.concatenate([x_fresh, code[...]], axis=1).astype(BF16)


def select_kernel(bucket, rows, code, out):
    places = lax.broadcasted_iota(jnp.int32, (out.shape[0], bucket.shape[1]), 0)
    select = jnp.where(places == bucket[...], 1.0, 0.0).astype(BF16)
    width = rows.shape[1]
    out[:, 0:width] = dot(select, rows[...]).astype(BF16)
    out[:, width:] = dot(select, code[...]).astype(BF16)


def column_as_row(ref, column):
    lane = lax.broadcasted_iota(jnp.int32, (8, 128), 1)
    unit_row = jnp.where(lane == column, 1.0, 0.0).astype(BF16)
    tail = ref[:, ref.shape[1] - 128 :]
    return lax.dot_general(unit_row, tail, NT, preferred_element_type=F32)[0:1, :]


def place_rows(got, q_rows):
    code = column_as_row(got, 0)
    places = lax.broadcasted_iota(jnp.int32, (q_rows, got.shape[0]), 0).astype(F32) + 1.0
    placer = jnp.where(places == code, 1.0, 0.0).astype(BF16)
    return dot(placer, got[:, 0 : got.shape[1] - 128])


def earlier_kernel(
    where, got, w_in, left, right, left_swap, right_swap, high, high_swap, out, rows
):
    n = w_in.shape[0]
    rows[...] = place_rows(got, out.shape[0]).astype(BF16)
    own = dot(lanes(rows, where[1], n), w_in[...])
    columns = lanes(rows, where[4], n)
    x_a, x_b = dot(columns, high[n : 2 * n, :]), dot(columns, high_swap[n : 2 * n, :])
    for slot, (a, b) in enumerate(((left, left_swap), (right, right_swap))):
        columns = lanes(rows, where[slot + 2], n)
        x_a += dot(columns, a[3 * n : 4 * n, :])
        x_b += dot(columns, b[3 * n : 4 * n, :])
    out[...] = own + natural(where[0], x_a, x_b)


def scatter_kernel(where, rows, out):
    count = rows.shape[0]
    dest_row = column_as_row(rows, 1)
    dest = rows[:, rows.shape[1] - 128 :].astype(F32)[:, 1:2]
    index_a = lax.broadcasted_iota(jnp.int32, (count, count), 0)
    index_b = lax.broadcasted_iota(jnp.int32, (count, count), 1)
    before = jnp.where((dest == dest_row) & (index_a < index_b), 1.0, 0.0)
    rank = jnp.sum(before, axis=0, keepdims=True).astype(jnp.int32)
    shard = dest_row.astype(jnp.int32)
    plane = N_Y * N_CORE
    room = out.shape[0] // plane
    inside = shard - where[5] * plane
    bucket = jnp.where((inside >= 0) & (inside < plane), inside * room + rank, -1)
    places = lax.broadcasted_iota(jnp.int32, (out.shape[0], count), 0)
    select = jnp.where(places == bucket, 1.0, 0.0).astype(BF16)
    out[...] = dot(select, rows[...]).astype(BF16)


def arrive_kernel(got, earlier, out):
    rows = (place_rows(got, out.shape[1]) + earlier[...]).astype(BF16)
    for copy in range(out.shape[0]):
        out[copy] = rows


def local_call(body, outs, scratch, flops, size, *operands):
    vmem = pl.BlockSpec(memory_space=pltpu.VMEM)
    return pl.pallas_call(
        body,
        in_specs=[pl.BlockSpec(memory_space=pltpu.SMEM)] + [vmem] * (len(operands) - 1),
        out_specs=jax.tree.map(lambda _: vmem, outs),
        out_shape=outs,
        scratch_shapes=scratch,
        compiler_params=pltpu.CompilerParams(vmem_limit_bytes=16 * 2**20),
        cost_estimate=pl.CostEstimate(flops=flops, bytes_accessed=size, transcendentals=0),
    )(*operands)


def head_lanes(shape, head):
    lane = lax.broadcasted_iota(jnp.int32, shape, len(shape) - 1)
    return (lane >= head * HS) & (lane < (head + 1) * HS)


def dilated(shape, off_lane):
    return lax.rem(lax.broadcasted_iota(jnp.int32, shape, 0), RB) == off_lane


def project_kernel(x, ln_gain, w_q, w_k, w_v, q_gain, k_gain, off_lane, q, k, v, far_q, far_kv):
    rows, width = q.shape
    normed = layer_norm(x[...].astype(F32), ln_gain[...]).astype(BF16)
    chosen = dilated((rows, width), off_lane[...])

    def unit(raw, gain):
        raw = raw.astype(BF16).astype(F32)
        square = raw * raw
        mean = jnp.zeros_like(raw)
        for head in range(width // HS):
            inside = head_lanes(raw.shape, head)
            total = jnp.sum(jnp.where(inside, square, 0.0), axis=1, keepdims=True) * (1.0 / HS)
            mean = jnp.where(inside, total, mean)
        return (raw * lax.rsqrt(mean + 1e-06) * gain).astype(BF16)

    def far_rows(part):
        kept = jnp.where(chosen, part.astype(F32), 0.0)
        return jnp.sum(kept.reshape(rows // RB, RB, width), axis=1)

    q_rows = unit(dot(normed, w_q[...]), q_gain[...])
    k_rows = unit(dot(normed, w_k[...]), k_gain[...])
    v_rows = dot(normed, w_v[...]).astype(BF16)
    q[...], k[...], v[...] = q_rows, k_rows, v_rows
    far_q[...] = far_rows(q_rows)
    pairs = jnp.concatenate([far_rows(k_rows), far_rows(v_rows)], axis=1).astype(BF16)
    for copy in range(far_kv.shape[0]):
        far_kv[copy] = pairs


def by_head(block):
    heads = block.shape[1] // HS
    wide = block.astype(F32)
    kept = [jnp.where(head_lanes(wide.shape, head), wide, 0.0) for head in range(heads)]
    return jnp.concatenate(kept, axis=0)


def back(block, rows, width):
    out = jnp.zeros((rows, width), F32)
    for head in range(width // HS):
        part = jnp.broadcast_to(block[head * rows : (head + 1) * rows], (rows, width))
        out = jnp.where(head_lanes(out.shape, head), part, out)
    return out


def weigh(queries, keys, values):
    scores = lax.dot_general(queries, keys, NT, preferred_element_type=F32)
    weights = jnp.exp(scores * (1.0 / math.sqrt(HS)))
    return jnp.sum(weights, axis=1, keepdims=True), dot(weights.astype(BF16), values)


def far_part(far_q, kv):
    rows, width = far_q.shape
    spread_q = by_head(far_q[...])
    spread_q = jnp.concatenate([spread_q, jnp.zeros_like(spread_q)], axis=1).astype(BF16)
    den, num = weigh(spread_q, kv[...], kv[...])
    return back(den, rows, width), back(num[:, width:], rows, width)


def near_kernel(where, q, k, v, far_q, kv, x, den, num, far_den, far_num, residual):
    wanted = lax.broadcasted_iota(jnp.int32, (residual.shape[0], x.shape[1]), 0)
    column = lax.broadcasted_iota(jnp.int32, (residual.shape[0], x.shape[1]), 1)
    pick = jnp.where(column == wanted + where[1] * residual.shape[0], 1.0, 0.0).astype(BF16)
    residual[...] = lax.dot_general(pick, x[...], NT, preferred_element_type=F32)
    rows, width = q.shape
    local_den, local_num = weigh(by_head(q[...]).astype(BF16), k[...], v[...])
    den[...] = back(local_den, rows, width)
    num[...] = back(local_num, rows, width)
    far_den[...], far_num[...] = far_part(far_q, kv)


def far_kernel(far_q, kv, off_lane, den, num, far_den, far_num, w_out, out):
    rows, width = num.shape
    chosen = dilated((rows, width), off_lane[...])
    more_den, more_num = far_part(far_q, kv)

    def placed(block):
        wide = jnp.broadcast_to(block[:, None, :], (rows // RB, RB, width))
        return jnp.where(chosen, wide.reshape(rows, width), 0.0)

    attended = (num[...] + placed(far_num[...] + more_num)) / (
        den[...] + placed(far_den[...] + more_den)
    )
    attended = attended.astype(BF16)
    out[...] = lax.dot_general(w_out[...], attended, NT, preferred_element_type=F32).astype(BF16)


def sum_kernel(residual, parts, out):
    total = residual[...]
    for part in range(parts.shape[0]):
        total += parts[part].astype(F32)
    out[...] = total.astype(BF16)


def vmem_call(body, outs, flops, size, exps, *operands, scratch=()):
    vmem = pl.BlockSpec(memory_space=pltpu.VMEM)
    return pl.pallas_call(
        body,
        in_specs=[vmem] * len(operands),
        out_specs=jax.tree.map(lambda _: vmem, outs),
        out_shape=outs,
        scratch_shapes=list(scratch),
        compiler_params=pltpu.CompilerParams(vmem_limit_bytes=16 * 2**20),
        cost_estimate=pl.CostEstimate(flops=flops, bytes_accessed=size, transcendentals=exps),
    )(*operands)


def shards(
    feats,
    dw_weight,
    dw_bias,
    ln1_gain,
    w_up,
    b_up,
    w_down,
    b_down,
    layer_scale,
    lnf_gain,
    w_head,
    prior,
    counts,
    positions,
    w_in,
    ln_gain,
    w_qkv,
    qn_gain,
    kn_gain,
    offsets,
    w_out,
):
    n_section = N_SECTION
    n_seq = N_Z * N_Y * N_CORE
    section_idx = lax.axis_index("section")
    core = lax.axis_index("core")
    tiles = feats.shape[0]
    channels = feats.shape[3]
    half = channels // N_CORE
    share = w_up.shape[0]

    row = lambda vec: vec[None, :]
    others = [(section_idx + step) % N_SECTION for step in (3, 1, 2)]
    where = jnp.stack([core, section_idx] + others + [lax.axis_index("z")]).astype(jnp.int32)

    block = pack(core, w_up, w_down, w_head, w_in, b_up)
    block, prior = lax.optimization_barrier((block, prior))
    left = rotate(block, "section", N_SECTION, 1)
    right = rotate(block, "section", N_SECTION, -1)

    q_rows = ROWS // n_section
    capacity = -(-(tiles + prior.shape[0]) // n_seq)
    slot_ids = jnp.arange(prior.shape[0])
    live_mask = slot_ids < counts[0]
    dest_shard = positions // ROWS
    row_code = (positions % ROWS - section_idx * q_rows + 1).astype(BF16)
    dest_prior = dest_shard[tiles:]
    earlier = (
        (dest_prior[None, :] == dest_prior[:, None])
        & (slot_ids[None, :] < slot_ids[:, None])
        & live_mask[None, :]
    )
    within = jnp.sum(earlier.astype(jnp.int32), axis=1)
    bucket = jnp.where(live_mask, dest_prior * capacity + within, -1)
    code_prior = jnp.broadcast_to(row_code[tiles:, None], (prior.shape[0], 128))
    send = vmem_call(
        select_kernel,
        jax.ShapeDtypeStruct((n_seq * capacity, prior.shape[1] + 128), BF16),
        200_000_000,
        2_000_000,
        0,
        row(bucket), prior, code_prior,
    )

    got_prior = lax.all_to_all(
        send.reshape(n_seq, capacity, send.shape[1]), SEQ_AXES, 0, 0, tiled=True
    )
    left, right, low_in, high_in, feats = lax.optimization_barrier(
        (left, right, left[: 2 * share], right[2 * share :], feats)
    )
    low = rotate(low_in, "section", N_SECTION, 1)
    high = rotate(high_in, "section", N_SECTION, -1)
    left_swap = rotate(left, "core", N_CORE, 1)
    right_swap = rotate(right, "core", N_CORE, 1)
    pixels = feats.shape[1] * feats.shape[2]
    normed_maps, feat_mean = vmem_call(
        conv_kernel,
        (
            jax.ShapeDtypeStruct((tiles * pixels, channels), BF16),
            jax.ShapeDtypeStruct((tiles, channels), F32),
        ),
        30_000_000_000,
        8_000_000,
        0,
        feats.reshape(-1, channels), dw_weight.reshape(-1, channels), row(dw_bias), row(ln1_gain),
        scratch=[pltpu.VMEM((pixels, channels), F32)],
    )
    low, high, normed_maps, feat_mean = lax.optimization_barrier(
        (low, high, normed_maps, feat_mean)
    )
    low_swap = rotate(low, "core", N_CORE, 1)
    high_swap = rotate(high, "core", N_CORE, 1)
    code_fresh = jnp.where(
        jnp.arange(128)[None, :] == 0,
        row_code[:tiles, None].astype(F32),
        dest_shard[:tiles, None].astype(F32),
    )
    hid = local_call(
        early_kernel,
        jax.ShapeDtypeStruct((3, tiles, share), F32),
        [],
        2_000_000_000,
        6_000_000,
        where, normed_maps, w_up, block, left, right, left_swap, right_swap,
    )
    fresh = local_call(
        late_kernel,
        jax.ShapeDtypeStruct((tiles, channels + 128), BF16),
        [],
        2_000_000_000,
        8_000_000,
        where, normed_maps, hid, feat_mean, row(layer_scale), row(b_down), row(lnf_gain),
        code_fresh, w_down, w_head, w_in, left, right, left_swap, right_swap, low, high, low_swap,
        high_swap,
    )
    got_prior, fresh = lax.optimization_barrier((got_prior, fresh))
    fresh_z = exchange(jnp.broadcast_to(fresh[None], (N_Z,) + fresh.shape), "z")
    fresh_z = fresh_z.reshape(N_Z * tiles, channels + 128)
    x_earlier = local_call(
        earlier_kernel,
        jax.ShapeDtypeStruct((q_rows, channels), F32),
        [pltpu.VMEM((q_rows, prior.shape[1]), BF16)],
        500_000_000,
        4_000_000,
        where, got_prior.reshape(send.shape), w_in, left, right, left_swap, right_swap, high,
        high_swap,
    )
    fresh_z, x_earlier = lax.optimization_barrier((fresh_z, x_earlier))
    plane = N_Y * N_CORE
    room = N_Z * capacity
    to_plane = local_call(
        scatter_kernel,
        jax.ShapeDtypeStruct((plane * room, channels + 128), BF16),
        [],
        60_000_000,
        1_000_000,
        where, fresh_z,
    )
    got = lax.all_to_all(
        to_plane.reshape(plane, room, channels + 128), SEQ_AXES[1:], 0, 0, tiled=True
    ).reshape(plane * room, channels + 128)
    x_copies = vmem_call(
        arrive_kernel,
        jax.ShapeDtypeStruct((n_section, q_rows, channels), BF16),
        30_000_000,
        1_000_000,
        0,
        got, x_earlier,
    )
    x_rows = exchange(x_copies, "section").reshape(ROWS, channels)

    heads_here = w_qkv.shape[1] // (3 * HS)
    width = heads_here * HS
    stride_rows = ROWS // RB
    my_offsets = lax.dynamic_slice_in_dim(offsets, section_idx * heads_here, heads_here)
    off_lane = row(jnp.repeat(my_offsets, HS))
    w_q, w_k, w_v = (w_qkv[:, part * width : (part + 1) * width] for part in range(3))
    small = lambda rows, kind: jax.ShapeDtypeStruct((rows, width), kind)
    q, k, v, far_q, far_kv = vmem_call(
        project_kernel,
        (small(ROWS, BF16),) * 3
        + (small(stride_rows, F32), jax.ShapeDtypeStruct((N_Z, stride_rows, 2 * width), BF16)),
        300_000_000,
        2_000_000,
        0,
        x_rows, row(ln_gain), w_q, w_k, w_v, row(jnp.tile(qn_gain, heads_here)),
        row(jnp.tile(kn_gain, heads_here)), off_lane,
    )
    z_kv = exchange(far_kv, "z").reshape(N_Z * stride_rows, 2 * width)
    half_kv = lax.all_gather(z_kv, "y", axis=0, tiled=True)
    other_kv = rotate(half_kv, "core", N_CORE, 1)
    width_part = channels // n_section
    den, num, far_den, far_num, residual = local_call(
        near_kernel,
        (small(ROWS, F32),) * 2
        + (small(stride_rows, F32),) * 2
        + (jax.ShapeDtypeStruct((width_part, ROWS), F32),),
        [],
        2_000_000_000,
        2_000_000,
        where, q, k, v, far_q, half_kv, x_rows,
    )
    partial_out = vmem_call(
        far_kernel,
        jax.ShapeDtypeStruct((channels, ROWS), BF16),
        150_000_000,
        2_000_000,
        50_000,
        far_q, other_kv, off_lane, den, num, far_den, far_num,
        jnp.transpose(w_out),
    )
    parts = lax.all_to_all(
        partial_out.reshape(n_section, width_part, ROWS), "section", 0, 0, tiled=True
    )
    total = vmem_call(
        sum_kernel,
        jax.ShapeDtypeStruct((width_part, ROWS), BF16),
        1_000_000,
        1_000_000,
        0,
        residual, parts,
    )
    return jnp.transpose(total)


def solution(mesh):
    fine = Mesh(
        mesh.devices.reshape(N_SECTION, N_Z, N_Y, N_CORE), ("section",) + SEQ_AXES
    )
    both = ("section",) + SEQ_AXES
    placed = (
        P(both, None, None, None),
        P(),
        P(),
        P(),
        P("section", None),
        P("section"),
        P("section", None),
        P(),
        P(),
        P(),
        P(None, "section"),
        P(both, None),
        P(both),
        P(both),
        P("section", None),
        P(),
        P(None, "section"),
        P(),
        P(),
        P(),
        P("section", None),
    )
    return jax.shard_map(
        shards, mesh=fine, in_specs=placed, out_specs=P(SEQ_AXES, "section"), check_vma=False
    )
```

```python
import math

import jax
import jax.numpy as jnp
from jax import lax
from jax.experimental import pallas as pl
from jax.experimental.pallas import tpu as pltpu
from jax.sharding import Mesh
from jax.sharding import PartitionSpec as P

HS = 64
RB = 16
ROWS = 256
N_SECTION = 4
N_Z, N_Y, N_CORE = 16, 4, 2
SEQ_AXES = ("z", "y", "core")
F32 = jnp.float32
BF16 = jnp.bfloat16


def layer_norm(values, gain_vec):
    row_mean = jnp.mean(values, axis=-1, keepdims=True)
    centered = values - row_mean
    variance = jnp.mean(centered * centered, axis=-1, keepdims=True)
    return centered * lax.rsqrt(variance + 1e-06) * gain_vec


def rotate(block, axis, size, step):
    return lax.ppermute(block, axis, [(i, (i + step) % size) for i in range(size)])


def exchange(copies, axis):
    return lax.all_to_all(copies, axis, 0, 0, tiled=True)


NT = (((1,), (1,)), ((), ()))


def dot(a, b):
    return jnp.dot(a, b, preferred_element_type=F32)


def gelu_mean(pre, tiles):
    hidden = (0.5 * pre * (1.0 + lax.erf(pre * (1.0 / math.sqrt(2.0))))).astype(BF16).astype(F32)
    return jnp.mean(hidden.reshape(tiles, hidden.shape[0] // tiles, hidden.shape[1]), axis=1)


def lanes(ref, index, width):
    return ref[:, pl.ds(pl.multiple_of(index * width, 128), width)]


def pack_kernel(core_ref, w_up, w_down, w_head, w_in, bias, out, sems):
    n = w_up.shape[0]
    start = pl.multiple_of(core_ref[0] * n, n)
    parts = (
        w_up.at[:, pl.ds(start, n)],
        w_down.at[:, pl.ds(start, n)],
        w_head.at[pl.ds(start, n), :],
        w_in.at[:, pl.ds(start, n)],
    )
    copies = [
        pltpu.make_async_copy(part, out.at[pl.ds(k * n, n), :], sems.at[k])
        for k, part in enumerate(parts)
    ]
    for copy in copies:
        copy.start()
    out[4 * n :, :] = jnp.broadcast_to(bias[...][None, :], (16, n))
    for copy in copies:
        copy.wait()


def pack(core, w_up, w_down, w_head, w_in, bias):
    n = w_up.shape[0]
    vmem = pl.BlockSpec(memory_space=pltpu.VMEM)
    return pl.pallas_call(
        pack_kernel,
        in_specs=[pl.BlockSpec(memory_space=pltpu.SMEM)]
        + [pl.BlockSpec(memory_space=pl.ANY)] * 4
        + [vmem],
        out_specs=vmem,
        out_shape=jax.ShapeDtypeStruct((4 * n + 16, n), BF16),
        scratch_shapes=[pltpu.SemaphoreType.DMA((4,))],
        cost_estimate=pl.CostEstimate(flops=0, bytes_accessed=4 * n * n * 4, transcendentals=0),
    )(core.astype(jnp.int32)[None], w_up, w_down, w_head, w_in, bias)


def natural(core, a, b):
    return jnp.where(core == 0, jnp.concatenate([a, b], 1), jnp.concatenate([b, a], 1))


def conv_kernel(feats, dw_weight, dw_bias, gain, out, mean, conv):
    tiles, channels = mean.shape
    side = math.isqrt(feats.shape[0] // tiles)
    taps = math.isqrt(dw_weight.shape[0])
    reach = (taps - 1) // 2
    column = lax.broadcasted_iota(jnp.int32, (side, side, 128), 1)
    tile_row = lax.broadcasted_iota(jnp.int32, (tiles, 128), 0)
    mean[...] = jnp.zeros_like(mean)

    def one_tile(tile, carry):
        start = pl.multiple_of(tile * side * side, side * side)
        for chunk in range(channels // 128):
            cols = pl.ds(chunk * 128, 128)
            source = feats[pl.ds(start, side * side), cols].astype(F32)
            source = source.reshape(side, side, 128)
            total = jnp.sum(jnp.sum(source, axis=0), axis=0, keepdims=True)
            total = jnp.broadcast_to(total * (1.0 / (side * side)), (tiles, 128))
            mean[:, cols] = jnp.where(tile_row == tile, total, mean[:, cols])
            bias = jnp.broadcast_to(dw_bias[0:1, cols], (side, 128))
            sums = [bias] * side
            for b in range(taps):
                move = b - reach
                moved = source
                if move:
                    moved = pltpu.roll(source, (-move) % side, 1)
                    inside = (column + move >= 0) & (column + move < side)
                    moved = jnp.where(inside, moved, 0.0)
                for a in range(taps):
                    tap = dw_weight[a * taps + b : a * taps + b + 1, cols]
                    tap = jnp.broadcast_to(tap, (side, 128))
                    for i in range(side):
                        if 0 <= i + a - reach < side:
                            sums[i] = sums[i] + moved[i + a - reach] * tap
            for i in range(side):
                conv[i * side : (i + 1) * side, cols] = sums[i]
        out[pl.ds(start, side * side), :] = layer_norm(conv[...], gain[...]).astype(BF16)
        return carry

    lax.fori_loop(0, tiles, one_tile, 0)


def first_row(ref, start):
    return ref[start : start + 16, :].astype(F32)[0:1, :]


def early_kernel(where, maps, up, block, left, right, left_swap, right_swap, hid):
    core = where[0]
    n = up.shape[0]
    tiles = hid.shape[1]
    maps_a, maps_b = lanes(maps, core, n), lanes(maps, 1 - core, n)
    pre = lax.dot_general(maps[...], up[...], NT, preferred_element_type=F32)
    hid[0] = gelu_mean(pre + first_row(block, 4 * n), tiles)
    for slot, (a, b) in enumerate(((left, left_swap), (right, right_swap))):
        pre = lax.dot_general(maps_a, a[0:n, :], NT, preferred_element_type=F32)
        pre += lax.dot_general(maps_b, b[0:n, :], NT, preferred_element_type=F32)
        hid[slot + 1] = gelu_mean(pre + first_row(a, 4 * n), tiles)


def late_kernel(
    where, maps, hid, feat_mean, layer_scale, b_down, lnf_gain, code, w_down, w_head, w_in,
    left, right, left_swap, right_swap, low, high, low_swap, high_swap, out,
):
    core = where[0]
    n = w_down.shape[0]
    tiles = hid.shape[1]
    pre = lax.dot_general(lanes(maps, core, n), low[0:n, :], NT, preferred_element_type=F32)
    pre += lax.dot_general(
        lanes(maps, 1 - core, n), low_swap[0:n, :], NT, preferred_element_type=F32
    )
    hid_far = gelu_mean(pre + first_row(high, 2 * n), tiles)

    def exact(block):
        upper = block.astype(BF16)
        lower = (block - upper.astype(F32)).astype(BF16)
        return jnp.concatenate([upper.astype(F32), lower.astype(F32)], 0).astype(BF16)

    sides = ((left, left_swap), (right, right_swap))
    own = dot(exact(hid[0]), w_down[...])
    part = exact(hid_far)
    br_a, br_b = dot(part, low[n : 2 * n, :]), dot(part, low_swap[n : 2 * n, :])
    for slot, (a, b) in enumerate(sides):
        part = exact(hid[slot + 1])
        br_a += dot(part, a[n : 2 * n, :])
        br_b += dot(part, b[n : 2 * n, :])
    branch = own + natural(core, br_a, br_b)
    branch = branch[0:tiles] + branch[tiles : 2 * tiles]
    pooled = feat_mean[...] + layer_scale[...] * (branch + b_down[...])
    feature = layer_norm(pooled, lnf_gain[...])
    first, second = feature[:, 0:n], feature[:, n : 2 * n]
    feature_a = jnp.where(core == 0, first, second).astype(BF16)
    feature_b = jnp.where(core == 0, second, first).astype(BF16)
    emb = dot(feature.astype(BF16), w_head[...]).astype(BF16)
    own = dot(emb, w_in[...])
    emb = (dot(feature_a, high[0:n, :]) + dot(feature_b, high_swap[0:n, :])).astype(BF16)
    x_a, x_b = dot(emb, high[n : 2 * n, :]), dot(emb, high_swap[n : 2 * n, :])
    for a, b in sides:
        emb = dot(feature_a, a[2 * n : 3 * n, :]) + dot(feature_b, b[2 * n : 3 * n, :])
        emb = emb.astype(BF16)
        x_a += dot(emb, a[3 * n : 4 * n, :])
        x_b += dot(emb, b[3 * n : 4 * n, :])
    x_fresh = own + natural(core, x_a, x_b)
    out[...] = jnp.concatenate([x_fresh, code[...]], axis=1).astype(BF16)


def select_kernel(bucket, rows, code, out):
    places = lax.broadcasted_iota(jnp.int32, (out.shape[0], bucket.shape[1]), 0)
    select = jnp.where(places == bucket[...], 1.0, 0.0).astype(BF16)
    width = rows.shape[1]
    out[:, 0:width] = dot(select, rows[...]).astype(BF16)
    out[:, width:] = dot(select, code[...]).astype(BF16)


def column_as_row(ref, column):
    lane = lax.broadcasted_iota(jnp.int32, (8, 128), 1)
    unit_row = jnp.where(lane == column, 1.0, 0.0).astype(BF16)
    tail = ref[:, ref.shape[1] - 128 :]
    return lax.dot_general(unit_row, tail, NT, preferred_element_type=F32)[0:1, :]


def place_rows(got, q_rows):
    code = column_as_row(got, 0)
    places = lax.broadcasted_iota(jnp.int32, (q_rows, got.shape[0]), 0).astype(F32) + 1.0
    placer = jnp.where(places == code, 1.0, 0.0).astype(BF16)
    return dot(placer, got[:, 0 : got.shape[1] - 128])


def earlier_kernel(
    where, got, w_in, left, right, left_swap, right_swap, high, high_swap, out, rows
):
    n = w_in.shape[0]
    rows[...] = place_rows(got, out.shape[0]).astype(BF16)
    own = dot(lanes(rows, where[1], n), w_in[...])
    columns = lanes(rows, where[4], n)
    x_a, x_b = dot(columns, high[n : 2 * n, :]), dot(columns, high_swap[n : 2 * n, :])
    for slot, (a, b) in enumerate(((left, left_swap), (right, right_swap))):
        columns = lanes(rows, where[slot + 2], n)
        x_a += dot(columns, a[3 * n : 4 * n, :])
        x_b += dot(columns, b[3 * n : 4 * n, :])
    out[...] = own + natural(where[0], x_a, x_b)


def scatter_kernel(where, rows, out):
    count = rows.shape[0]
    dest_row = column_as_row(rows, 1)
    dest = rows[:, rows.shape[1] - 128 :].astype(F32)[:, 1:2]
    index_a = lax.broadcasted_iota(jnp.int32, (count, count), 0)
    index_b = lax.broadcasted_iota(jnp.int32, (count, count), 1)
    before = jnp.where((dest == dest_row) & (index_a < index_b), 1.0, 0.0)
    rank = jnp.sum(before, axis=0, keepdims=True).astype(jnp.int32)
    shard = dest_row.astype(jnp.int32)
    plane = N_Y * N_CORE
    room = out.shape[0] // plane
    inside = shard - where[5] * plane
    bucket = jnp.where((inside >= 0) & (inside < plane), inside * room + rank, -1)
    places = lax.broadcasted_iota(jnp.int32, (out.shape[0], count), 0)
    select = jnp.where(places == bucket, 1.0, 0.0).astype(BF16)
    out[...] = dot(select, rows[...]).astype(BF16)


def arrive_kernel(got, earlier, out):
    rows = (place_rows(got, out.shape[1]) + earlier[...]).astype(BF16)
    for copy in range(out.shape[0]):
        out[copy] = rows


def local_call(body, outs, scratch, flops, size, *operands):
    vmem = pl.BlockSpec(memory_space=pltpu.VMEM)
    return pl.pallas_call(
        body,
        in_specs=[pl.BlockSpec(memory_space=pltpu.SMEM)] + [vmem] * (len(operands) - 1),
        out_specs=jax.tree.map(lambda _: vmem, outs),
        out_shape=outs,
        scratch_shapes=scratch,
        compiler_params=pltpu.CompilerParams(vmem_limit_bytes=16 * 2**20),
        cost_estimate=pl.CostEstimate(flops=flops, bytes_accessed=size, transcendentals=0),
    )(*operands)


def head_lanes(shape, head):
    lane = lax.broadcasted_iota(jnp.int32, shape, len(shape) - 1)
    return (lane >= head * HS) & (lane < (head + 1) * HS)


def dilated(shape, off_lane):
    return lax.rem(lax.broadcasted_iota(jnp.int32, shape, 0), RB) == off_lane


def project_kernel(x, ln_gain, w_q, w_k, w_v, q_gain, k_gain, off_lane, q, k, v, far_q, far_kv):
    rows, width = q.shape
    normed = layer_norm(x[...].astype(F32), ln_gain[...]).astype(BF16)
    chosen = dilated((rows, width), off_lane[...])

    def unit(raw, gain):
        raw = raw.astype(BF16).astype(F32)
        square = raw * raw
        mean = jnp.zeros_like(raw)
        for head in range(width // HS):
            inside = head_lanes(raw.shape, head)
            total = jnp.sum(jnp.where(inside, square, 0.0), axis=1, keepdims=True) * (1.0 / HS)
            mean = jnp.where(inside, total, mean)
        return (raw * lax.rsqrt(mean + 1e-06) * gain).astype(BF16)

    def far_rows(part):
        kept = jnp.where(chosen, part.astype(F32), 0.0)
        return jnp.sum(kept.reshape(rows // RB, RB, width), axis=1)

    q_rows = unit(dot(normed, w_q[...]), q_gain[...])
    k_rows = unit(dot(normed, w_k[...]), k_gain[...])
    v_rows = dot(normed, w_v[...]).astype(BF16)
    q[...], k[...], v[...] = q_rows, k_rows, v_rows
    far_q[...] = far_rows(q_rows)
    pairs = jnp.concatenate([far_rows(k_rows), far_rows(v_rows)], axis=1).astype(BF16)
    for copy in range(far_kv.shape[0]):
        far_kv[copy] = pairs


def by_head(block):
    heads = block.shape[1] // HS
    wide = block.astype(F32)
    kept = [jnp.where(head_lanes(wide.shape, head), wide, 0.0) for head in range(heads)]
    return jnp.concatenate(kept, axis=0)


def back(block, rows, width):
    out = jnp.zeros((rows, width), F32)
    for head in range(width // HS):
        part = jnp.broadcast_to(block[head * rows : (head + 1) * rows], (rows, width))
        out = jnp.where(head_lanes(out.shape, head), part, out)
    return out


def weigh(queries, keys, values):
    scores = lax.dot_general(queries, keys, NT, preferred_element_type=F32)
    weights = jnp.exp(scores * (1.0 / math.sqrt(HS)))
    return jnp.sum(weights, axis=1, keepdims=True), dot(weights.astype(BF16), values)


def far_part(far_q, kv):
    rows, width = far_q.shape
    spread_q = by_head(far_q[...])
    spread_q = jnp.concatenate([spread_q, jnp.zeros_like(spread_q)], axis=1).astype(BF16)
    den, num = weigh(spread_q, kv[...], kv[...])
    return back(den, rows, width), back(num[:, width:], rows, width)


def near_kernel(where, q, k, v, far_q, kv, x, den, num, far_den, far_num, residual):
    wanted = lax.broadcasted_iota(jnp.int32, (residual.shape[0], x.shape[1]), 0)
    column = lax.broadcasted_iota(jnp.int32, (residual.shape[0], x.shape[1]), 1)
    pick = jnp.where(column == wanted + where[1] * residual.shape[0], 1.0, 0.0).astype(BF16)
    residual[...] = lax.dot_general(pick, x[...], NT, preferred_element_type=F32)
    rows, width = q.shape
    local_den, local_num = weigh(by_head(q[...]).astype(BF16), k[...], v[...])
    den[...] = back(local_den, rows, width)
    num[...] = back(local_num, rows, width)
    far_den[...], far_num[...] = far_part(far_q, kv)


def far_kernel(far_q, kv, off_lane, den, num, far_den, far_num, w_out, out):
    rows, width = num.shape
    chosen = dilated((rows, width), off_lane[...])
    more_den, more_num = far_part(far_q, kv)

    def placed(block):
        wide = jnp.broadcast_to(block[:, None, :], (rows // RB, RB, width))
        return jnp.where(chosen, wide.reshape(rows, width), 0.0)

    attended = (num[...] + placed(far_num[...] + more_num)) / (
        den[...] + placed(far_den[...] + more_den)
    )
    attended = attended.astype(BF16)
    out[...] = lax.dot_general(w_out[...], attended, NT, preferred_element_type=F32).astype(BF16)


def sum_kernel(residual, parts, out):
    total = residual[...]
    for part in range(parts.shape[0]):
        total += parts[part].astype(F32)
    out[...] = total.astype(BF16)


def vmem_call(body, outs, flops, size, exps, *operands, scratch=()):
    vmem = pl.BlockSpec(memory_space=pltpu.VMEM)
    return pl.pallas_call(
        body,
        in_specs=[vmem] * len(operands),
        out_specs=jax.tree.map(lambda _: vmem, outs),
        out_shape=outs,
        scratch_shapes=list(scratch),
        compiler_params=pltpu.CompilerParams(vmem_limit_bytes=16 * 2**20),
        cost_estimate=pl.CostEstimate(flops=flops, bytes_accessed=size, transcendentals=exps),
    )(*operands)


def shards(
    feats,
    dw_weight,
    dw_bias,
    ln1_gain,
    w_up,
    b_up,
    w_down,
    b_down,
    layer_scale,
    lnf_gain,
    w_head,
    prior,
    counts,
    positions,
    w_in,
    ln_gain,
    w_qkv,
    qn_gain,
    kn_gain,
    offsets,
    w_out,
):
    n_section = N_SECTION
    n_seq = N_Z * N_Y * N_CORE
    section_idx = lax.axis_index("section")
    core = lax.axis_index("core")
    tiles = feats.shape[0]
    channels = feats.shape[3]
    half = channels // N_CORE
    share = w_up.shape[0]

    row = lambda vec: vec[None, :]
    others = [(section_idx + step) % N_SECTION for step in (3, 1, 2)]
    where = jnp.stack([core, section_idx] + others + [lax.axis_index("z")]).astype(jnp.int32)

    block = pack(core, w_up, w_down, w_head, w_in, b_up)
    block, prior = lax.optimization_barrier((block, prior))
    left = rotate(block, "section", N_SECTION, 1)
    right = rotate(block, "section", N_SECTION, -1)

    q_rows = ROWS // n_section
    capacity = -(-(tiles + prior.shape[0]) // n_seq)
    slot_ids = jnp.arange(prior.shape[0])
    live_mask = slot_ids < counts[0]
    dest_shard = positions // ROWS
    row_code = (positions % ROWS - section_idx * q_rows + 1).astype(BF16)
    dest_prior = dest_shard[tiles:]
    earlier = (
        (dest_prior[None, :] == dest_prior[:, None])
        & (slot_ids[None, :] < slot_ids[:, None])
        & live_mask[None, :]
    )
    within = jnp.sum(earlier.astype(jnp.int32), axis=1)
    bucket = jnp.where(live_mask, dest_prior * capacity + within, -1)
    code_prior = jnp.broadcast_to(row_code[tiles:, None], (prior.shape[0], 128))
    send = vmem_call(
        select_kernel,
        jax.ShapeDtypeStruct((n_seq * capacity, prior.shape[1] + 128), BF16),
        200_000_000,
        2_000_000,
        0,
        row(bucket), prior, code_prior,
    )

    got_prior = lax.all_to_all(
        send.reshape(n_seq, capacity, send.shape[1]), SEQ_AXES, 0, 0, tiled=True
    )
    left, right, low_in, high_in, feats = lax.optimization_barrier(
        (left, right, left[: 2 * share], right[2 * share :], feats)
    )
    low = rotate(low_in, "section", N_SECTION, 1)
    high = rotate(high_in, "section", N_SECTION, -1)
    left_swap = rotate(left, "core", N_CORE, 1)
    right_swap = rotate(right, "core", N_CORE, 1)
    pixels = feats.shape[1] * feats.shape[2]
    normed_maps, feat_mean = vmem_call(
        conv_kernel,
        (
            jax.ShapeDtypeStruct((tiles * pixels, channels), BF16),
            jax.ShapeDtypeStruct((tiles, channels), F32),
        ),
        30_000_000_000,
        8_000_000,
        0,
        feats.reshape(-1, channels), dw_weight.reshape(-1, channels), row(dw_bias), row(ln1_gain),
        scratch=[pltpu.VMEM((pixels, channels), F32)],
    )
    low, high, normed_maps, feat_mean = lax.optimization_barrier(
        (low, high, normed_maps, feat_mean)
    )
    low_swap = rotate(low, "core", N_CORE, 1)
    high_swap = rotate(high, "core", N_CORE, 1)
    code_fresh = jnp.where(
        jnp.arange(128)[None, :] == 0,
        row_code[:tiles, None].astype(F32),
        dest_shard[:tiles, None].astype(F32),
    )
    hid = local_call(
        early_kernel,
        jax.ShapeDtypeStruct((3, tiles, share), F32),
        [],
        2_000_000_000,
        6_000_000,
        where, normed_maps, w_up, block, left, right, left_swap, right_swap,
    )
    fresh = local_call(
        late_kernel,
        jax.ShapeDtypeStruct((tiles, channels + 128), BF16),
        [],
        2_000_000_000,
        8_000_000,
        where, normed_maps, hid, feat_mean, row(layer_scale), row(b_down), row(lnf_gain),
        code_fresh, w_down, w_head, w_in, left, right, left_swap, right_swap, low, high, low_swap,
        high_swap,
    )
    got_prior, fresh = lax.optimization_barrier((got_prior, fresh))
    fresh_z = exchange(jnp.broadcast_to(fresh[None], (N_Z,) + fresh.shape), "z")
    fresh_z = fresh_z.reshape(N_Z * tiles, channels + 128)
    x_earlier = local_call(
        earlier_kernel,
        jax.ShapeDtypeStruct((q_rows, channels), F32),
        [pltpu.VMEM((q_rows, prior.shape[1]), BF16)],
        500_000_000,
        4_000_000,
        where, got_prior.reshape(send.shape), w_in, left, right, left_swap, right_swap, high,
        high_swap,
    )
    fresh_z, x_earlier = lax.optimization_barrier((fresh_z, x_earlier))
    plane = N_Y * N_CORE
    room = N_Z * capacity
    to_plane = local_call(
        scatter_kernel,
        jax.ShapeDtypeStruct((plane * room, channels + 128), BF16),
        [],
        60_000_000,
        1_000_000,
        where, fresh_z,
    )
    got = lax.all_to_all(
        to_plane.reshape(plane, room, channels + 128), SEQ_AXES[1:], 0, 0, tiled=True
    ).reshape(plane * room, channels + 128)
    x_copies = vmem_call(
        arrive_kernel,
        jax.ShapeDtypeStruct((n_section, q_rows, channels), BF16),
        30_000_000,
        1_000_000,
        0,
        got, x_earlier,
    )
    x_rows = exchange(x_copies, "section").reshape(ROWS, channels)

    heads_here = w_qkv.shape[1] // (3 * HS)
    width = heads_here * HS
    stride_rows = ROWS // RB
    my_offsets = lax.dynamic_slice_in_dim(offsets, section_idx * heads_here, heads_here)
    off_lane = row(jnp.repeat(my_offsets, HS))
    w_q, w_k, w_v = (w_qkv[:, part * width : (part + 1) * width] for part in range(3))
    small = lambda rows, kind: jax.ShapeDtypeStruct((rows, width), kind)
    q, k, v, far_q, far_kv = vmem_call(
        project_kernel,
        (small(ROWS, BF16),) * 3
        + (small(stride_rows, F32), jax.ShapeDtypeStruct((N_Z, stride_rows, 2 * width), BF16)),
        300_000_000,
        2_000_000,
        0,
        x_rows, row(ln_gain), w_q, w_k, w_v, row(jnp.tile(qn_gain, heads_here)),
        row(jnp.tile(kn_gain, heads_here)), off_lane,
    )
    z_kv = exchange(far_kv, "z").reshape(N_Z * stride_rows, 2 * width)
    half_kv = lax.all_gather(z_kv, "y", axis=0, tiled=True)
    other_kv = rotate(half_kv, "core", N_CORE, 1)
    width_part = channels // n_section
    den, num, far_den, far_num, residual = local_call(
        near_kernel,
        (small(ROWS, F32),) * 2
        + (small(stride_rows, F32),) * 2
        + (jax.ShapeDtypeStruct((width_part, ROWS), F32),),
        [],
        2_000_000_000,
        2_000_000,
        where, q, k, v, far_q, half_kv, x_rows,
    )
    partial_out = vmem_call(
        far_kernel,
        jax.ShapeDtypeStruct((channels, ROWS), BF16),
        150_000_000,
        2_000_000,
        50_000,
        far_q, other_kv, off_lane, den, num, far_den, far_num,
        jnp.transpose(w_out),
    )
    parts = lax.all_to_all(
        partial_out.reshape(n_section, width_part, ROWS), "section", 0, 0, tiled=True
    )
    total = vmem_call(
        sum_kernel,
        jax.ShapeDtypeStruct((width_part, ROWS), BF16),
        1_000_000,
        1_000_000,
        0,
        residual, parts,
    )
    return jnp.transpose(total)


def solution(mesh):
    fine = Mesh(
        mesh.devices.reshape(N_SECTION, N_Z, N_Y, N_CORE), ("section",) + SEQ_AXES
    )
    both = ("section",) + SEQ_AXES
    placed = (
        P(both, None, None, None),
        P(),
        P(),
        P(),
        P("section", None),
        P("section"),
        P("section", None),
        P(),
        P(),
        P(),
        P(None, "section"),
        P(both, None),
        P(both),
        P(both),
        P("section", None),
        P(),
        P(None, "section"),
        P(),
        P(),
        P(),
        P("section", None),
    )
    return jax.shard_map(
        shards, mesh=fine, in_specs=placed, out_specs=P(SEQ_AXES, "section"), check_vma=False
    )
```
